128 devices in a mesh: fsdp: 128 (over x, z, y, core).
Axes of the slice: x: 4, y: 4, z: 4, core: 2. Of those that a mesh axis runs over, the one named last changes fastest.
Arguments:
- inputs: bfloat16 [2, 8192, 512], P(None, 'fsdp'), may hold values from -6 to 6
- cotangent: bfloat16 [2, 8192, 512], P(None, 'fsdp'), may hold values from -24 to 24
- lengths: int32 [2, 192], replicated, may hold values from 1 to 64, 8192 in all within a row
- query_weight: bfloat16 [2, 512, 512], P(None, 'fsdp'), may hold values from -0.25 to 0.25
- key_weight: bfloat16 [2, 512, 512], P(None, 'fsdp'), may hold values from -0.25 to 0.25
- value_weight: bfloat16 [2, 512, 864], P(None, 'fsdp'), may hold values from -0.25 to 0.25
- swish_weight: bfloat16 [2, 512, 864], P(None, 'fsdp'), may hold values from -0.25 to 0.25
- output_weight: bfloat16 [2, 864, 512], P(None, None, 'fsdp'), may hold values from -0.21875 to 0.21875
- upward_weight: bfloat16 [2, 512, 864], P(None, 'fsdp'), may hold values from -0.25 to 0.25
- gating_weight: bfloat16 [2, 512, 864], P(None, 'fsdp'), may hold values from -0.25 to 0.25
- downward_weight: bfloat16 [2, 864, 512], P(None, None, 'fsdp'), may hold values from -0.21875 to 0.21875
- norm_gains: bfloat16 [2, 2, 512], P(None, None, 'fsdp'), may hold values from 0.25 to 1.75
- norm_biases: bfloat16 [2, 2, 512], P(None, None, 'fsdp'), may hold values from -1.5 to 1.5
Outputs:
- outputs: bfloat16 [2, 8192, 512], P(None, 'fsdp')
- input_grad: bfloat16 [2, 8192, 512], P(None, 'fsdp')
- query_grad: float32 [2, 512, 512], P(None, 'fsdp')
- key_grad: float32 [2, 512, 512], P(None, 'fsdp')
- value_grad: float32 [2, 512, 864], P(None, 'fsdp')
- swish_grad: float32 [2, 512, 864], P(None, 'fsdp')
- output_grad: float32 [2, 864, 512], P(None, None, 'fsdp')
- upward_grad: float32 [2, 512, 864], P(None, 'fsdp')
- gating_grad: float32 [2, 512, 864], P(None, 'fsdp')
- downward_grad: float32 [2, 864, 512], P(None, None, 'fsdp')
- gain_grad: float32 [2, 2, 512], P(None, None, 'fsdp')
- bias_grad: float32 [2, 2, 512], P(None, None, 'fsdp')
The draws below stay inside these ranges and needn't reach their ends.
Inputs may be any that keep to these rules, and one draw needn't show every extreme that they name: Each row of lengths sums to 8192, and in each row one length equals 64.
All inputs are finite; a program needn't handle non-finite values.
Results may differ from the reference program's by a relative error of at most 0.03.
Values may be sent and summed in bfloat16 or wider, within the bound.
No kernel may reach another device: no remote copies, remote signals or barrier semaphores. Data moves between devices by JAX's collectives and lax.ppermute only.
A program may use at most 192 MiB of HBM per device.

```python
import math
import jax
import jax.numpy as jnp
import numpy as np
from jax import lax

D = 512
HEADS = 2
DK = 256
DV = 432
FF = 864
LAYERS = 2
MB = 2
TOK_MB = 64
LMAX = 64
TOKENS = 8192
NSEQ = 192
QK = 512
VD = 864
N_FSDP = 128


def spiked(values, rng, source, target, blocks, factor):
    owner, partner = [(jnp.arange(values.shape[dim]) // (values.shape[dim] // blocks)).reshape([-1 if axis == dim else 1 for axis in range(values.ndim)]) for dim in (source, target)]
    chosen = jax.random.permutation(rng, blocks)[partner]
    strong = (owner == chosen) | (owner == (partner + blocks // 2) % blocks)
    return jnp.where(strong, factor * values, values)


def levels(stream_key, dims, shards, low, largest):
    def one(dim, shards_of):
        heights = jax.random.uniform(jax.random.fold_in(jax.random.fold_in(stream_key, 6), dim), (shards_of,), jnp.float32, low / len(shards), largest / len(shards))
        return jnp.repeat(jnp.exp(heights), dims[dim] // shards_of).reshape((-1,) + (1,) * (len(dims) - dim - 1))

    factor_of = one(*shards[0])
    for cut in shards[1:]:
        factor_of = factor_of * one(*cut)
    return factor_of


def split_up(number_of, total, reach, skew):
    weights = [(1 << 20) // math.isqrt(grade ** skew) + 1 for grade in range(2, number_of + 1)]
    rest, counts = total - reach - (number_of - 1), [1] * (number_of - 1)
    while rest > 0:
        free = [i for i in range(number_of - 1) if counts[i] < reach]
        mass, remaining = sum([weights[i] for i in free]), rest
        for i in free:
            extra = min(reach - counts[i], max(1, remaining * weights[i] // mass), rest)
            counts[i] = counts[i] + extra
            rest = rest - extra
    return np.array([reach] + counts)


def ragged(rng, amount, total, bound, lean):
    if amount == 2:
        one = jax.random.randint(rng, (), max(1, total - bound), min(bound, total - 1) + 1)
        return jnp.stack([one, total - one])
    sizes = jnp.asarray(split_up(amount, total, bound, lean), jnp.int32)
    pairs = (amount - 1) // 2
    source_of, taker = sizes[1:1 + 2 * pairs:2], sizes[2:2 + 2 * pairs:2]
    margin = jnp.minimum(source_of - 1, bound - taker)
    moved = jax.random.randint(jax.random.fold_in(rng, 1), (pairs,), 0, 1 << 20) % (margin + 1)
    sizes = sizes.at[1:1 + 2 * pairs:2].set(source_of - moved).at[2:2 + 2 * pairs:2].set(taker + moved)
    return sizes[jax.random.permutation(jax.random.fold_in(rng, 2), amount)]


def noise(own_key, shape, scale, bound, split=(), held_as=jnp.bfloat16):
    factor_of = levels(own_key, shape, split, -0.22, 0.18) if split else 1.0
    values = jax.random.normal(own_key, shape, jnp.float32) * scale * factor_of
    return jnp.minimum(jnp.maximum(values, -bound), bound).astype(held_as)


def noise_with(rng, dims, scale, reach, pieces, heavy, held_as=jnp.bfloat16):
    entries = scale * jax.random.normal(rng, dims, jnp.float32)
    if pieces:
        entries = entries * levels(rng, dims, pieces, -0.22, 0.18)
    return jnp.clip(spiked(entries, jax.random.fold_in(rng, 3), *heavy), -reach, reach).astype(held_as)


def setup_inputs(seed: int = 0) -> dict:
    keys = jax.random.split(jax.random.key(seed), 14)
    inputs = noise(keys[0], (MB, TOKENS, D), 1.0, 6.0, ((1, 128),))
    cotangent = noise_with(keys[1], (MB, TOKENS, D), 1.0, 24.0, ((1, 128),), (1, 2, 128, 5.5))
    lengths = jax.vmap(lambda own: ragged(own, NSEQ, TOKENS, LMAX, 0))(jax.random.split(keys[2], MB)).reshape((MB, NSEQ)).astype(jnp.int32)
    query_weight = noise(keys[3], (LAYERS, D, QK), D ** -0.5, 0.25, ((1, 128),))
    key_weight = noise(keys[4], (LAYERS, D, QK), D ** -0.5, 0.25, ((1, 128),))
    value_weight = noise(keys[5], (LAYERS, D, VD), D ** -0.5, 0.25, ((1, 128),))
    swish_weight = noise(keys[6], (LAYERS, D, VD), D ** -0.5, 0.25, ((1, 128),))
    output_weight = noise(keys[7], (LAYERS, VD, D), VD ** -0.5, 0.21875, ((2, 128),))
    upward_weight = noise(keys[8], (LAYERS, D, FF), D ** -0.5, 0.25, ((1, 128),))
    gating_weight = noise(keys[9], (LAYERS, D, FF), D ** -0.5, 0.25, ((1, 128),))
    downward_weight = noise(keys[10], (LAYERS, FF, D), FF ** -0.5, 0.21875, ((2, 128),))
    norm_gains = jnp.clip(1.0 + 0.15 * jax.random.normal(keys[11], (LAYERS, 2, D), jnp.float32), 0.25, 1.75).astype(jnp.bfloat16)
    norm_biases = noise(keys[12], (LAYERS, 2, D), 0.3, 1.5, ((2, 128),))
    return {"inputs": inputs, "cotangent": cotangent, "lengths": lengths, "query_weight": query_weight, "key_weight": key_weight, "value_weight": value_weight, "swish_weight": swish_weight, "output_weight": output_weight, "upward_weight": upward_weight, "gating_weight": gating_weight, "downward_weight": downward_weight, "norm_gains": norm_gains, "norm_biases": norm_biases}


@jax.custom_vjp
def low(v):
    return lax.optimization_barrier(v.astype(jnp.bfloat16)).astype(jnp.float32)

@jax.custom_vjp
def low_back(v):
    return v

def low_keep(v):
    return (low(v), None)

def low_pass(kept, grad):
    return (grad,)

def back_keep(v):
    return (v, None)

def back_low(kept, grad):
    return (low(grad),)
low.defvjp(low_keep, low_pass)
low_back.defvjp(back_keep, back_low)
PRECISE = lax.Precision.HIGHEST
NORM_EPSILON = 1e-05
GROUP_EPSILON = 1.0
GROUP_WINDOWS = 8

def row_layout(length_row, window_rows, first_row, block_rows, total_rows):
    seq_ends = jnp.cumsum(length_row).astype(jnp.int32)
    starts = (seq_ends - length_row).astype(jnp.int32)
    before = starts[None, :] <= window_rows[:, None]
    segment = (lax.optimization_barrier(jnp.sum(before.astype(jnp.int32), axis=1)) - 1).astype(jnp.int32)
    anchor = lax.optimization_barrier(jnp.max(jnp.where(before, starts[None, :], 0), axis=1)).astype(jnp.int32)
    position = (window_rows - anchor).astype(jnp.float32)
    owned = (anchor >= first_row) & (anchor < first_row + block_rows) & (window_rows < total_rows)
    return (jnp.where(owned, segment, -1).astype(jnp.int32), position, anchor)

def decay_mask(segment, position):
    same_seq = (segment[:, None] == segment[None, :]) & (segment[:, None] >= 0)
    distance = position[:, None] - position[None, :]
    log_rates = jnp.log(1.0 - 2.0 ** (-5.0 - jnp.arange(HEADS).astype(jnp.float32)))
    allowed = (same_seq & (distance >= 0))[None]
    clamped = jnp.where(distance >= 0, distance, 0.0)
    return jnp.where(allowed, jnp.exp(log_rates[:, None, None] * clamped[None]), 0.0)

def rotary_tables(position):
    frequency = 1.0 / 10000.0 ** jnp.linspace(0.0, 1.0, DK // 2)
    frequency = jnp.repeat(frequency, 2)
    phases = position[..., None] * frequency
    return (jnp.cos(phases)[..., None, :], jnp.sin(phases)[..., None, :])

def rotate(values, cosine, sine_table):
    paired = values.reshape(values.shape[:-1] + (DK // 2, 2))
    turned = jnp.stack([-paired[..., 1], paired[..., 0]], axis=-1).reshape(values.shape)
    return values * cosine + turned * sine_table

def layer_norm(values, gain_row, bias_row):
    center = values - lax.optimization_barrier(jnp.mean(values, axis=-1, keepdims=True))
    spread = lax.optimization_barrier(jnp.mean(center * center, axis=-1, keepdims=True))
    return center * lax.rsqrt(spread + NORM_EPSILON) * gain_row + bias_row

def group_norm(retained):
    return retained * lax.rsqrt(lax.optimization_barrier(jnp.mean(retained * retained, axis=-1, keepdims=True)) + GROUP_EPSILON)

def project(values, matrix):
    return jnp.einsum('grd,dk->grk', values, matrix, precision=PRECISE)

def retnet_layer(stream, decays, cosine, sine_table, params):
    query_w, key_w, value_w, swish_w, output_w, upward_w, gating_w, downward_w, gains, biases = params
    groups, window = (stream.shape[0], stream.shape[1])
    normed = low(layer_norm(stream, gains[0], biases[0]))
    query_pre = low_back(project(normed, query_w)).reshape(groups, window, HEADS, DK)
    key_pre = low_back(project(normed, key_w)).reshape(groups, window, HEADS, DK)
    query_low = low(rotate(query_pre, cosine, sine_table))
    key_low = low(rotate(key_pre, cosine, sine_table) * DK ** (-0.5))
    value_low = low(low_back(project(normed, value_w))).reshape(groups, window, HEADS, DV)
    scores = jnp.einsum('grhd,gshd->ghrs', query_low, key_low, precision=PRECISE)
    weights_low = low(decays * low_back(scores))
    retained = low_back(jnp.einsum('ghrs,gshd->grhd', weights_low, value_low, precision=PRECISE))
    normalized = group_norm(retained).reshape(groups, window, HEADS * DV)
    gate_pre = low_back(project(normed, swish_w))
    mixed_low = low(normalized * jax.nn.silu(gate_pre))
    middle = stream + low_back(project(mixed_low, output_w))
    normed_two = low(layer_norm(middle, gains[1], biases[1]))
    upward = low_back(project(normed_two, upward_w))
    gating = low_back(project(normed_two, gating_w))
    hidden = low(jax.nn.gelu(upward) * gating)
    return middle + low_back(project(hidden, downward_w))

def run_layers(stream, decays, cosine, sine_table, weights):
    for which_layer in range(LAYERS):
        stream = retnet_layer(stream, decays, cosine, sine_table, tuple((stacked_param[which_layer] for stacked_param in weights)))
    return stream

def reference(inputs, cotangent, lengths, query_weight, key_weight, value_weight, swish_weight, output_weight, upward_weight, gating_weight, downward_weight, norm_gains, norm_biases):
    params = tuple((matrix.astype(jnp.float32) for matrix in (query_weight, key_weight, value_weight, swish_weight, output_weight, upward_weight, gating_weight, downward_weight, norm_gains, norm_biases)))
    block_rows = TOK_MB
    firsts = jnp.arange(N_FSDP, dtype=jnp.int32) * block_rows
    window_rows = (firsts[:, None] + jnp.arange(2 * block_rows, dtype=jnp.int32)[None, :]).reshape(-1).astype(jnp.int32)
    first_rows = jnp.repeat(firsts, 2 * block_rows).astype(jnp.int32)
    segments, positions, anchors = jax.vmap(lambda length_row: row_layout(length_row.astype(jnp.int32), window_rows, first_rows, block_rows, TOKENS))(lengths)

    def windows(stream):
        padded = jnp.concatenate([stream, jnp.zeros((MB, block_rows, D), stream.dtype)], axis=1)
        padded = padded.reshape(MB, N_FSDP + 1, block_rows, D)
        return jnp.concatenate([padded[:, :-1], padded[:, 1:]], axis=2)
    count = MB * N_FSDP // GROUP_WINDOWS
    shape_rows = (count, GROUP_WINDOWS, 2 * block_rows)
    live = (segments >= 0).astype(jnp.float32).reshape(shape_rows)
    stream_groups = windows(inputs.astype(jnp.float32)).reshape(shape_rows + (D,))
    grad_groups = windows(cotangent.astype(jnp.float32)).reshape(shape_rows + (D,)) * live[..., None]
    segment_groups = segments.reshape(shape_rows)
    position_groups = positions.reshape(shape_rows)

    def group_step(totals, group_item):
        stream, grad_out, segment, position = group_item
        decays = jax.vmap(decay_mask)(segment, position)
        cosine, sine_table = rotary_tables(position)

        def forward(weights, stream_in):
            return run_layers(stream_in, decays, cosine, sine_table, weights)
        result, pullback = jax.vjp(forward, params, stream)
        gradients, grad_in = pullback(grad_out)
        return (jax.tree.map(jnp.add, totals, gradients), (result, grad_in))
    start_totals = jax.tree.map(jnp.zeros_like, params)
    totals, (results, grads_in) = lax.scan(group_step, start_totals, (stream_groups, grad_groups, segment_groups, position_groups))
    owner_flag = anchors.reshape(MB, N_FSDP, 2 * block_rows)[:, :, :block_rows] >= firsts[None, :, None]

    def restore(stacked):
        stacked = stacked.reshape(MB, N_FSDP, 2 * block_rows, D)
        own_rows = stacked[:, :, :block_rows]
        lent_rows = jnp.concatenate([jnp.zeros_like(stacked[:, :1, block_rows:]), stacked[:, :-1, block_rows:]], axis=1)
        return jnp.where(owner_flag[..., None], own_rows, lent_rows).reshape(MB, TOKENS, D).astype(jnp.bfloat16)
    return (restore(results), restore(grads_in), totals[0], totals[1], totals[2], totals[3], totals[4], totals[5], totals[6], totals[7], totals[8], totals[9])
```

```python
import functools

import jax
import jax.numpy as jnp
import numpy as np
from jax import lax
from jax.experimental import pallas as pl
from jax.experimental.pallas import tpu as pltpu
from jax.sharding import PartitionSpec as P

HEADS = 2
DK = 256
DV = 432
D = 512
ROWS = 256
WIN = 128
BLOCK = 64
TOKENS = 8192
NSEQ = 192
NORM_EPSILON = 1e-05
GROUP_EPSILON = 1.0
BF = jnp.bfloat16
F32 = jnp.float32

Q0, K0, V0, S0, O0, U0, G0, D0, WIDTH = 0, 512, 1024, 1920, 2816, 3712, 4608, 5504, 6400
VP = 896
NORM_LANE = 96
LINES = WIDTH // 128

UNITS = (((0, 0), (1, 0), (0, 3)), ((0, 1), (1, 1), (1, 3)), ((0, 2), (1, 2)))
AXES = ("xzy", "zyx", "yxz")
FLAT = (160, 160, 112)
WIDE = tuple(len(u) * WIDTH for u in UNITS)
COLOR_OF = {unit: (c, k) for c, units in enumerate(UNITS) for k, unit in enumerate(units)}
STRIDE = {"x": 32, "z": 8, "y": 2}
STEPS = tuple((2 - k // 2, k % 2) for k in range(6))


def mask_of(core, second):
    return 3 if (core == 0) == bool(second) else 1


def step_pairs(color, step):
    stage, second = STEPS[step]
    stride = STRIDE[AXES[color][stage]]
    return [(i, i ^ (mask_of(i & 1, second) * stride)) for i in range(128)]


CORE_PAIRS = [(i, i ^ 1) for i in range(128)]


def dot(a, b):
    return lax.dot_general(a, b, (((1,), (0,)), ((), ())), preferred_element_type=F32)


def dot_nt(a, b):
    return lax.dot_general(a, b, (((1,), (1,)), ((), ())), preferred_element_type=F32)


def dot_tn(a, b):
    return lax.dot_general(a, b, (((0,), (0,)), ((), ())), preferred_element_type=F32)


def iota(shape, dim):
    return lax.broadcasted_iota(jnp.int32, shape, dim)


def source_feature(pos, me, third_color):
    core = (me & 1) ^ (pos >> 8)
    row = (pos >> 6) & 3
    color = jnp.where(row == 3, third_color, row)
    device = (me & ~1) | core
    first = jnp.where(core == 0, 1, 3)
    second = jnp.where(core == 0, 3, 1)
    for step, (stage, later) in enumerate(STEPS):
        bit = (pos >> step) & 1
        mask = second if later else first
        strides = [STRIDE[AXES[c][stage]] for c in range(3)]
        stride = jnp.where(color == 0, strides[0], jnp.where(color == 1, strides[1], strides[2]))
        device = device ^ (bit * mask * stride)
    return device * 4 + row


def swap_rows():
    r, c = iota((256, 256), 0), iota((256, 256), 1)
    return (((r & 15) * 16 + (r >> 4)) == c).astype(BF)


def pack_kernel(q, k, v, s, o, u, g, d, gain, bias, a_ref, b_ref, c_ref, row):
    row[...] = jnp.zeros_like(row)
    for layer in range(2):
        for weight, at, width in ((q, Q0, 512), (k, K0, 512), (v, V0, 864), (s, S0, 864), (u, U0, 864), (g, G0, 864)):
            row[layer, 0:4, at : at + width] = weight[layer].astype(F32)
        eye = (iota((8, 4), 0) == iota((8, 4), 1)).astype(BF)
        for weight, at in ((o, O0), (d, D0)):
            row[layer, :, at : at + 864] = dot_nt(eye, weight[layer])
        norms = jnp.concatenate(
            [gain[layer, 0:1].astype(F32), gain[layer, 1:2].astype(F32), bias[layer, 0:1].astype(F32), bias[layer, 1:2].astype(F32)],
            axis=0,
        ).astype(BF)
        spread = (iota((4, 128), 1) == iota((4, 128), 0) + NORM_LANE).astype(BF)
        tile = lax.dot_general(norms, spread, (((0,), (0,)), ((), ())), preferred_element_type=F32)
        row[layer, 0:4, V0 + 768 : V0 + 896] = row[layer, 0:4, V0 + 768 : V0 + 896] + tile
    for out, units, lines in zip((a_ref, b_ref, c_ref), UNITS, FLAT):
        pieces = []
        for layer, r in units:
            for j in range(LINES):
                pieces.append(row[layer, r : r + 1, j * 128 : (j + 1) * 128])
        pad = lines - len(pieces)
        out[...] = jnp.concatenate(pieces + [jnp.zeros((pad, 128), F32)], axis=0).astype(BF)


def pack(*weights):
    return pl.pallas_call(
        pack_kernel,
        out_shape=[jax.ShapeDtypeStruct((n, 128), BF) for n in FLAT],
        scratch_shapes=[pltpu.VMEM((2, 8, WIDTH), F32)],
    )(*weights)


def rows_kernel(a, b, c, a_out, b_out, c_out):
    swap = swap_rows()
    for src, out, wide in zip((a, b, c), (a_out, b_out, c_out), WIDE):
        lines = wide // 128
        for i in range(0, lines, 16):
            block = src[:, i : i + 16, :].reshape(256, 128)
            turned = dot(swap, block).astype(BF)
            for k in range(min(16, lines - i)):
                out[:, (i + k) * 128 : (i + k + 1) * 128] = turned[k * 16 : (k + 1) * 16]


def to_rows(flats):
    return pl.pallas_call(
        rows_kernel,
        out_shape=[jax.ShapeDtypeStruct((16, w), BF) for w in WIDE],
        compiler_params=pltpu.CompilerParams(vmem_limit_bytes=16 << 20),
    )(*flats)


def gather(flats):
    cur = [f[None] for f in flats]
    for step in range(4):
        got = [lax.ppermute(cur[c], "fsdp", step_pairs(c, step)) for c in range(3)]
        cur = [jnp.concatenate([cur[c], got[c]], axis=0) for c in range(3)]
    first = to_rows(cur)
    pieces = []
    for c in range(3):
        one = lax.ppermute(first[c], "fsdp", step_pairs(c, 4))
        two = lax.ppermute(first[c], "fsdp", step_pairs(c, 5))
        three = lax.ppermute(one, "fsdp", step_pairs(c, 5))
        pieces.append((first[c], one, two, three))
    other = [[lax.ppermute(p, "fsdp", CORE_PAIRS) for p in pieces[c]] for c in range(3)]
    return [p for held in (pieces, other) for c in range(3) for p in held[c]]


def tables_kernel(me_ref, lengths, trig, decay, cos, sin_a, sin_b, live, flags, order, third):
    me = me_ref[0]
    first_row = me * BLOCK
    tri = (iota((NSEQ, NSEQ), 0) > iota((NSEQ, NSEQ), 1)).astype(BF)
    lens = lengths[...].astype(F32).astype(BF)
    lens8 = jnp.concatenate([lens, jnp.zeros((6, NSEQ), BF)], axis=0)
    starts_col = dot_nt(tri, lens8)
    starts_row = dot_nt(lens8, tri)
    for b in range(2):
        rows_c = (iota((WIN, NSEQ), 0) + first_row).astype(F32)
        st_r = starts_row[b : b + 1, :]
        anchor_c = jnp.max(jnp.where(st_r <= rows_c, st_r, 0.0), axis=1, keepdims=True)
        rows_r = (iota((NSEQ, WIN), 1) + first_row).astype(F32)
        st_c = starts_col[:, b : b + 1]
        anchor_r = jnp.max(jnp.where(st_c <= rows_r, st_c, 0.0), axis=0, keepdims=True)
        low = first_row.astype(F32)
        row_c = (iota((WIN, 1), 0) + first_row).astype(F32)
        row_r = (iota((1, WIN), 1) + first_row).astype(F32)
        own_c = (anchor_c >= low) & (anchor_c < low + BLOCK) & (row_c < TOKENS)
        own_r = (anchor_r >= low) & (anchor_r < low + BLOCK) & (row_r < TOKENS)
        distance = row_c - row_r
        allowed = (anchor_c == anchor_r) & own_c & own_r & (distance >= 0)
        clamped = jnp.maximum(distance, 0.0)
        for h in range(HEADS):
            rate = float(np.log(np.float32(1.0 - 2.0 ** (-5.0 - h))))
            decay[b, h] = jnp.where(allowed, jnp.exp(rate * clamped), 0.0)
        live[b * WIN : (b + 1) * WIN, :] = jnp.broadcast_to(own_c.astype(F32), (WIN, 128))
        flags[b] = jnp.broadcast_to((anchor_c[:BLOCK] >= low).astype(F32), (BLOCK, 128))
        position = jnp.minimum(row_c - anchor_c, float(WIN - 1))
        hot = (position == iota((WIN, WIN), 1).astype(F32)).astype(F32)
        values = lax.dot_general(
            hot, trig[...], (((1,), (0,)), ((), ())), preferred_element_type=F32, precision=lax.Precision.HIGHEST
        )
        sin = values[:, DK:]
        even = (iota((WIN, DK), 1) & 1) == 0
        cos[b * WIN : (b + 1) * WIN, :] = values[:, :DK]
        sin_a[b * WIN : (b + 1) * WIN, :] = jnp.where(even, -sin, 0.0)
        sin_b[b * WIN : (b + 1) * WIN, :] = jnp.where(even, 0.0, sin)
    pos = iota((1, D), 1)
    order[...] = (iota((D, D), 0) == source_feature(pos, me, 0)).astype(BF)
    for core in range(2):
        base = core * 256 + 192
        want = source_feature(base + iota((64, 1), 0), me, 0)
        have = source_feature(base + iota((1, 64), 1), me, 1)
        third[core] = (want == have).astype(BF)


def trig_table():
    frequency = 1.0 / 10000.0 ** np.linspace(0.0, 1.0, DK // 2, dtype=np.float32)
    frequency = np.repeat(frequency.astype(np.float32), 2)
    phases = np.arange(WIN, dtype=np.float32)[:, None] * frequency
    phases = phases.astype(np.float32).astype(np.float64)
    return np.concatenate([np.cos(phases), np.sin(phases)], axis=1).astype(np.float32)


def tables(me, lengths):
    return pl.pallas_call(
        tables_kernel,
        in_specs=[
            pl.BlockSpec(memory_space=pltpu.SMEM),
            pl.BlockSpec(memory_space=pltpu.VMEM),
            pl.BlockSpec(memory_space=pltpu.VMEM),
        ],
        out_shape=[
            jax.ShapeDtypeStruct((2, HEADS, WIN, WIN), F32),
            jax.ShapeDtypeStruct((ROWS, DK), F32),
            jax.ShapeDtypeStruct((ROWS, DK), F32),
            jax.ShapeDtypeStruct((ROWS, DK), F32),
            jax.ShapeDtypeStruct((ROWS, 128), F32),
            jax.ShapeDtypeStruct((2, BLOCK, 128), F32),
            jax.ShapeDtypeStruct((D, D), BF),
            jax.ShapeDtypeStruct((2, 64, 64), BF),
        ],
        compiler_params=pltpu.CompilerParams(vmem_limit_bytes=16 << 20),
    )(me, lengths, jnp.asarray(trig_table()))


def norm_parts(values):
    center = values - jnp.mean(values, axis=-1, keepdims=True)
    inv = lax.rsqrt(jnp.mean(center * center, axis=-1, keepdims=True) + NORM_EPSILON)
    return center * inv, inv


def norm_back(grad, hat, inv, gain):
    scaled = grad * gain
    mean_one = jnp.mean(scaled, axis=-1, keepdims=True)
    mean_two = jnp.mean(scaled * hat, axis=-1, keepdims=True)
    return inv * (scaled - mean_one - hat * mean_two)


def rotated(v, cos, sin_a, sin_b):
    return v * cos + pltpu.roll(v, DK - 1, 1) * sin_a + pltpu.roll(v, 1, 1) * sin_b


def rotated_back(v, cos, sin_a, sin_b):
    return v * cos - pltpu.roll(v, DK - 1, 1) * sin_a - pltpu.roll(v, 1, 1) * sin_b


def sigmoid(v):
    return 0.5 * jnp.tanh(0.5 * v) + 0.5


GELU_C = float(np.sqrt(2.0 / np.pi))


def gelu_tanh(v):
    return jnp.tanh(GELU_C * (v + 0.044715 * (v * v * v)))


class Saved:
    NAMES = ("x", "a", "q", "k", "v", "p", "r", "gp", "u", "m", "b", "up", "gt", "h")

    @staticmethod
    def shapes():
        wide, narrow = (ROWS, VP), (ROWS, D)
        return [
            (narrow, F32), (narrow, BF), (narrow, BF), (narrow, BF), (wide, BF), ((2, WIN, 2 * WIN), BF), (wide, F32),
            (wide, F32), (wide, BF), (narrow, F32), (narrow, BF), (wide, F32), (wide, F32), (wide, BF),
        ]

    def __init__(self, refs):
        for name, ref in zip(self.NAMES, refs):
            setattr(self, name, ref)


def head_masks(rows):
    lane = iota((rows, VP), 1)
    return lane < DV, (lane >= DV) & (lane < 2 * DV)


def forward(w, gb, sv, decay, cos, sin_a, sin_b):
    x = sv.x[...]
    hat, _ = norm_parts(x)
    sv.a[...] = (hat * gb[0:1, :] + gb[2:3, :]).astype(BF)
    a = sv.a[...]
    tabs = (cos[...], sin_a[...], sin_b[...])
    for h in range(HEADS):
        at = slice(h * DK, (h + 1) * DK)
        sv.q[:, at] = rotated(dot(a, w[:, Q0 + h * DK : Q0 + (h + 1) * DK]), *tabs).astype(BF)
        key = rotated(dot(a, w[:, K0 + h * DK : K0 + (h + 1) * DK]), *tabs) * DK ** (-0.5)
        sv.k[:, at] = key.astype(BF)
    sv.v[...] = dot(a, w[:, V0 : V0 + VP]).astype(BF)
    in_head = head_masks(WIN)
    for b in range(2):
        rows = slice(b * WIN, (b + 1) * WIN)
        for h in range(HEADS):
            at = slice(h * DK, (h + 1) * DK)
            scores = dot_nt(sv.q[rows, at], sv.k[rows, at])
            sv.p[b, :, h * WIN : (h + 1) * WIN] = (decay[b, h] * scores).astype(BF)
        v = sv.v[rows, :]
        both = jnp.concatenate([jnp.where(in_head[0], v, 0), jnp.where(in_head[1], v, 0)], axis=0)
        sv.r[rows, :] = dot(sv.p[b], both)
    sv.gp[...] = dot(a, w[:, S0 : S0 + VP])
    r = sv.r[...]
    scale = group_scale(r)
    gate = sv.gp[...]
    sv.u[...] = (r * scale * (gate * sigmoid(gate))).astype(BF)
    sv.m[...] = x + dot_nt(sv.u[...], w[:, O0 : O0 + VP])
    hat, _ = norm_parts(sv.m[...])
    sv.b[...] = (hat * gb[1:2, :] + gb[3:4, :]).astype(BF)
    b = sv.b[...]
    sv.up[...] = dot(b, w[:, U0 : U0 + VP])
    sv.gt[...] = dot(b, w[:, G0 : G0 + VP])
    up = sv.up[...]
    sv.h[...] = (0.5 * up * (1.0 + gelu_tanh(up)) * sv.gt[...]).astype(BF)
    return sv.m[...] + dot_nt(sv.h[...], w[:, D0 : D0 + VP])


def head_sums(values):
    first, second = head_masks(ROWS)
    return (
        jnp.sum(jnp.where(first, values, 0.0), axis=-1, keepdims=True),
        jnp.sum(jnp.where(second, values, 0.0), axis=-1, keepdims=True),
    )


def by_head(one, two):
    return jnp.where(iota((ROWS, VP), 1) < DV, one, two)


def group_scale(r):
    one, two = head_sums(r * r)
    return by_head(lax.rsqrt(one / DV + GROUP_EPSILON), lax.rsqrt(two / DV + GROUP_EPSILON))


def put_grad(own, oth, at, width, grad, third):
    low = grad.astype(BF)
    for core, out in ((0, own), (1, oth)):
        part = low[core * 256 : (core + 1) * 256]
        if third is None:
            out[:, at : at + width] = part
        else:
            out[0:192, at : at + width] = part[0:192]
            out[192:256, at : at + width] = dot_tn(third[core], part[192:256]).astype(BF)


def backward(w, gb, sv, decay, cos, sin_a, sin_b, g, own, oth, third):
    f = g.astype(BF)
    put_grad(own, oth, D0, VP, dot_tn(f, sv.h[...]), third)
    dh = dot(f, w[:, D0 : D0 + VP])
    up = sv.up[...]
    t = gelu_tanh(up)
    half = 0.5 * (1.0 + t)
    dgt = (dh * (up * half)).astype(BF)
    slope = half + 0.5 * up * (1.0 - t * t) * (GELU_C * (1.0 + 3 * 0.044715 * (up * up)))
    dup = (dh * sv.gt[...] * slope).astype(BF)
    b = sv.b[...]
    put_grad(own, oth, U0, VP, dot_tn(b, dup), third)
    put_grad(own, oth, G0, VP, dot_tn(b, dgt), third)
    db = dot_nt(dup, w[:, U0 : U0 + VP]) + dot_nt(dgt, w[:, G0 : G0 + VP])
    hat, inv = norm_parts(sv.m[...])
    dgain_two = jnp.sum(db * hat, axis=0, keepdims=True)
    dbias_two = jnp.sum(db, axis=0, keepdims=True)
    dm = g + norm_back(db, hat, inv, gb[1:2, :])
    e = dm.astype(BF)
    put_grad(own, oth, O0, VP, dot_tn(e, sv.u[...]), third)
    du = dot(e, w[:, O0 : O0 + VP])
    r = sv.r[...]
    scale = group_scale(r)
    gate = sv.gp[...]
    sig = sigmoid(gate)
    dgp = (du * (r * scale) * (sig * (1.0 + gate * (1.0 - sig)))).astype(BF)
    dn = du * (gate * sig)
    one, two = head_sums(dn * r)
    dr = (scale * dn - r * (scale * scale * scale) * by_head(one / DV, two / DV)).astype(BF)
    in_head = head_masks(WIN)
    tabs = (cos[...], sin_a[...], sin_b[...])
    dvs, dqs, dks = [], [[], []], [[], []]
    for bt in range(2):
        rows = slice(bt * WIN, (bt + 1) * WIN)
        part = dr[rows]
        both = jnp.concatenate([jnp.where(in_head[0], part, 0), jnp.where(in_head[1], part, 0)], axis=0)
        p = sv.p[bt]
        stacked = jnp.concatenate([p[:, :WIN], p[:, WIN:]], axis=0)
        dvs.append(dot_tn(stacked, both).astype(BF))
        dp = dot_nt(both, sv.v[rows, :])
        for h in range(HEADS):
            at = slice(h * DK, (h + 1) * DK)
            ds = (decay[bt, h] * dp[h * WIN : (h + 1) * WIN]).astype(BF)
            dqs[h].append(dot(ds, sv.k[rows, at]))
            dks[h].append(dot_tn(ds, sv.q[rows, at]))
    dv = jnp.concatenate(dvs, axis=0)
    dq = jnp.concatenate([rotated_back(jnp.concatenate(dqs[h], axis=0), *tabs).astype(BF) for h in range(HEADS)], axis=1)
    dk = jnp.concatenate(
        [rotated_back(jnp.concatenate(dks[h], axis=0) * DK ** (-0.5), *tabs).astype(BF) for h in range(HEADS)], axis=1
    )
    a = sv.a[...]
    put_grad(own, oth, Q0, 512, dot_tn(a, dq), third)
    put_grad(own, oth, K0, 512, dot_tn(a, dk), third)
    put_grad(own, oth, S0, VP, dot_tn(a, dgp), third)
    da = dot_nt(dq, w[:, Q0 : Q0 + 512]) + dot_nt(dk, w[:, K0 : K0 + 512])
    da = da + dot_nt(dv, w[:, V0 : V0 + VP]) + dot_nt(dgp, w[:, S0 : S0 + VP])
    hat, inv = norm_parts(sv.x[...])
    dgain_one = jnp.sum(da * hat, axis=0, keepdims=True)
    dbias_one = jnp.sum(da, axis=0, keepdims=True)
    norms = jnp.concatenate([dgain_one, dgain_two, dbias_one, dbias_two, jnp.zeros((4, D), F32)], axis=0).astype(BF)
    spread = (iota((8, VP), 1) == iota((8, VP), 0) + 864).astype(BF)
    put_grad(own, oth, V0, VP, dot_tn(a, dv) + dot_tn(norms, spread), third)
    return dm + norm_back(da, hat, inv, gb[0:1, :])


def layers_kernel(*refs):
    pieces = refs[:24]
    (x_in, x_next, g_in, g_next, decay, cos, sin_a, sin_b, live, order, third) = refs[24:35]
    out, grad, own1, oth1, own0, oth0 = refs[35:41]
    w, gb, sems = refs[41:44]
    n = len(Saved.NAMES)
    saved = [Saved(refs[44 : 44 + n]), Saved(refs[44 + n : 44 + 2 * n])]
    copies = []
    for layer in range(2):
        for core in range(2):
            for row in range(4):
                color, unit = COLOR_OF[(layer, row)]
                for k in range(4):
                    piece = pieces[core * 12 + color * 4 + k]
                    at = core * 256 + row * 64 + k * 16
                    copies.append(
                        pltpu.make_async_copy(
                            piece.at[:, unit * WIDTH : (unit + 1) * WIDTH],
                            w.at[layer, at : at + 16, :],
                            sems.at[len(copies)],
                        )
                    )
    for copy in copies:
        copy.start()
    for b in range(2):
        rows = slice(b * WIN, b * WIN + BLOCK)
        later = slice(b * WIN + BLOCK, (b + 1) * WIN)
        saved[0].x[rows, :] = dot(x_in[b], order[...])
        saved[0].x[later, :] = dot(x_next[b], order[...])
    for copy in copies:
        copy.wait()
    for core in range(2):
        at = slice(core * 256 + 192, core * 256 + 256)
        w[1, at, :] = dot(third[core], w[1, at, :]).astype(BF)
    pick = ((iota((8, 128), 1) == iota((8, 128), 0) + NORM_LANE) & (iota((8, 128), 0) < 4)).astype(BF)
    for layer in range(2):
        gb[layer] = dot_nt(pick, w[layer, :, V0 + 768 : V0 + VP])
    tabs = (decay, cos, sin_a, sin_b)
    saved[1].x[...] = forward(w.at[0], gb.at[0], saved[0], *tabs)
    last = forward(w.at[1], gb.at[1], saved[1], *tabs).astype(BF)
    out[...] = dot_nt(last, order[...]).astype(BF)
    gs = []
    for b in range(2):
        gs.append(dot(g_in[b], order[...]))
        gs.append(dot(g_next[b], order[...]))
    g = jnp.concatenate(gs, axis=0) * live[:, 0:1]
    g = backward(w.at[1], gb.at[1], saved[1], *tabs, g, own1, oth1, third)
    g = backward(w.at[0], gb.at[0], saved[0], *tabs, g, own0, oth0, None)
    grad[...] = dot_nt(g.astype(BF), order[...]).astype(BF)


def layers(pieces, x_in, x_next, g_in, g_next, tabs):
    decay, cos, sin_a, sin_b, live, order, third = tabs
    grads = jax.ShapeDtypeStruct((256, WIDTH), BF)
    rows = jax.ShapeDtypeStruct((ROWS, D), BF)
    any_space = pl.BlockSpec(memory_space=pl.ANY)
    vmem = pl.BlockSpec(memory_space=pltpu.VMEM)
    return pl.pallas_call(
        layers_kernel,
        in_specs=[any_space] * 24 + [vmem] * 11,
        out_specs=[vmem] * 6,
        out_shape=[rows, rows, grads, grads, grads, grads],
        scratch_shapes=[
            pltpu.VMEM((2, D, WIDTH), BF),
            pltpu.VMEM((2, 8, D), F32),
            pltpu.SemaphoreType.DMA((64,)),
        ]
        + [pltpu.VMEM(shape, dtype) for _ in range(2) for shape, dtype in Saved.shapes()],
        compiler_params=pltpu.CompilerParams(vmem_limit_bytes=60 << 20),
    )(*pieces, x_in, x_next, g_in, g_next, decay, cos, sin_a, sin_b, live, order, third)


def pair_sum_kernel(own0, got0, own1, got1, *outs):
    for color, units in enumerate(UNITS):
        for k, (layer, row) in enumerate(units):
            own, got = ((own0, got0), (own1, got1))[layer]
            at = slice(row * 64, (row + 1) * 64)
            total = (own[at, :].astype(F32) + got[at, :].astype(F32)).astype(BF)
            outs[2 * color][:, k * WIDTH : (k + 1) * WIDTH] = total[:32]
            outs[2 * color + 1][:, k * WIDTH : (k + 1) * WIDTH] = total[32:]


def pair_sum(own0, got0, own1, got1):
    return pl.pallas_call(
        pair_sum_kernel,
        out_shape=[jax.ShapeDtypeStruct((32, w), BF) for w in WIDE for _ in range(2)],
        compiler_params=pltpu.CompilerParams(vmem_limit_bytes=40 << 20),
    )(own0, got0, own1, got1)


def halve_kernel(keep, got, keep_out, send_out):
    total = (keep[...].astype(F32) + got[...].astype(F32)).astype(BF)
    keep_out[...] = total[:16]
    send_out[...] = total[16:]


def halve(keep, got):
    shape = jax.ShapeDtypeStruct((16, keep.shape[1]), BF)
    return pl.pallas_call(
        halve_kernel,
        out_shape=[shape, shape],
        compiler_params=pltpu.CompilerParams(vmem_limit_bytes=16 << 20),
    )(keep, got)


def lines_kernel(keep, got, keep_out, send_out):
    swap = swap_rows()
    lines = keep.shape[1] // 128
    for i in range(0, keep_out.shape[1], 16):
        parts = []
        for k in range(16):
            if i + k < lines:
                at = slice((i + k) * 128, (i + k + 1) * 128)
                parts.append((keep[:, at].astype(F32) + got[:, at].astype(F32)).astype(BF))
            else:
                parts.append(jnp.zeros((16, 128), BF))
        turned = dot(swap, jnp.concatenate(parts, axis=0)).astype(BF).reshape(16, 16, 128)
        keep_out[:, i : i + 16, :] = turned[:8]
        send_out[:, i : i + 16, :] = turned[8:]


def to_lines(keep, got, lines):
    shape = jax.ShapeDtypeStruct((8, lines, 128), BF)
    return pl.pallas_call(
        lines_kernel,
        out_shape=[shape, shape],
        compiler_params=pltpu.CompilerParams(vmem_limit_bytes=16 << 20),
    )(keep, got)


def scatter_sum(own0, oth0, own1, oth1):
    got1 = lax.ppermute(oth1, "fsdp", CORE_PAIRS)
    got0 = lax.ppermute(oth0, "fsdp", CORE_PAIRS)
    halves = pair_sum(own0, got0, own1, got1)
    keep, send = list(halves[0::2]), list(halves[1::2])
    for c in range(3):
        got = lax.ppermute(send[c], "fsdp", step_pairs(c, 5))
        keep[c], send[c] = halve(keep[c], got)
    for c in range(3):
        got = lax.ppermute(send[c], "fsdp", step_pairs(c, 4))
        keep[c], send[c] = to_lines(keep[c], got, FLAT[c])
    for step in (3, 2, 1):
        for c in range(3):
            got = lax.ppermute(send[c], "fsdp", step_pairs(c, step))
            total = keep[c].astype(F32) + got.astype(F32)
            half = total.shape[0] // 2
            keep[c], send[c] = total[:half].astype(BF), total[half:].astype(BF)
    got = [lax.ppermute(send[c], "fsdp", step_pairs(c, 0)) for c in range(3)]
    return [k[0] for k in keep], [g[0] for g in got]


def unpack_kernel(a, b, c, a_got, b_got, c_got, q, k, v, s, o, u, g, d, gain, bias, row):
    row[...] = jnp.zeros_like(row)
    for mine, got, units in ((a, a_got, UNITS[0]), (b, b_got, UNITS[1]), (c, c_got, UNITS[2])):
        total = mine[...].astype(F32) + got[...].astype(F32)
        for n, (layer, r) in enumerate(units):
            for j in range(LINES):
                row[layer, r : r + 1, j * 128 : (j + 1) * 128] = total[n * LINES + j : n * LINES + j + 1]
    for layer in range(2):
        for out, at, width in ((q, Q0, 512), (k, K0, 512), (v, V0, 864), (s, S0, 864), (u, U0, 864), (g, G0, 864)):
            out[layer] = row[layer, 0:4, at : at + width]
        for out, at in ((o, O0), (d, D0)):
            out[layer] = jnp.transpose(row[layer, :, at : at + VP])[:864, 0:4]
        norms = jnp.transpose(row[layer, :, V0 + 768 : V0 + VP])
        for kind in range(2):
            gain[layer, kind : kind + 1, :] = norms[NORM_LANE + kind : NORM_LANE + kind + 1, 0:4]
            bias[layer, kind : kind + 1, :] = norms[NORM_LANE + 2 + kind : NORM_LANE + 3 + kind, 0:4]


def unpack(keep, got):
    shapes = [(2, 4, 512)] * 2 + [(2, 4, 864)] * 2 + [(2, 864, 4)] + [(2, 4, 864)] * 2 + [(2, 864, 4)] + [(2, 2, 4)] * 2
    return pl.pallas_call(
        unpack_kernel,
        out_shape=[jax.ShapeDtypeStruct(shape, F32) for shape in shapes],
        scratch_shapes=[pltpu.VMEM((2, 8, WIDTH), F32)],
    )(*keep, *got)


def from_behind(value, by):
    pairs = [(i, i + by) for i in range(128) if 0 <= i + by < 128]
    return lax.ppermute(value, "fsdp", pairs)


def local(inputs, cotangent, lengths, *weights):
    me = lax.axis_index("fsdp").astype(jnp.int32)
    flats = pack(*weights)
    x_next, g_next = from_behind(inputs, -1), from_behind(cotangent, -1)
    decay, cos, sin_a, sin_b, live, flags, order, third = tables(me[None], lengths)
    pieces = gather(flats)
    out, grad, own1, oth1, own0, oth0 = layers(
        pieces, inputs, x_next, cotangent, g_next, (decay, cos, sin_a, sin_b, live, order, third)
    )
    out, grad = out.reshape(2, WIN, D), grad.reshape(2, WIN, D)
    lent_out, lent_grad = from_behind(out[:, BLOCK:], 1), from_behind(grad[:, BLOCK:], 1)
    mine = flags[:, :, 0:1] > 0
    final_out = jnp.where(mine, out[:, :BLOCK], lent_out)
    final_grad = jnp.where(mine, grad[:, :BLOCK], lent_grad)
    keep, got = scatter_sum(own0, oth0, own1, oth1)
    return (final_out, final_grad, *unpack(keep, got))


def solution(mesh):
    rows, wide = P(None, "fsdp", None), P(None, None, "fsdp")
    weights = (rows, rows, rows, rows, wide, rows, rows, wide, wide, wide)
    return jax.shard_map(
        local,
        mesh=mesh,
        in_specs=(rows, rows, P(), *weights),
        out_specs=(rows, rows, *weights),
        check_vma=False,
    )
```

```python
import functools

import jax
import jax.numpy as jnp
import numpy as np
from jax import lax
from jax.experimental import pallas as pl
from jax.experimental.pallas import tpu as pltpu
from jax.sharding import PartitionSpec as P

HEADS = 2
DK = 256
DV = 432
D = 512
ROWS = 256
WIN = 128
BLOCK = 64
TOKENS = 8192
NSEQ = 192
NORM_EPSILON = 1e-05
GROUP_EPSILON = 1.0
BF = jnp.bfloat16
F32 = jnp.float32

Q0, K0, V0, S0, O0, U0, G0, D0, WIDTH = 0, 512, 1024, 1920, 2816, 3712, 4608, 5504, 6400
VP = 896
NORM_LANE = 96
LINES = WIDTH // 128
LAYERS_VMEM = 44 << 20

UNITS = (((0, 0), (1, 0), (0, 3)), ((0, 1), (1, 1), (1, 3)), ((0, 2), (1, 2)))
AXES = ("xzy", "zyx", "yxz")
FLAT = (160, 160, 112)
WIDE = tuple(len(u) * WIDTH for u in UNITS)
COLOR_OF = {unit: (c, k) for c, units in enumerate(UNITS) for k, unit in enumerate(units)}
STRIDE = {"x": 32, "z": 8, "y": 2}
STEPS = tuple((2 - k // 2, k % 2) for k in range(6))


def mask_of(core, second):
    return 3 if (core == 0) == bool(second) else 1


def step_pairs(color, step):
    stage, second = STEPS[step]
    stride = STRIDE[AXES[color][stage]]
    return [(i, i ^ (mask_of(i & 1, second) * stride)) for i in range(128)]


CORE_PAIRS = [(i, i ^ 1) for i in range(128)]


def dot(a, b):
    return lax.dot_general(a, b, (((1,), (0,)), ((), ())), preferred_element_type=F32)


def dot_nt(a, b):
    return lax.dot_general(a, b, (((1,), (1,)), ((), ())), preferred_element_type=F32)


def dot_tn(a, b):
    return lax.dot_general(a, b, (((0,), (0,)), ((), ())), preferred_element_type=F32)


def iota(shape, dim):
    return lax.broadcasted_iota(jnp.int32, shape, dim)


def source_feature(pos, me, third_color):
    core = (me & 1) ^ (pos >> 8)
    row = (pos >> 6) & 3
    color = jnp.where(row == 3, third_color, row)
    device = (me & ~1) | core
    first = jnp.where(core == 0, 1, 3)
    second = jnp.where(core == 0, 3, 1)
    for step, (stage, later) in enumerate(STEPS):
        bit = (pos >> step) & 1
        mask = second if later else first
        strides = [STRIDE[AXES[c][stage]] for c in range(3)]
        stride = jnp.where(color == 0, strides[0], jnp.where(color == 1, strides[1], strides[2]))
        device = device ^ (bit * mask * stride)
    return device * 4 + row


def swap_rows():
    r, c = iota((256, 256), 0), iota((256, 256), 1)
    return (((r & 15) * 16 + (r >> 4)) == c).astype(BF)


def pack_kernel(q, k, v, s, o, u, g, d, gain, bias, x, cot, a_ref, b_ref, c_ref, both, row):
    both[0] = x[...]
    both[1] = cot[...]
    row[...] = jnp.zeros_like(row)
    for layer in range(2):
        for weight, at, width in (
            (q, Q0, 512), (k, K0, 512), (v, V0, 864), (s, S0, 864), (o, O0, 864), (u, U0, 864), (g, G0, 864), (d, D0, 864),
        ):
            row[layer, 0:4, at : at + width] = weight[layer].astype(F32)
        norms = jnp.concatenate(
            [part[layer, kind : kind + 1].astype(F32) for part in (gain, bias) for kind in range(2)], axis=0
        ).astype(BF)
        spread = (iota((4, 128), 1) == iota((4, 128), 0) + NORM_LANE).astype(BF)
        row[layer, 0:4, V0 + 768 : V0 + 896] = row[layer, 0:4, V0 + 768 : V0 + 896] + dot_tn(norms, spread)
    for out, units, lines in zip((a_ref, b_ref, c_ref), UNITS, FLAT):
        pieces = []
        for layer, r in units:
            for j in range(LINES):
                pieces.append(row[layer, r : r + 1, j * 128 : (j + 1) * 128])
        pad = lines - len(pieces)
        out[0] = jnp.concatenate(pieces + [jnp.zeros((pad, 128), F32)], axis=0).astype(BF)


def pack(weights, inputs, cotangent):
    return pl.pallas_call(
        pack_kernel,
        out_shape=[jax.ShapeDtypeStruct((1, n, 128), BF) for n in FLAT] + [jax.ShapeDtypeStruct((2, 2, BLOCK, D), BF)],
        scratch_shapes=[pltpu.VMEM((2, 8, WIDTH), F32)],
    )(*weights, inputs, cotangent)


def rows_kernel(a, b, c, a_out, b_out, c_out):
    swap = swap_rows()
    for src, out, wide in zip((a, b, c), (a_out, b_out, c_out), WIDE):
        lines = wide // 128
        for i in range(0, lines, 16):
            block = src[:, i : i + 16, :].reshape(256, 128)
            turned = dot(swap, block).astype(BF)
            for k in range(min(16, lines - i)):
                out[:, (i + k) * 128 : (i + k + 1) * 128] = turned[k * 16 : (k + 1) * 16]


def to_rows(flats):
    return pl.pallas_call(
        rows_kernel,
        out_shape=[jax.ShapeDtypeStruct((16, w), BF) for w in WIDE],
        compiler_params=pltpu.CompilerParams(vmem_limit_bytes=16 << 20),
    )(*flats)


def stack_kernel(a, b, c, a_got, b_got, c_got, a_out, b_out, c_out):
    for mine, got, out in ((a, a_got, a_out), (b, b_got, b_out), (c, c_got, c_out)):
        n = mine.shape[0]
        out[0:n] = mine[...]
        out[n : 2 * n] = got[...]


def stack(mine, got):
    return pl.pallas_call(
        stack_kernel,
        out_shape=[jax.ShapeDtypeStruct((2 * m.shape[0], *m.shape[1:]), BF) for m in mine],
        compiler_params=pltpu.CompilerParams(vmem_limit_bytes=16 << 20),
    )(*mine, *got)


def stack_all_kernel(a, b, c, a_got, b_got, c_got, a_out, b_out, c_out, every):
    at = 0
    for mine, got, out in ((a, a_got, a_out), (b, b_got, b_out), (c, c_got, c_out)):
        width = mine.shape[1]
        out[0:16] = mine[...]
        out[16:32] = got[...]
        every[0:16, at : at + width] = mine[...]
        every[16:32, at : at + width] = got[...]
        at += width


def stack_all(mine, got):
    return pl.pallas_call(
        stack_all_kernel,
        out_shape=[jax.ShapeDtypeStruct((32, w), BF) for w in (*WIDE, sum(WIDE))],
        compiler_params=pltpu.CompilerParams(vmem_limit_bytes=24 << 20),
    )(*mine, *got)


def permute_all(values, step):
    return [lax.ppermute(values[c], "fsdp", step_pairs(c, step)) for c in range(3)]


def swap_cores(value):
    return lax.ppermute(value, "fsdp", CORE_PAIRS)


def gather(flats, early):
    cur = flats
    for step in range(4):
        cur = stack(cur, permute_all(cur, step))
        if step == 1:
            cur, early = lax.optimization_barrier((cur, early))
    first = to_rows(cur)
    *halves, every = stack_all(first, permute_all(first, 4))
    rest = permute_all(halves, 5)
    return [every, *rest, swap_cores(every), *[swap_cores(r) for r in rest]], early


def tables_kernel(me_ref, lengths, trig, decay, cos, sin_a, sin_b, live, flags, order, third):
    me = me_ref[0]
    first_row = me * BLOCK
    tri = (iota((NSEQ, NSEQ), 0) > iota((NSEQ, NSEQ), 1)).astype(BF)
    lens = lengths[...].astype(F32).astype(BF)
    lens8 = jnp.concatenate([lens, jnp.zeros((6, NSEQ), BF)], axis=0)
    starts_col = dot_nt(tri, lens8)
    starts_row = dot_nt(lens8, tri)
    for b in range(2):
        rows_c = (iota((WIN, NSEQ), 0) + first_row).astype(F32)
        st_r = starts_row[b : b + 1, :]
        anchor_c = jnp.max(jnp.where(st_r <= rows_c, st_r, 0.0), axis=1, keepdims=True)
        rows_r = (iota((NSEQ, WIN), 1) + first_row).astype(F32)
        st_c = starts_col[:, b : b + 1]
        anchor_r = jnp.max(jnp.where(st_c <= rows_r, st_c, 0.0), axis=0, keepdims=True)
        low = first_row.astype(F32)
        row_c = (iota((WIN, 1), 0) + first_row).astype(F32)
        row_r = (iota((1, WIN), 1) + first_row).astype(F32)
        own_c = (anchor_c >= low) & (anchor_c < low + BLOCK) & (row_c < TOKENS)
        own_r = (anchor_r >= low) & (anchor_r < low + BLOCK) & (row_r < TOKENS)
        distance = row_c - row_r
        allowed = (anchor_c == anchor_r) & own_c & own_r & (distance >= 0)
        clamped = jnp.maximum(distance, 0.0)
        for h in range(HEADS):
            rate = float(np.log(np.float32(1.0 - 2.0 ** (-5.0 - h))))
            decay[b, h] = jnp.where(allowed, jnp.exp(rate * clamped), 0.0)
        live[b * WIN : (b + 1) * WIN, :] = jnp.broadcast_to(own_c.astype(F32), (WIN, 128))
        flags[b] = jnp.broadcast_to((anchor_c[:BLOCK] >= low).astype(F32), (BLOCK, 128))
        position = jnp.minimum(row_c - anchor_c, float(WIN - 1))
        hot = (position == iota((WIN, WIN), 1).astype(F32)).astype(F32)
        values = lax.dot_general(
            hot, trig[...], (((1,), (0,)), ((), ())), preferred_element_type=F32, precision=lax.Precision.HIGHEST
        )
        sin = values[:, DK:]
        even = (iota((WIN, DK), 1) & 1) == 0
        cos[b * WIN : (b + 1) * WIN, :] = values[:, :DK]
        sin_a[b * WIN : (b + 1) * WIN, :] = jnp.where(even, -sin, 0.0)
        sin_b[b * WIN : (b + 1) * WIN, :] = jnp.where(even, 0.0, sin)
    pos = iota((1, D), 1)
    order[...] = (iota((D, D), 0) == source_feature(pos, me, 0)).astype(BF)
    for core in range(2):
        base = core * 256 + 192
        want = source_feature(base + iota((64, 1), 0), me, 0)
        have = source_feature(base + iota((1, 64), 1), me, 1)
        third[core] = (want == have).astype(BF)


def trig_table():
    frequency = 1.0 / 10000.0 ** np.linspace(0.0, 1.0, DK // 2, dtype=np.float32)
    frequency = np.repeat(frequency.astype(np.float32), 2)
    phases = np.arange(WIN, dtype=np.float32)[:, None] * frequency
    phases = phases.astype(np.float32).astype(np.float64)
    return np.concatenate([np.cos(phases), np.sin(phases)], axis=1).astype(np.float32)


def tables(me, lengths):
    return pl.pallas_call(
        tables_kernel,
        in_specs=[
            pl.BlockSpec(memory_space=pltpu.SMEM),
            pl.BlockSpec(memory_space=pltpu.VMEM),
            pl.BlockSpec(memory_space=pltpu.VMEM),
        ],
        out_shape=[
            jax.ShapeDtypeStruct((2, HEADS, WIN, WIN), F32),
            jax.ShapeDtypeStruct((ROWS, DK), F32),
            jax.ShapeDtypeStruct((ROWS, DK), F32),
            jax.ShapeDtypeStruct((ROWS, DK), F32),
            jax.ShapeDtypeStruct((ROWS, 128), F32),
            jax.ShapeDtypeStruct((2, BLOCK, 128), F32),
            jax.ShapeDtypeStruct((D, D), BF),
            jax.ShapeDtypeStruct((2, 64, 64), BF),
        ],
        compiler_params=pltpu.CompilerParams(vmem_limit_bytes=16 << 20),
    )(me, lengths, jnp.asarray(trig_table()))


def norm_parts(values):
    center = values - jnp.mean(values, axis=-1, keepdims=True)
    inv = lax.rsqrt(jnp.mean(center * center, axis=-1, keepdims=True) + NORM_EPSILON)
    return center * inv, inv


def norm_back(grad, hat, inv, gain):
    scaled = grad * gain
    mean_one = jnp.mean(scaled, axis=-1, keepdims=True)
    mean_two = jnp.mean(scaled * hat, axis=-1, keepdims=True)
    return inv * (scaled - mean_one - hat * mean_two)


def rotated(v, cos, sin_a, sin_b):
    return v * cos + pltpu.roll(v, DK - 1, 1) * sin_a + pltpu.roll(v, 1, 1) * sin_b


def rotated_back(v, cos, sin_a, sin_b):
    return v * cos - pltpu.roll(v, DK - 1, 1) * sin_a - pltpu.roll(v, 1, 1) * sin_b


def sigmoid(v):
    return 0.5 * jnp.tanh(0.5 * v) + 0.5


GELU_C = float(np.sqrt(2.0 / np.pi))


def gelu_tanh(v):
    return jnp.tanh(GELU_C * (v + 0.044715 * (v * v * v)))


class Saved:
    NAMES = ("x", "a", "q", "k", "v", "p", "r", "gp", "u", "m", "b", "up", "gt", "h")

    @staticmethod
    def shapes():
        wide, narrow = (ROWS, VP), (ROWS, D)
        return [
            (narrow, F32), (narrow, BF), (narrow, BF), (narrow, BF), (wide, BF), ((2, WIN, 2 * WIN), BF), (wide, F32),
            (wide, F32), (wide, BF), (narrow, F32), (narrow, BF), (wide, F32), (wide, F32), (wide, BF),
        ]

    def __init__(self, refs):
        for name, ref in zip(self.NAMES, refs):
            setattr(self, name, ref)


def head_masks(rows):
    lane = iota((rows, VP), 1)
    return lane < DV, (lane >= DV) & (lane < 2 * DV)


def forward(w, gb, sv, decay, cos, sin_a, sin_b):
    x = sv.x[...]
    hat, _ = norm_parts(x)
    sv.a[...] = (hat * gb[0:1, :] + gb[2:3, :]).astype(BF)
    a = sv.a[...]
    tabs = (cos[...], sin_a[...], sin_b[...])
    for h in range(HEADS):
        at = slice(h * DK, (h + 1) * DK)
        sv.q[:, at] = rotated(w.times(a, Q0 + h * DK, DK), *tabs).astype(BF)
        key = rotated(w.times(a, K0 + h * DK, DK), *tabs) * DK ** (-0.5)
        sv.k[:, at] = key.astype(BF)
    sv.v[...] = w.times(a, V0, VP).astype(BF)
    in_head = head_masks(WIN)
    for b in range(2):
        rows = slice(b * WIN, (b + 1) * WIN)
        for h in range(HEADS):
            at = slice(h * DK, (h + 1) * DK)
            scores = dot_nt(sv.q[rows, at], sv.k[rows, at])
            sv.p[b, :, h * WIN : (h + 1) * WIN] = (decay[b, h] * scores).astype(BF)
        v = sv.v[rows, :]
        both = jnp.concatenate([jnp.where(in_head[0], v, 0), jnp.where(in_head[1], v, 0)], axis=0)
        sv.r[rows, :] = dot(sv.p[b], both)
    sv.gp[...] = w.times(a, S0, VP)
    r = sv.r[...]
    scale = group_scale(r)
    gate = sv.gp[...]
    sv.u[...] = (r * scale * (gate * sigmoid(gate))).astype(BF)
    sv.m[...] = x + w.turned(sv.u[...], O0, VP)
    hat, _ = norm_parts(sv.m[...])
    sv.b[...] = (hat * gb[1:2, :] + gb[3:4, :]).astype(BF)
    b = sv.b[...]
    sv.up[...] = w.times(b, U0, VP)
    sv.gt[...] = w.times(b, G0, VP)
    up = sv.up[...]
    sv.h[...] = (0.5 * up * (1.0 + gelu_tanh(up)) * sv.gt[...]).astype(BF)
    return sv.m[...] + w.turned(sv.h[...], D0, VP)


def head_sums(values):
    first, second = head_masks(ROWS)
    return (
        jnp.sum(jnp.where(first, values, 0.0), axis=-1, keepdims=True),
        jnp.sum(jnp.where(second, values, 0.0), axis=-1, keepdims=True),
    )


def by_head(one, two):
    return jnp.where(iota((ROWS, VP), 1) < DV, one, two)


def group_scale(r):
    one, two = head_sums(r * r)
    return by_head(lax.rsqrt(one / DV + GROUP_EPSILON), lax.rsqrt(two / DV + GROUP_EPSILON))


class Weights:
    def __init__(self, own, oth, third):
        self.own, self.oth, self.third = own, oth, third

    def times(self, a, at, width):
        one = dot(a[:, :256], self.own[:, at : at + width])
        return one + dot(a[:, 256:], self.oth[:, at : at + width])

    def turned(self, a, at, width):
        return jnp.concatenate([dot_nt(a, self.own[:, at : at + width]), dot_nt(a, self.oth[:, at : at + width])], axis=1)

    def put(self, at, width, grad):
        low = grad.astype(BF)
        for core, out in ((0, self.own), (1, self.oth)):
            part = low[core * 256 : (core + 1) * 256]
            if self.third is None:
                out[:, at : at + width] = part
            else:
                out[0:192, at : at + width] = part[0:192]
                out[192:256, at : at + width] = dot_tn(self.third[core], part[192:256]).astype(BF)


def backward(w, gb, sv, decay, cos, sin_a, sin_b, g):
    f = g.astype(BF)
    dh = w.times(f, D0, VP)
    w.put(D0, VP, dot_tn(f, sv.h[...]))
    up = sv.up[...]
    t = gelu_tanh(up)
    half = 0.5 * (1.0 + t)
    dgt = (dh * (up * half)).astype(BF)
    slope = half + 0.5 * up * (1.0 - t * t) * (GELU_C * (1.0 + 3 * 0.044715 * (up * up)))
    dup = (dh * sv.gt[...] * slope).astype(BF)
    b = sv.b[...]
    db = w.turned(dup, U0, VP) + w.turned(dgt, G0, VP)
    w.put(U0, VP, dot_tn(b, dup))
    w.put(G0, VP, dot_tn(b, dgt))
    hat, inv = norm_parts(sv.m[...])
    dgain_two = jnp.sum(db * hat, axis=0, keepdims=True)
    dbias_two = jnp.sum(db, axis=0, keepdims=True)
    dm = g + norm_back(db, hat, inv, gb[1:2, :])
    e = dm.astype(BF)
    du = w.times(e, O0, VP)
    w.put(O0, VP, dot_tn(e, sv.u[...]))
    r = sv.r[...]
    scale = group_scale(r)
    gate = sv.gp[...]
    sig = sigmoid(gate)
    dgp = (du * (r * scale) * (sig * (1.0 + gate * (1.0 - sig)))).astype(BF)
    dn = du * (gate * sig)
    one, two = head_sums(dn * r)
    dr = (scale * dn - r * (scale * scale * scale) * by_head(one / DV, two / DV)).astype(BF)
    in_head = head_masks(WIN)
    tabs = (cos[...], sin_a[...], sin_b[...])
    dvs, dqs, dks = [], [[], []], [[], []]
    for bt in range(2):
        rows = slice(bt * WIN, (bt + 1) * WIN)
        part = dr[rows]
        both = jnp.concatenate([jnp.where(in_head[0], part, 0), jnp.where(in_head[1], part, 0)], axis=0)
        p = sv.p[bt]
        stacked = jnp.concatenate([p[:, :WIN], p[:, WIN:]], axis=0)
        dvs.append(dot_tn(stacked, both).astype(BF))
        dp = dot_nt(both, sv.v[rows, :])
        for h in range(HEADS):
            at = slice(h * DK, (h + 1) * DK)
            ds = (decay[bt, h] * dp[h * WIN : (h + 1) * WIN]).astype(BF)
            dqs[h].append(dot(ds, sv.k[rows, at]))
            dks[h].append(dot_tn(ds, sv.q[rows, at]))
    dv = jnp.concatenate(dvs, axis=0)
    dq = jnp.concatenate([rotated_back(jnp.concatenate(dqs[h], axis=0), *tabs).astype(BF) for h in range(HEADS)], axis=1)
    dk = jnp.concatenate(
        [rotated_back(jnp.concatenate(dks[h], axis=0) * DK ** (-0.5), *tabs).astype(BF) for h in range(HEADS)], axis=1
    )
    a = sv.a[...]
    da = w.turned(dq, Q0, 512) + w.turned(dk, K0, 512)
    da = da + w.turned(dv, V0, VP) + w.turned(dgp, S0, VP)
    w.put(Q0, 512, dot_tn(a, dq))
    w.put(K0, 512, dot_tn(a, dk))
    w.put(S0, VP, dot_tn(a, dgp))
    hat, inv = norm_parts(sv.x[...])
    dgain_one = jnp.sum(da * hat, axis=0, keepdims=True)
    dbias_one = jnp.sum(da, axis=0, keepdims=True)
    norms = jnp.concatenate([dgain_one, dgain_two, dbias_one, dbias_two, jnp.zeros((4, D), F32)], axis=0).astype(BF)
    spread = (iota((8, VP), 1) == iota((8, VP), 0) + 864).astype(BF)
    w.put(V0, VP, dot_tn(a, dv) + dot_tn(norms, spread))
    return dm + norm_back(da, hat, inv, gb[0:1, :])


def layers_kernel(*refs):
    pieces = refs[:8]
    x_in, g_in, next_in, decay, cos, sin_a, sin_b, live, order, third = refs[8:18]
    out, lent, own0, oth0, own1, oth1 = refs[18:24]
    gb, sems = refs[24:26]
    n = len(Saved.NAMES)
    saved = [Saved(refs[26 : 26 + n]), Saved(refs[26 + n : 26 + 2 * n])]
    held = ((own0, oth0), (own1, oth1))
    copies = []
    for layer in range(2):
        for core in range(2):
            for row in range(4):
                color, unit = COLOR_OF[(layer, row)]
                start = unit * WIDTH
                for half in range(2):
                    piece = pieces[core * 4 + (1 + color if half else 0)]
                    at = start if half else start + sum(WIDE[:color])
                    copies.append(
                        pltpu.make_async_copy(
                            piece.at[:, at : at + WIDTH],
                            held[layer][core].at[row * 64 + half * 32 : row * 64 + half * 32 + 32, :],
                            sems.at[len(copies)],
                        )
                    )
    for copy in copies:
        copy.start()
    for b in range(2):
        rows = slice(b * WIN, b * WIN + BLOCK)
        later = slice(b * WIN + BLOCK, (b + 1) * WIN)
        saved[0].x[rows, :] = dot(x_in[b], order[...])
        saved[0].x[later, :] = dot(next_in[0, b], order[...])
    for copy in copies:
        copy.wait()
    for core in range(2):
        at = slice(192, 256)
        held[1][core][at, :] = dot(third[core], held[1][core][at, :]).astype(BF)
    pick = ((iota((8, 128), 1) == iota((8, 128), 0) + NORM_LANE) & (iota((8, 128), 0) < 4)).astype(BF)
    weights = (Weights(own0, oth0, None), Weights(own1, oth1, third))
    for layer in range(2):
        gb[layer] = weights[layer].turned(pick, V0 + 768, 128)
    tabs = (decay, cos, sin_a, sin_b)
    saved[1].x[...] = forward(weights[0], gb.at[0], saved[0], *tabs)
    last = forward(weights[1], gb.at[1], saved[1], *tabs).astype(BF)
    last = dot_nt(last, order[...]).astype(BF)
    gs = []
    for b in range(2):
        gs.append(dot(g_in[b], order[...]))
        gs.append(dot(next_in[1, b], order[...]))
    g = jnp.concatenate(gs, axis=0) * live[:, 0:1]
    g = backward(weights[1], gb.at[1], saved[1], *tabs, g)
    g = backward(weights[0], gb.at[0], saved[0], *tabs, g)
    g = dot_nt(g.astype(BF), order[...]).astype(BF)
    for k, result in enumerate((last, g)):
        for b in range(2):
            out[k, b] = result[b * WIN : b * WIN + BLOCK]
            lent[k, b] = result[b * WIN + BLOCK : (b + 1) * WIN]


def layers(pieces, x_in, g_in, next_in, tabs):
    grads = jax.ShapeDtypeStruct((256, WIDTH), BF)
    rows = jax.ShapeDtypeStruct((2, 2, BLOCK, D), BF)
    any_space = pl.BlockSpec(memory_space=pl.ANY)
    vmem = pl.BlockSpec(memory_space=pltpu.VMEM)
    return pl.pallas_call(
        layers_kernel,
        in_specs=[any_space] * 8 + [vmem] * 10,
        out_specs=[vmem] * 6,
        out_shape=[rows, rows, grads, grads, grads, grads],
        scratch_shapes=[pltpu.VMEM((2, 8, D), F32), pltpu.SemaphoreType.DMA((32,))]
        + [pltpu.VMEM(shape, dtype) for _ in range(2) for shape, dtype in Saved.shapes()],
        compiler_params=pltpu.CompilerParams(vmem_limit_bytes=LAYERS_VMEM),
    )(*pieces, x_in, g_in, next_in, *tabs)


def pair_sum_kernel(own0, got0, own1, got1, *outs):
    for color, units in enumerate(UNITS):
        for k, (layer, row) in enumerate(units):
            own, got = ((own0, got0), (own1, got1))[layer]
            at = slice(row * 64, (row + 1) * 64)
            total = (own[at, :].astype(F32) + got[at, :].astype(F32)).astype(BF)
            outs[2 * color][:, k * WIDTH : (k + 1) * WIDTH] = total[:32]
            outs[2 * color + 1][:, k * WIDTH : (k + 1) * WIDTH] = total[32:]


def pair_sum(own0, got0, own1, got1):
    return pl.pallas_call(
        pair_sum_kernel,
        out_shape=[jax.ShapeDtypeStruct((32, w), BF) for w in WIDE for _ in range(2)],
        compiler_params=pltpu.CompilerParams(vmem_limit_bytes=40 << 20),
    )(own0, got0, own1, got1)


def halve_kernel(*refs):
    for c in range(3):
        total = (refs[c][...].astype(F32) + refs[3 + c][...].astype(F32)).astype(BF)
        half = total.shape[0] // 2
        refs[6 + 2 * c][...] = total[:half]
        refs[7 + 2 * c][...] = total[half:]


def halve(keep, got):
    shapes = [jax.ShapeDtypeStruct((k.shape[0] // 2, *k.shape[1:]), BF) for k in keep for _ in range(2)]
    halves = pl.pallas_call(
        halve_kernel, out_shape=shapes, compiler_params=pltpu.CompilerParams(vmem_limit_bytes=24 << 20)
    )(*keep, *got)
    return halves[0::2], halves[1::2]


def lines_kernel(*refs):
    swap = swap_rows()
    for c in range(3):
        keep, got, keep_out, send_out = refs[c], refs[3 + c], refs[6 + 2 * c], refs[7 + 2 * c]
        lines = keep.shape[1] // 128
        for i in range(0, keep_out.shape[1], 16):
            parts = []
            for k in range(16):
                if i + k < lines:
                    at = slice((i + k) * 128, (i + k + 1) * 128)
                    parts.append((keep[:, at].astype(F32) + got[:, at].astype(F32)).astype(BF))
                else:
                    parts.append(jnp.zeros((16, 128), BF))
            turned = dot(swap, jnp.concatenate(parts, axis=0)).astype(BF).reshape(16, 16, 128)
            keep_out[:, i : i + 16, :] = turned[:8]
            send_out[:, i : i + 16, :] = turned[8:]


def to_lines(keep, got):
    halves = pl.pallas_call(
        lines_kernel,
        out_shape=[jax.ShapeDtypeStruct((8, n, 128), BF) for n in FLAT for _ in range(2)],
        compiler_params=pltpu.CompilerParams(vmem_limit_bytes=24 << 20),
    )(*keep, *got)
    return halves[0::2], halves[1::2]


def scatter_sum(own0, got0, own1, got1):
    halves = pair_sum(own0, got0, own1, got1)
    keep, send = halves[0::2], halves[1::2]
    keep, send = halve(keep, permute_all(send, 5))
    keep, send = to_lines(keep, permute_all(send, 4))
    for step in (3, 2, 1):
        keep, send = halve(keep, permute_all(send, step))
    return keep, permute_all(send, 0)


def unpack_kernel(a, b, c, a_got, b_got, c_got, q, k, v, s, o, u, g, d, gain, bias, row):
    row[...] = jnp.zeros_like(row)
    for mine, got, units in ((a, a_got, UNITS[0]), (b, b_got, UNITS[1]), (c, c_got, UNITS[2])):
        total = mine[0].astype(F32) + got[0].astype(F32)
        for n, (layer, r) in enumerate(units):
            for j in range(LINES):
                row[layer, r : r + 1, j * 128 : (j + 1) * 128] = total[n * LINES + j : n * LINES + j + 1]
    for layer in range(2):
        for out, at, width in (
            (q, Q0, 512), (k, K0, 512), (v, V0, 864), (s, S0, 864), (o, O0, 864), (u, U0, 864), (g, G0, 864), (d, D0, 864),
        ):
            out[layer] = row[layer, 0:4, at : at + width]
        norms = jnp.transpose(row[layer, :, V0 + 768 : V0 + VP])
        for kind in range(2):
            gain[layer, kind : kind + 1, :] = norms[NORM_LANE + kind : NORM_LANE + kind + 1, 0:4]
            bias[layer, kind : kind + 1, :] = norms[NORM_LANE + 2 + kind : NORM_LANE + 3 + kind, 0:4]


def unpack(keep, got):
    shapes = [(2, 4, 512)] * 2 + [(2, 4, 864)] * 6 + [(2, 2, 4)] * 2
    return pl.pallas_call(
        unpack_kernel,
        out_shape=[jax.ShapeDtypeStruct(shape, F32) for shape in shapes],
        scratch_shapes=[pltpu.VMEM((2, 8, WIDTH), F32)],
    )(*keep, *got)


def from_behind(value, by):
    pairs = [(i, i + by) for i in range(128) if 0 <= i + by < 128]
    return lax.ppermute(value, "fsdp", pairs)


def local(inputs, cotangent, lengths, *weights):
    me = lax.axis_index("fsdp").astype(jnp.int32)
    q, k, v, s, o, u, g, d, gain, bias = weights
    o, d = jnp.swapaxes(o, 1, 2), jnp.swapaxes(d, 1, 2)
    *flats, both = pack((q, k, v, s, o, u, g, d, gain, bias), inputs, cotangent)
    early = (from_behind(both, -1), tables(me[None], lengths))
    pieces, (next_in, (decay, cos, sin_a, sin_b, live, flags, order, third)) = gather(flats, early)
    out, lent, own0, oth0, own1, oth1 = layers(
        pieces, inputs, cotangent, next_in, (decay, cos, sin_a, sin_b, live, order, third)
    )
    got0, got1 = swap_cores(oth0), swap_cores(oth1)
    final = jnp.where(flags[None, :, :, 0:1] > 0, out, from_behind(lent, 1))
    got0, got1, final = lax.optimization_barrier((got0, got1, final))
    keep, got = scatter_sum(own0, got0, own1, got1)
    q, k, v, s, o, u, g, d, gain, bias = unpack(keep, got)
    return final[0], final[1], q, k, v, s, jnp.swapaxes(o, 1, 2), u, g, jnp.swapaxes(d, 1, 2), gain, bias


def solution(mesh):
    rows, wide = P(None, "fsdp", None), P(None, None, "fsdp")
    weights = (rows, rows, rows, rows, wide, rows, rows, wide, wide, wide)
    return jax.shard_map(
        local,
        mesh=mesh,
        in_specs=(rows, rows, P(), *weights),
        out_specs=(rows, rows, *weights),
        check_vma=False,
    )
```

```python
import functools

import jax
import jax.numpy as jnp
import numpy as np
from jax import lax
from jax.experimental import pallas as pl
from jax.experimental.pallas import tpu as pltpu
from jax.sharding import PartitionSpec as P

HEADS = 2
DK = 256
DV = 432
D = 512
ROWS = 256
WIN = 128
BLOCK = 64
TOKENS = 8192
NSEQ = 192
NORM_EPSILON = 1e-05
GROUP_EPSILON = 1.0
BF = jnp.bfloat16
F32 = jnp.float32

Q0, K0, V0, S0, O0, U0, G0, D0, WIDTH = 0, 512, 1024, 1920, 2816, 3712, 4608, 5504, 6400
VP = 896
NORM_LANE = 96
LINES = WIDTH // 128
LAYERS_VMEM = 48 << 20
PAIR_VMEM = 24 << 20

UNITS = (((0, 0), (1, 0), (0, 3)), ((0, 1), (1, 1), (1, 3)), ((0, 2), (1, 2)))
FLAT = (160, 160, 112)
LINES_ALL = sum(FLAT)
WIDE = tuple(len(u) * WIDTH for u in UNITS)
COLOR_OF = {unit: (c, k) for c, units in enumerate(UNITS) for k, unit in enumerate(units)}
STRIDE = {"x": 32, "z": 8, "y": 2}
LOW_AXES = "xzy"
HIGH_AXES = ("yzx", "xyz", "zxy")


def mask_of(core, second):
    return 3 if (core == 0) == bool(second) else 1


def low_pairs(bits):
    flip = [(STRIDE[LOW_AXES[k]], bits >> k & 1) for k in range(3)]
    return [(i, i ^ sum(mask_of(i & 1, 0) * stride * bit for stride, bit in flip)) for i in range(128)]


def high_pairs(color, step):
    stride = STRIDE[HIGH_AXES[color][step]]
    return [(i, i ^ (mask_of(i & 1, 1) * stride)) for i in range(128)]


CORE_PAIRS = [(i, i ^ 1) for i in range(128)]


def dot(a, b):
    return lax.dot_general(a, b, (((1,), (0,)), ((), ())), preferred_element_type=F32)


def dot_nt(a, b):
    return lax.dot_general(a, b, (((1,), (1,)), ((), ())), preferred_element_type=F32)


def dot_tn(a, b):
    return lax.dot_general(a, b, (((0,), (0,)), ((), ())), preferred_element_type=F32)


def iota(shape, dim):
    return lax.broadcasted_iota(jnp.int32, shape, dim)


def source_feature(pos, me, third_color):
    core = (me & 1) ^ (pos >> 8)
    row = (pos >> 6) & 3
    color = jnp.where(row == 3, third_color, row)
    device = (me & ~1) | core
    first = jnp.where(core == 0, mask_of(0, 0), mask_of(1, 0))
    second = jnp.where(core == 0, mask_of(0, 1), mask_of(1, 1))
    for k in range(3):
        device = device ^ (((pos >> k) & 1) * first * STRIDE[LOW_AXES[k]])
        strides = [STRIDE[HIGH_AXES[c][k]] for c in range(3)]
        stride = jnp.where(color == 0, strides[0], jnp.where(color == 1, strides[1], strides[2]))
        device = device ^ (((pos >> (3 + k)) & 1) * second * stride)
    return device * 4 + row


def swap_rows():
    r, c = iota((256, 256), 0), iota((256, 256), 1)
    return (((r & 15) * 16 + (r >> 4)) == c).astype(BF)


def pack_kernel(*refs):
    given, (flat, both, row, sems), held = refs[:12], refs[12:16], refs[16:]
    copies = [pltpu.make_async_copy(src, dst, sems.at[k]) for k, (src, dst) in enumerate(zip(given, held))]
    for copy in copies:
        copy.start()
    q, k, v, s, o, u, g, d, gain, bias, x, cot = held
    row[...] = jnp.zeros_like(row)
    for copy in copies:
        copy.wait()
    both[0] = x[...]
    both[1] = cot[...]
    for layer in range(2):
        for weight, at, width in (
            (q, Q0, 512), (k, K0, 512), (v, V0, 864), (s, S0, 864), (o, O0, 864), (u, U0, 864), (g, G0, 864), (d, D0, 864),
        ):
            row[layer, 0:4, at : at + width] = weight[layer].astype(F32)
        norms = jnp.concatenate(
            [part[layer, kind : kind + 1].astype(F32) for part in (gain, bias) for kind in range(2)], axis=0
        ).astype(BF)
        spread = (iota((4, 128), 1) == iota((4, 128), 0) + NORM_LANE).astype(BF)
        row[layer, 0:4, V0 + 768 : V0 + 896] = row[layer, 0:4, V0 + 768 : V0 + 896] + dot_tn(norms, spread)
    for units, lines, start in zip(UNITS, FLAT, (0, FLAT[0], FLAT[0] + FLAT[1])):
        pieces = []
        for layer, r in units:
            for j in range(LINES):
                pieces.append(row[layer, r : r + 1, j * 128 : (j + 1) * 128])
        pad = lines - len(pieces)
        flat[start : start + lines] = jnp.concatenate(pieces + [jnp.zeros((pad, 128), F32)], axis=0).astype(BF)


def in_hbm(values):
    return [pltpu.with_memory_space_constraint(v, pltpu.HBM) for v in values]


def pack(weights, inputs, cotangent):
    values = (*weights, inputs, cotangent)
    return pl.pallas_call(
        pack_kernel,
        in_specs=[pl.BlockSpec(memory_space=pltpu.HBM)] * len(values),
        out_shape=[jax.ShapeDtypeStruct((LINES_ALL, 128), BF), jax.ShapeDtypeStruct((2, 2, BLOCK, D), BF)],
        scratch_shapes=[pltpu.VMEM((2, 8, WIDTH), F32), pltpu.SemaphoreType.DMA((len(values),))]
        + [pltpu.VMEM(v.shape, v.dtype) for v in values],
        compiler_params=pltpu.CompilerParams(vmem_limit_bytes=8 << 20),
    )(*in_hbm(values))


def stack_kernel(*refs):
    for k in range(8):
        start = 0
        for out, lines in zip(refs[8:], FLAT):
            out[k] = refs[k][start : start + lines]
            start += lines


def stack(parts):
    return pl.pallas_call(
        stack_kernel,
        out_shape=[jax.ShapeDtypeStruct((8, n, 128), BF) for n in FLAT],
        compiler_params=pltpu.CompilerParams(vmem_limit_bytes=16 << 20),
    )(*parts)


def rows_kernel(a, b, c, a_got, b_got, c_got, both, a_out, b_out, c_out, both_out):
    both_out[...] = both[...]
    swap = swap_rows()
    for src, got, out, wide in zip((a, b, c), (a_got, b_got, c_got), (a_out, b_out, c_out), WIDE):
        lines = wide // 128
        for i in range(0, lines, 16):
            at = slice(i, i + 16)
            block = jnp.concatenate([src[:, at, :].reshape(128, 128), got[:, at, :].reshape(128, 128)], axis=0)
            turned = dot(swap, block).astype(BF)
            for k in range(min(16, lines - i)):
                out[:, (i + k) * 128 : (i + k + 1) * 128] = turned[k * 16 : (k + 1) * 16]


def to_rows(mine, got, both):
    return pl.pallas_call(
        rows_kernel,
        out_shape=[jax.ShapeDtypeStruct((16, w), BF) for w in WIDE] + [jax.ShapeDtypeStruct(both.shape, BF)],
        compiler_params=pltpu.CompilerParams(vmem_limit_bytes=16 << 20),
    )(*mine, *got, both)


def stack_all_kernel(a, b, c, a_got, b_got, c_got, behind, a_out, b_out, c_out, every):
    del behind
    at = 0
    for mine, got, out in ((a, a_got, a_out), (b, b_got, b_out), (c, c_got, c_out)):
        width = mine.shape[1]
        out[0:16] = mine[...]
        out[16:32] = got[...]
        every[0:16, at : at + width] = mine[...]
        every[16:32, at : at + width] = got[...]
        at += width


def stack_all(mine, got, behind):
    vmem, anywhere = pl.BlockSpec(memory_space=pltpu.VMEM), pl.BlockSpec(memory_space=pl.ANY)
    return pl.pallas_call(
        stack_all_kernel,
        in_specs=[vmem] * 6 + [anywhere],
        out_shape=[jax.ShapeDtypeStruct((32, w), BF) for w in (*WIDE, sum(WIDE))],
        compiler_params=pltpu.CompilerParams(vmem_limit_bytes=24 << 20),
    )(*mine, *got, behind)


def permute_all(values, step):
    return [lax.ppermute(values[c], "fsdp", high_pairs(c, step)) for c in range(3)]


def swap_cores(value):
    return lax.ppermute(value, "fsdp", CORE_PAIRS)


def gather(flat, both):
    cur = stack([flat] + [lax.ppermute(flat, "fsdp", low_pairs(bits)) for bits in range(1, 8)])
    *first, both = to_rows(cur, permute_all(cur, 0), both)
    next_in = from_behind(both, -1)
    *halves, every = stack_all(first, permute_all(first, 1), next_in)
    rest = permute_all(halves, 2)
    return [every, *rest, swap_cores(every), *[swap_cores(r) for r in rest]], next_in


def tables_kernel(me_ref, lengths, trig, decay, cos, sin_a, sin_b, live, flags, order, third):
    me = me_ref[0]
    first_row = me * BLOCK
    tri = (iota((NSEQ, NSEQ), 0) > iota((NSEQ, NSEQ), 1)).astype(BF)
    lens = lengths[...].astype(F32).astype(BF)
    lens8 = jnp.concatenate([lens, jnp.zeros((6, NSEQ), BF)], axis=0)
    starts_col = dot_nt(tri, lens8)
    starts_row = dot_nt(lens8, tri)
    for b in range(2):
        rows_c = (iota((WIN, NSEQ), 0) + first_row).astype(F32)
        st_r = starts_row[b : b + 1, :]
        anchor_c = jnp.max(jnp.where(st_r <= rows_c, st_r, 0.0), axis=1, keepdims=True)
        rows_r = (iota((NSEQ, WIN), 1) + first_row).astype(F32)
        st_c = starts_col[:, b : b + 1]
        anchor_r = jnp.max(jnp.where(st_c <= rows_r, st_c, 0.0), axis=0, keepdims=True)
        low = first_row.astype(F32)
        row_c = (iota((WIN, 1), 0) + first_row).astype(F32)
        row_r = (iota((1, WIN), 1) + first_row).astype(F32)
        own_c = (anchor_c >= low) & (anchor_c < low + BLOCK) & (row_c < TOKENS)
        own_r = (anchor_r >= low) & (anchor_r < low + BLOCK) & (row_r < TOKENS)
        distance = row_c - row_r
        allowed = (anchor_c == anchor_r) & own_c & own_r & (distance >= 0)
        clamped = jnp.maximum(distance, 0.0)
        for h in range(HEADS):
            rate = float(np.log(np.float32(1.0 - 2.0 ** (-5.0 - h))))
            decay[b, h] = jnp.where(allowed, jnp.exp(rate * clamped), 0.0)
        live[b * WIN : (b + 1) * WIN, :] = jnp.broadcast_to(own_c.astype(F32), (WIN, 128))
        flags[b] = jnp.broadcast_to((anchor_c[:BLOCK] >= low).astype(F32), (BLOCK, 128))
        position = jnp.minimum(row_c - anchor_c, float(WIN - 1))
        hot = (position == iota((WIN, WIN), 1).astype(F32)).astype(F32)
        values = lax.dot_general(
            hot, trig[...], (((1,), (0,)), ((), ())), preferred_element_type=F32, precision=lax.Precision.HIGHEST
        )
        sin = values[:, DK:]
        even = (iota((WIN, DK), 1) & 1) == 0
        cos[b * WIN : (b + 1) * WIN, :] = values[:, :DK]
        sin_a[b * WIN : (b + 1) * WIN, :] = jnp.where(even, -sin, 0.0)
        sin_b[b * WIN : (b + 1) * WIN, :] = jnp.where(even, 0.0, sin)
    pos = iota((1, D), 1)
    order[...] = (iota((D, D), 0) == source_feature(pos, me, 0)).astype(BF)
    for core in range(2):
        base = core * 256 + 192
        want = source_feature(base + iota((64, 1), 0), me, 0)
        have = source_feature(base + iota((1, 64), 1), me, 1)
        third[core] = (want == have).astype(BF)


def trig_table():
    frequency = 1.0 / 10000.0 ** np.linspace(0.0, 1.0, DK // 2, dtype=np.float32)
    frequency = np.repeat(frequency.astype(np.float32), 2)
    phases = np.arange(WIN, dtype=np.float32)[:, None] * frequency
    phases = phases.astype(np.float32).astype(np.float64)
    return np.concatenate([np.cos(phases), np.sin(phases)], axis=1).astype(np.float32)


def tables(me, lengths):
    return pl.pallas_call(
        tables_kernel,
        in_specs=[
            pl.BlockSpec(memory_space=pltpu.SMEM),
            pl.BlockSpec(memory_space=pltpu.VMEM),
            pl.BlockSpec(memory_space=pltpu.VMEM),
        ],
        out_shape=[
            jax.ShapeDtypeStruct((2, HEADS, WIN, WIN), F32),
            jax.ShapeDtypeStruct((ROWS, DK), F32),
            jax.ShapeDtypeStruct((ROWS, DK), F32),
            jax.ShapeDtypeStruct((ROWS, DK), F32),
            jax.ShapeDtypeStruct((ROWS, 128), F32),
            jax.ShapeDtypeStruct((2, BLOCK, 128), F32),
            jax.ShapeDtypeStruct((D, D), BF),
            jax.ShapeDtypeStruct((2, 64, 64), BF),
        ],
        compiler_params=pltpu.CompilerParams(vmem_limit_bytes=16 << 20),
    )(me, lengths, jnp.asarray(trig_table()))


def norm_parts(values):
    center = values - jnp.mean(values, axis=-1, keepdims=True)
    inv = lax.rsqrt(jnp.mean(center * center, axis=-1, keepdims=True) + NORM_EPSILON)
    return center * inv, inv


def norm_back(grad, hat, inv, gain):
    scaled = grad * gain
    mean_one = jnp.mean(scaled, axis=-1, keepdims=True)
    mean_two = jnp.mean(scaled * hat, axis=-1, keepdims=True)
    return inv * (scaled - mean_one - hat * mean_two)


def rotated(v, cos, sin_a, sin_b):
    return v * cos + pltpu.roll(v, DK - 1, 1) * sin_a + pltpu.roll(v, 1, 1) * sin_b


def rotated_back(v, cos, sin_a, sin_b):
    return v * cos - pltpu.roll(v, DK - 1, 1) * sin_a - pltpu.roll(v, 1, 1) * sin_b


def sigmoid(v):
    return 0.5 * jnp.tanh(0.5 * v) + 0.5


GELU_C = float(np.sqrt(2.0 / np.pi))


def gelu_tanh(v):
    return jnp.tanh(GELU_C * (v + 0.044715 * (v * v * v)))


class Saved:
    NAMES = ("x", "a", "q", "k", "v", "p", "r", "gp", "u", "m", "b", "up", "gt", "h")

    @staticmethod
    def shapes():
        wide, narrow = (ROWS, VP), (ROWS, D)
        return [
            (narrow, F32), (narrow, BF), (narrow, BF), (narrow, BF), (wide, BF), ((2, WIN, 2 * WIN), BF), (wide, F32),
            (wide, F32), (wide, BF), (narrow, F32), (narrow, BF), (wide, F32), (wide, F32), (wide, BF),
        ]

    def __init__(self, refs):
        for name, ref in zip(self.NAMES, refs):
            setattr(self, name, ref)


def head_masks(rows):
    lane = iota((rows, VP), 1)
    return lane < DV, (lane >= DV) & (lane < 2 * DV)


def forward(w, gb, sv, decay, cos, sin_a, sin_b, later):
    x = sv.x[...]
    hat, _ = norm_parts(x)
    sv.a[...] = (hat * gb[0:1, :] + gb[2:3, :]).astype(BF)
    a = sv.a[...]
    tabs = (cos[...], sin_a[...], sin_b[...])
    for h in range(HEADS):
        at = slice(h * DK, (h + 1) * DK)
        sv.q[:, at] = rotated(w.times(a, Q0 + h * DK, DK), *tabs).astype(BF)
        key = rotated(w.times(a, K0 + h * DK, DK), *tabs) * DK ** (-0.5)
        sv.k[:, at] = key.astype(BF)
    sv.v[...] = w.times(a, V0, VP).astype(BF)
    in_head = head_masks(WIN)
    for b in range(2):
        rows = slice(b * WIN, (b + 1) * WIN)
        for h in range(HEADS):
            at = slice(h * DK, (h + 1) * DK)
            scores = dot_nt(sv.q[rows, at], sv.k[rows, at])
            sv.p[b, :, h * WIN : (h + 1) * WIN] = (decay[b, h] * scores).astype(BF)
        v = sv.v[rows, :]
        both = jnp.concatenate([jnp.where(in_head[0], v, 0), jnp.where(in_head[1], v, 0)], axis=0)
        sv.r[rows, :] = dot(sv.p[b], both)
    sv.gp[...] = w.times(a, S0, VP)
    for copy in later:
        copy.wait()
    r = sv.r[...]
    scale = group_scale(r)
    gate = sv.gp[...]
    sv.u[...] = (r * scale * (gate * sigmoid(gate))).astype(BF)
    sv.m[...] = x + w.turned(sv.u[...], O0, VP)
    hat, _ = norm_parts(sv.m[...])
    sv.b[...] = (hat * gb[1:2, :] + gb[3:4, :]).astype(BF)
    b = sv.b[...]
    sv.up[...] = w.times(b, U0, VP)
    sv.gt[...] = w.times(b, G0, VP)
    up = sv.up[...]
    sv.h[...] = (0.5 * up * (1.0 + gelu_tanh(up)) * sv.gt[...]).astype(BF)
    return sv.m[...] + w.turned(sv.h[...], D0, VP)


def head_sums(values):
    first, second = head_masks(ROWS)
    return (
        jnp.sum(jnp.where(first, values, 0.0), axis=-1, keepdims=True),
        jnp.sum(jnp.where(second, values, 0.0), axis=-1, keepdims=True),
    )


def by_head(one, two):
    return jnp.where(iota((ROWS, VP), 1) < DV, one, two)


def group_scale(r):
    one, two = head_sums(r * r)
    return by_head(lax.rsqrt(one / DV + GROUP_EPSILON), lax.rsqrt(two / DV + GROUP_EPSILON))


class Weights:
    def __init__(self, own, oth, third, outs, sems):
        self.own, self.oth, self.third, self.outs, self.sems = own, oth, third, outs, sems
        self.leaving = []

    def done(self, start, end):
        for ref, out in zip((self.own, self.oth), self.outs):
            copy = pltpu.make_async_copy(
                ref.at[:, start:end], out.at[:, start:end], self.sems.at[len(self.leaving)]
            )
            copy.start()
            self.leaving.append(copy)

    def times(self, a, at, width):
        one = dot(a[:, :256], self.own[:, at : at + width])
        return one + dot(a[:, 256:], self.oth[:, at : at + width])

    def turned(self, a, at, width):
        return jnp.concatenate([dot_nt(a, self.own[:, at : at + width]), dot_nt(a, self.oth[:, at : at + width])], axis=1)

    def put(self, at, width, grad):
        low = grad.astype(BF)
        for core, out in ((0, self.own), (1, self.oth)):
            part = low[core * 256 : (core + 1) * 256]
            if self.third is None:
                out[:, at : at + width] = part
            else:
                out[0:192, at : at + width] = part[0:192]
                out[192:256, at : at + width] = dot_tn(self.third[core], part[192:256]).astype(BF)


def backward(w, gb, sv, decay, cos, sin_a, sin_b, g):
    f = g.astype(BF)
    dh = w.times(f, D0, VP)
    w.put(D0, VP, dot_tn(f, sv.h[...]))
    w.done(D0, WIDTH)
    up = sv.up[...]
    t = gelu_tanh(up)
    half = 0.5 * (1.0 + t)
    dgt = (dh * (up * half)).astype(BF)
    slope = half + 0.5 * up * (1.0 - t * t) * (GELU_C * (1.0 + 3 * 0.044715 * (up * up)))
    dup = (dh * sv.gt[...] * slope).astype(BF)
    b = sv.b[...]
    db = w.turned(dup, U0, VP) + w.turned(dgt, G0, VP)
    w.put(U0, VP, dot_tn(b, dup))
    w.put(G0, VP, dot_tn(b, dgt))
    w.done(U0, D0)
    hat, inv = norm_parts(sv.m[...])
    dgain_two = jnp.sum(db * hat, axis=0, keepdims=True)
    dbias_two = jnp.sum(db, axis=0, keepdims=True)
    dm = g + norm_back(db, hat, inv, gb[1:2, :])
    e = dm.astype(BF)
    du = w.times(e, O0, VP)
    w.put(O0, VP, dot_tn(e, sv.u[...]))
    w.done(O0, U0)
    r = sv.r[...]
    scale = group_scale(r)
    gate = sv.gp[...]
    sig = sigmoid(gate)
    dgp = (du * (r * scale) * (sig * (1.0 + gate * (1.0 - sig)))).astype(BF)
    dn = du * (gate * sig)
    one, two = head_sums(dn * r)
    dr = (scale * dn - r * (scale * scale * scale) * by_head(one / DV, two / DV)).astype(BF)
    in_head = head_masks(WIN)
    tabs = (cos[...], sin_a[...], sin_b[...])
    dvs, dqs, dks = [], [[], []], [[], []]
    for bt in range(2):
        rows = slice(bt * WIN, (bt + 1) * WIN)
        part = dr[rows]
        both = jnp.concatenate([jnp.where(in_head[0], part, 0), jnp.where(in_head[1], part, 0)], axis=0)
        p = sv.p[bt]
        stacked = jnp.concatenate([p[:, :WIN], p[:, WIN:]], axis=0)
        dvs.append(dot_tn(stacked, both).astype(BF))
        dp = dot_nt(both, sv.v[rows, :])
        for h in range(HEADS):
            at = slice(h * DK, (h + 1) * DK)
            ds = (decay[bt, h] * dp[h * WIN : (h + 1) * WIN]).astype(BF)
            dqs[h].append(dot(ds, sv.k[rows, at]))
            dks[h].append(dot_tn(ds, sv.q[rows, at]))
    dv = jnp.concatenate(dvs, axis=0)
    dq = jnp.concatenate([rotated_back(jnp.concatenate(dqs[h], axis=0), *tabs).astype(BF) for h in range(HEADS)], axis=1)
    dk = jnp.concatenate(
        [rotated_back(jnp.concatenate(dks[h], axis=0) * DK ** (-0.5), *tabs).astype(BF) for h in range(HEADS)], axis=1
    )
    a = sv.a[...]
    da = w.turned(dq, Q0, 512) + w.turned(dk, K0, 512)
    da = da + w.turned(dv, V0, VP) + w.turned(dgp, S0, VP)
    w.put(Q0, 512, dot_tn(a, dq))
    w.put(K0, 512, dot_tn(a, dk))
    w.put(S0, VP, dot_tn(a, dgp))
    w.done(S0, O0)
    w.done(Q0, V0)
    hat, inv = norm_parts(sv.x[...])
    dgain_one = jnp.sum(da * hat, axis=0, keepdims=True)
    dbias_one = jnp.sum(da, axis=0, keepdims=True)
    norms = jnp.concatenate([dgain_one, dgain_two, dbias_one, dbias_two, jnp.zeros((4, D), F32)], axis=0).astype(BF)
    spread = (iota((8, VP), 1) == iota((8, VP), 0) + 864).astype(BF)
    w.put(V0, VP, dot_tn(a, dv) + dot_tn(norms, spread))
    w.done(V0, S0)
    return dm + norm_back(da, hat, inv, gb[0:1, :])


def layers_kernel(*refs):
    pieces = refs[:8]
    x_in, g_in, next_in, decay, cos, sin_a, sin_b, live, order, third = refs[8:18]
    out, lent = refs[18:20]
    outs = (refs[20:22], refs[22:24])
    gb, sems, out_sems = refs[24:27]
    held = ((refs[27], refs[28]), (refs[29], refs[30]))
    n = len(Saved.NAMES)
    saved = [Saved(refs[31 : 31 + n]), Saved(refs[31 + n : 31 + 2 * n])]
    groups = []
    count = 0
    for layer, start, end in ((0, 0, O0), (0, O0, WIDTH), (1, 0, WIDTH)):
        group = []
        for core in range(2):
            for row in range(4):
                color, unit = COLOR_OF[(layer, row)]
                for half in range(2):
                    piece = pieces[core * 4 + (1 + color if half else 0)]
                    at = unit * WIDTH + (0 if half else sum(WIDE[:color]))
                    rows = slice(row * 64 + half * 32, row * 64 + half * 32 + 32)
                    copy = pltpu.make_async_copy(
                        piece.at[:, at + start : at + end], held[layer][core].at[rows, start:end], sems.at[count]
                    )
                    copy.start()
                    group.append(copy)
                    count += 1
        groups.append(group)
    for b in range(2):
        rows = slice(b * WIN, b * WIN + BLOCK)
        later = slice(b * WIN + BLOCK, (b + 1) * WIN)
        saved[0].x[rows, :] = dot(x_in[b], order[...])
        saved[0].x[later, :] = dot(next_in[0, b], order[...])
    tabs = (decay, cos, sin_a, sin_b)
    weights = (
        Weights(*held[0], None, outs[0], out_sems.at[0]),
        Weights(*held[1], third, outs[1], out_sems.at[1]),
    )
    pick = ((iota((8, 128), 1) == iota((8, 128), 0) + NORM_LANE) & (iota((8, 128), 0) < 4)).astype(BF)
    for copy in groups[0]:
        copy.wait()
    gb[0] = weights[0].turned(pick, V0 + 768, 128)
    saved[1].x[...] = forward(weights[0], gb.at[0], saved[0], *tabs, groups[1])
    for copy in groups[2]:
        copy.wait()
    for core in range(2):
        at = slice(192, 256)
        held[1][core][at, :] = dot(third[core], held[1][core][at, :]).astype(BF)
    gb[1] = weights[1].turned(pick, V0 + 768, 128)
    last = forward(weights[1], gb.at[1], saved[1], *tabs, []).astype(BF)
    last = dot_nt(last, order[...]).astype(BF)
    gs = []
    for b in range(2):
        gs.append(dot(g_in[b], order[...]))
        gs.append(dot(next_in[1, b], order[...]))
    g = jnp.concatenate(gs, axis=0) * live[:, 0:1]
    g = backward(weights[1], gb.at[1], saved[1], *tabs, g)
    g = backward(weights[0], gb.at[0], saved[0], *tabs, g)
    g = dot_nt(g.astype(BF), order[...]).astype(BF)
    for k, result in enumerate((last, g)):
        for b in range(2):
            out[k, b] = result[b * WIN : b * WIN + BLOCK]
            lent[k, b] = result[b * WIN + BLOCK : (b + 1) * WIN]
    for one in weights:
        for copy in one.leaving:
            copy.wait()


def layers(pieces, x_in, g_in, next_in, tabs):
    grads = jax.ShapeDtypeStruct((256, WIDTH), BF)
    rows = jax.ShapeDtypeStruct((2, 2, BLOCK, D), BF)
    any_space = pl.BlockSpec(memory_space=pl.ANY)
    vmem = pl.BlockSpec(memory_space=pltpu.VMEM)
    return pl.pallas_call(
        layers_kernel,
        in_specs=[any_space] * 8 + [vmem] * 10,
        out_specs=[vmem] * 2 + [any_space] * 4,
        out_shape=[rows, rows, grads, grads, grads, grads],
        scratch_shapes=[pltpu.VMEM((2, 8, D), F32), pltpu.SemaphoreType.DMA((48,)), pltpu.SemaphoreType.DMA((2, 12))]
        + [pltpu.VMEM((256, WIDTH), BF)] * 4
        + [pltpu.VMEM(shape, dtype) for _ in range(2) for shape, dtype in Saved.shapes()],
        compiler_params=pltpu.CompilerParams(vmem_limit_bytes=LAYERS_VMEM),
    )(*pieces, x_in, g_in, next_in, *tabs)


def pair_sum(layer, own, got, before, passed):
    order = [(c, k, row) for c in range(3) for k, (at, row) in enumerate(UNITS[c]) if at == layer]
    extra = len(before)

    def kernel(own, got, passed, *refs):
        befores, outs, (mine, theirs, sems) = refs[:extra], refs[extra : extra + 7], refs[extra + 7 :]
        copies = []
        for n, (_, _, row) in enumerate(order):
            at = slice(row * 64, (row + 1) * 64)
            pair = [
                pltpu.make_async_copy(src.at[at, :], dst.at[n], sems.at[n, k])
                for k, (src, dst) in enumerate(((own, mine), (got, theirs)))
            ]
            for copy in pair:
                copy.start()
            copies.append(pair)
        outs[6][...] = passed[...]
        if befores:
            for c in range(3):
                for k, (at, _) in enumerate(UNITS[c]):
                    if at != layer:
                        cols = slice(k * WIDTH, (k + 1) * WIDTH)
                        for half in range(2):
                            outs[2 * c + half][:, cols] = befores[2 * c + half][:, cols]
        for n, (c, k, _) in enumerate(order):
            for copy in copies[n]:
                copy.wait()
            total = (mine[n].astype(F32) + theirs[n].astype(F32)).astype(BF)
            outs[2 * c][:, k * WIDTH : (k + 1) * WIDTH] = total[:32]
            outs[2 * c + 1][:, k * WIDTH : (k + 1) * WIDTH] = total[32:]

    vmem, anywhere = pl.BlockSpec(memory_space=pltpu.VMEM), pl.BlockSpec(memory_space=pl.ANY)
    return pl.pallas_call(
        kernel,
        in_specs=[anywhere] * 2 + [vmem] * (1 + extra),
        out_shape=[jax.ShapeDtypeStruct((32, w), BF) for w in WIDE for _ in range(2)]
        + [jax.ShapeDtypeStruct(passed.shape, BF)],
        scratch_shapes=[pltpu.VMEM((4, 64, WIDTH), BF), pltpu.VMEM((4, 64, WIDTH), BF), pltpu.SemaphoreType.DMA((4, 2))],
        compiler_params=pltpu.CompilerParams(vmem_limit_bytes=PAIR_VMEM),
    )(own, got, passed, *before)


def halve_kernel(*refs):
    for c in range(3):
        total = (refs[c][...].astype(F32) + refs[3 + c][...].astype(F32)).astype(BF)
        half = total.shape[0] // 2
        refs[-6 + 2 * c][...] = total[:half]
        refs[-5 + 2 * c][...] = total[half:]


def halve(keep, got, after):
    vmem, anywhere = pl.BlockSpec(memory_space=pltpu.VMEM), pl.BlockSpec(memory_space=pl.ANY)
    halves = pl.pallas_call(
        halve_kernel,
        in_specs=[vmem] * 6 + [anywhere] * len(after),
        out_shape=[jax.ShapeDtypeStruct((k.shape[0] // 2, *k.shape[1:]), BF) for k in keep for _ in range(2)],
        compiler_params=pltpu.CompilerParams(vmem_limit_bytes=24 << 20),
    )(*keep, *got, *after)
    return halves[0::2], halves[1::2]


def lines_kernel(*refs):
    swap = swap_rows()
    for c in range(3):
        keep, got, keep_out, send_out = refs[c], refs[3 + c], refs[6 + 2 * c], refs[7 + 2 * c]
        lines = keep.shape[1] // 128
        for i in range(0, keep_out.shape[1], 16):
            parts = []
            for k in range(16):
                if i + k < lines:
                    at = slice((i + k) * 128, (i + k + 1) * 128)
                    parts.append((keep[:, at].astype(F32) + got[:, at].astype(F32)).astype(BF))
                else:
                    parts.append(jnp.zeros((16, 128), BF))
            turned = dot(swap, jnp.concatenate(parts, axis=0)).astype(BF).reshape(16, 16, 128)
            keep_out[:, i : i + 16, :] = turned[:8]
            send_out[:, i : i + 16, :] = turned[8:]


def to_lines(keep, got):
    halves = pl.pallas_call(
        lines_kernel,
        out_shape=[jax.ShapeDtypeStruct((8, n, 128), BF) for n in FLAT for _ in range(2)],
        compiler_params=pltpu.CompilerParams(vmem_limit_bytes=24 << 20),
    )(*keep, *got)
    return halves[0::2], halves[1::2]


def cube_kernel(*refs):
    for c, start in enumerate((0, FLAT[0], FLAT[0] + FLAT[1])):
        for k in range(8):
            total = refs[c][k].astype(F32) + refs[3 + c][k].astype(F32)
            refs[6 + k][start : start + FLAT[c]] = total.astype(BF)


def to_cube(keep, got):
    return pl.pallas_call(
        cube_kernel,
        out_shape=[jax.ShapeDtypeStruct((LINES_ALL, 128), BF) for _ in range(8)],
        compiler_params=pltpu.CompilerParams(vmem_limit_bytes=16 << 20),
    )(*keep, *got)


def scatter_sum(own0, oth0, own1, oth1, lent, finish):
    got1, got0 = swap_cores(oth1), swap_cores(oth0)
    *before, lent = pair_sum(1, own1, got1, (), lent)
    *halves, lent = pair_sum(0, own0, got0, before, lent)
    finals = finish(from_behind(lent, 1))
    keep, send = halves[0::2], halves[1::2]
    keep, send = halve(keep, permute_all(send, 2), finals)
    keep, send = to_lines(keep, permute_all(send, 1))
    mine, *rest = to_cube(keep, permute_all(send, 0))
    return finals, [mine] + [lax.ppermute(rest[bits - 1], "fsdp", low_pairs(bits)) for bits in range(1, 8)]


def unpack_kernel(*refs):
    q, k, v, s, o, u, g, d, gain, bias, row = refs[8:]
    row[...] = jnp.zeros_like(row)
    total = refs[0][...].astype(F32)
    for part in refs[1:8]:
        total = total + part[...].astype(F32)
    for units, start in zip(UNITS, (0, FLAT[0], FLAT[0] + FLAT[1])):
        for n, (layer, r) in enumerate(units):
            for j in range(LINES):
                at = start + n * LINES + j
                row[layer, r : r + 1, j * 128 : (j + 1) * 128] = total[at : at + 1]
    for layer in range(2):
        for out, at, width in (
            (q, Q0, 512), (k, K0, 512), (v, V0, 864), (s, S0, 864), (o, O0, 864), (u, U0, 864), (g, G0, 864), (d, D0, 864),
        ):
            out[layer] = row[layer, 0:4, at : at + width]
        norms = jnp.transpose(row[layer, :, V0 + 768 : V0 + VP])
        for kind in range(2):
            gain[layer, kind : kind + 1, :] = norms[NORM_LANE + kind : NORM_LANE + kind + 1, 0:4]
            bias[layer, kind : kind + 1, :] = norms[NORM_LANE + 2 + kind : NORM_LANE + 3 + kind, 0:4]


def unpack(parts):
    shapes = [(2, 4, 512)] * 2 + [(2, 4, 864)] * 6 + [(2, 2, 4)] * 2
    return pl.pallas_call(
        unpack_kernel,
        out_shape=[jax.ShapeDtypeStruct(shape, F32) for shape in shapes],
        scratch_shapes=[pltpu.VMEM((2, 8, WIDTH), F32)],
        compiler_params=pltpu.CompilerParams(vmem_limit_bytes=8 << 20),
    )(*parts)


def from_behind(value, by):
    pairs = [(i, i + by) for i in range(128) if 0 <= i + by < 128]
    return lax.ppermute(value, "fsdp", pairs)


def local(inputs, cotangent, lengths, *weights):
    me = lax.axis_index("fsdp").astype(jnp.int32)
    q, k, v, s, o, u, g, d, gain, bias = weights
    o, d = jnp.swapaxes(o, 1, 2), jnp.swapaxes(d, 1, 2)
    flat, both = pack((q, k, v, s, o, u, g, d, gain, bias), inputs, cotangent)
    pieces, next_in = gather(flat, both)
    decay, cos, sin_a, sin_b, live, flags, order, third = tables(me[None], lengths)
    out, lent, own0, oth0, own1, oth1 = layers(
        pieces, inputs, cotangent, next_in, (decay, cos, sin_a, sin_b, live, order, third)
    )

    def finish(borrowed):
        mine = flags[:, :, 0:1] > 0
        return [jnp.where(mine, out[k], borrowed[k]) for k in range(2)]

    (result, grad), parts = scatter_sum(own0, oth0, own1, oth1, lent, finish)
    q, k, v, s, o, u, g, d, gain, bias = unpack(parts)
    return result, grad, q, k, v, s, jnp.swapaxes(o, 1, 2), u, g, jnp.swapaxes(d, 1, 2), gain, bias


def solution(mesh):
    rows, wide = P(None, "fsdp", None), P(None, None, "fsdp")
    weights = (rows, rows, rows, rows, wide, rows, rows, wide, wide, wide)
    return jax.shard_map(
        local,
        mesh=mesh,
        in_specs=(rows, rows, P(), *weights),
        out_specs=(rows, rows, *weights),
        check_vma=False,
    )
```

```python
import functools

import jax
import jax.numpy as jnp
import numpy as np
from jax import lax
from jax.experimental import pallas as pl
from jax.experimental.pallas import tpu as pltpu
from jax.sharding import PartitionSpec as P

HEADS = 2
DK = 256
DV = 432
D = 512
ROWS = 256
WIN = 128
BLOCK = 64
TOKENS = 8192
NSEQ = 192
NORM_EPSILON = 1e-05
GROUP_EPSILON = 1.0
BF = jnp.bfloat16
F32 = jnp.float32

Q0, K0, V0, S0, O0, U0, G0, D0, WIDTH = 0, 512, 1024, 1920, 2816, 3712, 4608, 5504, 6400
VP = 896
NORM_LANE = 96
LINES = WIDTH // 128
LAYERS_VMEM = 44 << 20
PAIR_VMEM = 24 << 20

UNITS = (((0, 0), (1, 0), (0, 3)), ((0, 1), (1, 1), (1, 3)), ((0, 2), (1, 2)))
FLAT = (160, 160, 112)
LINES_ALL = sum(FLAT)
WIDE = tuple(len(u) * WIDTH for u in UNITS)
COLOR_OF = {unit: (c, k) for c, units in enumerate(UNITS) for k, unit in enumerate(units)}
STRIDE = {"x": 32, "z": 8, "y": 2}
LOW_AXES = "xzy"
HIGH_AXES = ("yzx", "xyz", "zxy")


def mask_of(core, second):
    return 3 if (core == 0) == bool(second) else 1


def low_pairs(bits):
    flip = [(STRIDE[LOW_AXES[k]], bits >> k & 1) for k in range(3)]
    return [(i, i ^ sum(mask_of(i & 1, 0) * stride * bit for stride, bit in flip)) for i in range(128)]


def high_pairs(color, step):
    stride = STRIDE[HIGH_AXES[color][step]]
    return [(i, i ^ (mask_of(i & 1, 1) * stride)) for i in range(128)]


CORE_PAIRS = [(i, i ^ 1) for i in range(128)]


def dot(a, b):
    return lax.dot_general(a, b, (((1,), (0,)), ((), ())), preferred_element_type=F32)


def dot_nt(a, b):
    return lax.dot_general(a, b, (((1,), (1,)), ((), ())), preferred_element_type=F32)


def dot_tn(a, b):
    return lax.dot_general(a, b, (((0,), (0,)), ((), ())), preferred_element_type=F32)


def iota(shape, dim):
    return lax.broadcasted_iota(jnp.int32, shape, dim)


def source_feature(pos, me, third_color):
    core = (me & 1) ^ (pos >> 8)
    row = (pos >> 6) & 3
    color = jnp.where(row == 3, third_color, row)
    device = (me & ~1) | core
    first = jnp.where(core == 0, mask_of(0, 0), mask_of(1, 0))
    second = jnp.where(core == 0, mask_of(0, 1), mask_of(1, 1))
    for k in range(3):
        device = device ^ (((pos >> k) & 1) * first * STRIDE[LOW_AXES[k]])
        strides = [STRIDE[HIGH_AXES[c][k]] for c in range(3)]
        stride = jnp.where(color == 0, strides[0], jnp.where(color == 1, strides[1], strides[2]))
        device = device ^ (((pos >> (3 + k)) & 1) * second * stride)
    return device * 4 + row


def swap_rows():
    r, c = iota((256, 256), 0), iota((256, 256), 1)
    return (((r & 15) * 16 + (r >> 4)) == c).astype(BF)


def pack_kernel(*refs):
    given, (flat, both, row, sems), held = refs[:12], refs[12:16], refs[16:]
    copies = [pltpu.make_async_copy(src, dst, sems.at[k]) for k, (src, dst) in enumerate(zip(given, held))]
    for copy in copies:
        copy.start()
    q, k, v, s, o, u, g, d, gain, bias, x, cot = held
    row[...] = jnp.zeros_like(row)
    for copy in copies:
        copy.wait()
    both[0] = x[...]
    both[1] = cot[...]
    for layer in range(2):
        for weight, at, width in (
            (q, Q0, 512), (k, K0, 512), (v, V0, 864), (s, S0, 864), (o, O0, 864), (u, U0, 864), (g, G0, 864), (d, D0, 864),
        ):
            row[layer, 0:4, at : at + width] = weight[layer].astype(F32)
        norms = jnp.concatenate(
            [part[layer, kind : kind + 1].astype(F32) for part in (gain, bias) for kind in range(2)], axis=0
        ).astype(BF)
        spread = (iota((4, 128), 1) == iota((4, 128), 0) + NORM_LANE).astype(BF)
        row[layer, 0:4, V0 + 768 : V0 + 896] = row[layer, 0:4, V0 + 768 : V0 + 896] + dot_tn(norms, spread)
    for units, lines, start in zip(UNITS, FLAT, (0, FLAT[0], FLAT[0] + FLAT[1])):
        pieces = []
        for layer, r in units:
            for j in range(LINES):
                pieces.append(row[layer, r : r + 1, j * 128 : (j + 1) * 128])
        pad = lines - len(pieces)
        flat[start : start + lines] = jnp.concatenate(pieces + [jnp.zeros((pad, 128), F32)], axis=0).astype(BF)


def in_hbm(values):
    return [pltpu.with_memory_space_constraint(v, pltpu.HBM) for v in values]


def pack(weights, inputs, cotangent):
    values = (*weights, inputs, cotangent)
    return pl.pallas_call(
        pack_kernel,
        in_specs=[pl.BlockSpec(memory_space=pltpu.HBM)] * len(values),
        out_shape=[jax.ShapeDtypeStruct((LINES_ALL, 128), BF), jax.ShapeDtypeStruct((2, 2, BLOCK, D), BF)],
        scratch_shapes=[pltpu.VMEM((2, 8, WIDTH), F32), pltpu.SemaphoreType.DMA((len(values),))]
        + [pltpu.VMEM(v.shape, v.dtype) for v in values],
        compiler_params=pltpu.CompilerParams(vmem_limit_bytes=8 << 20),
    )(*in_hbm(values))


def stack_kernel(*refs):
    for k in range(8):
        start = 0
        for out, lines in zip(refs[8:], FLAT):
            out[k] = refs[k][start : start + lines]
            start += lines


def stack(parts):
    return pl.pallas_call(
        stack_kernel,
        out_shape=[jax.ShapeDtypeStruct((8, n, 128), BF) for n in FLAT],
        compiler_params=pltpu.CompilerParams(vmem_limit_bytes=16 << 20),
    )(*parts)


def rows_kernel(a, b, c, a_got, b_got, c_got, both, a_out, b_out, c_out, both_out):
    both_out[...] = both[...]
    swap = swap_rows()
    for src, got, out, wide in zip((a, b, c), (a_got, b_got, c_got), (a_out, b_out, c_out), WIDE):
        lines = wide // 128
        for i in range(0, lines, 16):
            at = slice(i, i + 16)
            block = jnp.concatenate([src[:, at, :].reshape(128, 128), got[:, at, :].reshape(128, 128)], axis=0)
            turned = dot(swap, block).astype(BF)
            for k in range(min(16, lines - i)):
                out[:, (i + k) * 128 : (i + k + 1) * 128] = turned[k * 16 : (k + 1) * 16]


def to_rows(mine, got, both):
    return pl.pallas_call(
        rows_kernel,
        out_shape=[jax.ShapeDtypeStruct((16, w), BF) for w in WIDE] + [jax.ShapeDtypeStruct(both.shape, BF)],
        compiler_params=pltpu.CompilerParams(vmem_limit_bytes=16 << 20),
    )(*mine, *got, both)


def stack_all_kernel(a, b, c, a_got, b_got, c_got, behind, a_out, b_out, c_out):
    del behind
    for mine, got, out in ((a, a_got, a_out), (b, b_got, b_out), (c, c_got, c_out)):
        out[0:16] = mine[...]
        out[16:32] = got[...]


def stack_all(mine, got, behind):
    vmem, anywhere = pl.BlockSpec(memory_space=pltpu.VMEM), pl.BlockSpec(memory_space=pl.ANY)
    return pl.pallas_call(
        stack_all_kernel,
        in_specs=[vmem] * 6 + [anywhere],
        out_shape=[jax.ShapeDtypeStruct((32, w), BF) for w in WIDE],
        compiler_params=pltpu.CompilerParams(vmem_limit_bytes=24 << 20),
    )(*mine, *got, behind)


def permute_all(values, step):
    return [lax.ppermute(values[c], "fsdp", high_pairs(c, step)) for c in range(3)]


def swap_cores(value):
    return lax.ppermute(value, "fsdp", CORE_PAIRS)


def gather(flat, both):
    cur = stack([flat] + [lax.ppermute(flat, "fsdp", low_pairs(bits)) for bits in range(1, 8)])
    *first, both = to_rows(cur, permute_all(cur, 0), both)
    next_in = from_behind(both, -1)
    halves = stack_all(first, permute_all(first, 1), next_in)
    rest = permute_all(halves, 2)
    return [*halves, *rest, *in_hbm([swap_cores(h) for h in halves]), *[swap_cores(r) for r in rest]], both, next_in


def tables_kernel(me_ref, lengths, trig, here, decay, cos, sin_a, sin_b, live, flags, order, third, here_out):
    here_out[...] = here[...]
    me = me_ref[0]
    first_row = me * BLOCK
    tri = (iota((NSEQ, NSEQ), 0) > iota((NSEQ, NSEQ), 1)).astype(BF)
    lens = lengths[...].astype(F32).astype(BF)
    lens8 = jnp.concatenate([lens, jnp.zeros((6, NSEQ), BF)], axis=0)
    starts_col = dot_nt(tri, lens8)
    starts_row = dot_nt(lens8, tri)
    for b in range(2):
        rows_c = (iota((WIN, NSEQ), 0) + first_row).astype(F32)
        st_r = starts_row[b : b + 1, :]
        anchor_c = jnp.max(jnp.where(st_r <= rows_c, st_r, 0.0), axis=1, keepdims=True)
        rows_r = (iota((NSEQ, WIN), 1) + first_row).astype(F32)
        st_c = starts_col[:, b : b + 1]
        anchor_r = jnp.max(jnp.where(st_c <= rows_r, st_c, 0.0), axis=0, keepdims=True)
        low = first_row.astype(F32)
        row_c = (iota((WIN, 1), 0) + first_row).astype(F32)
        row_r = (iota((1, WIN), 1) + first_row).astype(F32)
        own_c = (anchor_c >= low) & (anchor_c < low + BLOCK) & (row_c < TOKENS)
        own_r = (anchor_r >= low) & (anchor_r < low + BLOCK) & (row_r < TOKENS)
        distance = row_c - row_r
        allowed = (anchor_c == anchor_r) & own_c & own_r & (distance >= 0)
        clamped = jnp.maximum(distance, 0.0)
        for h in range(HEADS):
            rate = float(np.log(np.float32(1.0 - 2.0 ** (-5.0 - h))))
            decay[b, h] = jnp.where(allowed, jnp.exp(rate * clamped), 0.0)
        live[b * WIN : (b + 1) * WIN, :] = jnp.broadcast_to(own_c.astype(F32), (WIN, 128))
        flags[b] = jnp.broadcast_to((anchor_c[:BLOCK] >= low).astype(F32), (BLOCK, 128))
        position = jnp.minimum(row_c - anchor_c, float(WIN - 1))
        hot = (position == iota((WIN, WIN), 1).astype(F32)).astype(F32)
        values = lax.dot_general(
            hot, trig[...], (((1,), (0,)), ((), ())), preferred_element_type=F32, precision=lax.Precision.HIGHEST
        )
        sin = values[:, DK:]
        even = (iota((WIN, DK), 1) & 1) == 0
        cos[b * WIN : (b + 1) * WIN, :] = values[:, :DK]
        sin_a[b * WIN : (b + 1) * WIN, :] = jnp.where(even, -sin, 0.0)
        sin_b[b * WIN : (b + 1) * WIN, :] = jnp.where(even, 0.0, sin)
    pos = iota((1, D), 1)
    order[...] = (iota((D, D), 0) == source_feature(pos, me, 0)).astype(BF)
    for core in range(2):
        base = core * 256 + 192
        want = source_feature(base + iota((64, 1), 0), me, 0)
        have = source_feature(base + iota((1, 64), 1), me, 1)
        third[core] = (want == have).astype(BF)


def trig_table():
    frequency = 1.0 / 10000.0 ** np.linspace(0.0, 1.0, DK // 2, dtype=np.float32)
    frequency = np.repeat(frequency.astype(np.float32), 2)
    phases = np.arange(WIN, dtype=np.float32)[:, None] * frequency
    phases = phases.astype(np.float32).astype(np.float64)
    return np.concatenate([np.cos(phases), np.sin(phases)], axis=1).astype(np.float32)


def tables(me, lengths, here):
    return pl.pallas_call(
        tables_kernel,
        in_specs=[
            pl.BlockSpec(memory_space=pltpu.SMEM),
            pl.BlockSpec(memory_space=pltpu.VMEM),
            pl.BlockSpec(memory_space=pltpu.VMEM),
            pl.BlockSpec(memory_space=pltpu.VMEM),
        ],
        out_shape=[
            jax.ShapeDtypeStruct((2, HEADS, WIN, WIN), F32),
            jax.ShapeDtypeStruct((ROWS, DK), F32),
            jax.ShapeDtypeStruct((ROWS, DK), F32),
            jax.ShapeDtypeStruct((ROWS, DK), F32),
            jax.ShapeDtypeStruct((ROWS, 128), F32),
            jax.ShapeDtypeStruct((2, BLOCK, 128), F32),
            jax.ShapeDtypeStruct((D, D), BF),
            jax.ShapeDtypeStruct((2, 64, 64), BF),
            jax.ShapeDtypeStruct(here.shape, BF),
        ],
        compiler_params=pltpu.CompilerParams(vmem_limit_bytes=16 << 20),
    )(me, lengths, jnp.asarray(trig_table()), here)


def norm_parts(values):
    center = values - jnp.mean(values, axis=-1, keepdims=True)
    inv = lax.rsqrt(jnp.mean(center * center, axis=-1, keepdims=True) + NORM_EPSILON)
    return center * inv, inv


def norm_back(grad, hat, inv, gain):
    scaled = grad * gain
    mean_one = jnp.mean(scaled, axis=-1, keepdims=True)
    mean_two = jnp.mean(scaled * hat, axis=-1, keepdims=True)
    return inv * (scaled - mean_one - hat * mean_two)


def rotated(v, cos, sin_a, sin_b):
    return v * cos + pltpu.roll(v, DK - 1, 1) * sin_a + pltpu.roll(v, 1, 1) * sin_b


def rotated_back(v, cos, sin_a, sin_b):
    return v * cos - pltpu.roll(v, DK - 1, 1) * sin_a - pltpu.roll(v, 1, 1) * sin_b


def sigmoid(v):
    return 0.5 * jnp.tanh(0.5 * v) + 0.5


GELU_C = float(np.sqrt(2.0 / np.pi))


def gelu_tanh(v):
    return jnp.tanh(GELU_C * (v + 0.044715 * (v * v * v)))


class Saved:
    NAMES = ("x", "a", "q", "k", "v", "p", "r", "gp", "u", "m", "b", "up", "gt", "h")

    @staticmethod
    def shapes():
        wide, narrow = (ROWS, VP), (ROWS, D)
        return [
            (narrow, F32), (narrow, BF), (narrow, BF), (narrow, BF), (wide, BF), ((2, WIN, 2 * WIN), BF), (wide, F32),
            (wide, F32), (wide, BF), (narrow, F32), (narrow, BF), (wide, F32), (wide, F32), (wide, BF),
        ]

    def __init__(self, refs):
        for name, ref in zip(self.NAMES, refs):
            setattr(self, name, ref)


def head_masks(rows):
    lane = iota((rows, VP), 1)
    return lane < DV, (lane >= DV) & (lane < 2 * DV)


def forward(w, gb, sv, decay, cos, sin_a, sin_b, later):
    x = sv.x[...]
    hat, _ = norm_parts(x)
    sv.a[...] = (hat * gb[0:1, :] + gb[2:3, :]).astype(BF)
    a = sv.a[...]
    tabs = (cos[...], sin_a[...], sin_b[...])
    for h in range(HEADS):
        at = slice(h * DK, (h + 1) * DK)
        sv.q[:, at] = rotated(w.times(a, Q0 + h * DK, DK), *tabs).astype(BF)
        key = rotated(w.times(a, K0 + h * DK, DK), *tabs) * DK ** (-0.5)
        sv.k[:, at] = key.astype(BF)
    sv.v[...] = w.times(a, V0, VP).astype(BF)
    in_head = head_masks(WIN)
    for b in range(2):
        rows = slice(b * WIN, (b + 1) * WIN)
        for h in range(HEADS):
            at = slice(h * DK, (h + 1) * DK)
            scores = dot_nt(sv.q[rows, at], sv.k[rows, at])
            sv.p[b, :, h * WIN : (h + 1) * WIN] = (decay[b, h] * scores).astype(BF)
        v = sv.v[rows, :]
        both = jnp.concatenate([jnp.where(in_head[0], v, 0), jnp.where(in_head[1], v, 0)], axis=0)
        sv.r[rows, :] = dot(sv.p[b], both)
    for copy in later:
        copy.wait()
    one, two = group_scales(sv.r[...])
    for at, end in CHUNKS:
        gate = w.times(a, S0 + at, end - at)
        sv.gp[:, at:end] = gate
        scale = by_head(one, two, at, end)
        sv.u[:, at:end] = (sv.r[:, at:end] * scale * (gate * sigmoid(gate))).astype(BF)
    sv.m[...] = x + w.turned(sv.u[...], O0, VP)
    hat, _ = norm_parts(sv.m[...])
    sv.b[...] = (hat * gb[1:2, :] + gb[3:4, :]).astype(BF)
    b = sv.b[...]
    for at, end in CHUNKS:
        up = w.times(b, U0 + at, end - at)
        gate = w.times(b, G0 + at, end - at)
        sv.up[:, at:end] = up
        sv.gt[:, at:end] = gate
        sv.h[:, at:end] = (0.5 * up * (1.0 + gelu_tanh(up)) * gate).astype(BF)
    return sv.m[...] + w.turned(sv.h[...], D0, VP)


def head_sums(values):
    first, second = head_masks(ROWS)
    return (
        jnp.sum(jnp.where(first, values, 0.0), axis=-1, keepdims=True),
        jnp.sum(jnp.where(second, values, 0.0), axis=-1, keepdims=True),
    )


def by_head(one, two, at=0, end=VP):
    return jnp.where(iota((ROWS, end - at), 1) + at < DV, one, two)


def group_scales(r):
    one, two = head_sums(r * r)
    return lax.rsqrt(one / DV + GROUP_EPSILON), lax.rsqrt(two / DV + GROUP_EPSILON)


CHUNKS = ((0, 256), (256, 512), (512, 768), (768, 896))


class Weights:
    def __init__(self, own, oth, third, outs, sems):
        self.own, self.oth, self.third, self.outs, self.sems = own, oth, third, outs, sems
        self.leaving = []

    def done(self, start, end):
        for ref, out in zip((self.own, self.oth), self.outs):
            copy = pltpu.make_async_copy(
                ref.at[:, start:end], out.at[:, start:end], self.sems.at[len(self.leaving)]
            )
            copy.start()
            self.leaving.append(copy)

    def times(self, a, at, width):
        one = dot(a[:, :256], self.own[:, at : at + width])
        return one + dot(a[:, 256:], self.oth[:, at : at + width])

    def turned(self, a, at, width):
        return jnp.concatenate([dot_nt(a, self.own[:, at : at + width]), dot_nt(a, self.oth[:, at : at + width])], axis=1)

    def put(self, at, width, grad):
        low = grad.astype(BF)
        for core, out in ((0, self.own), (1, self.oth)):
            part = low[core * 256 : (core + 1) * 256]
            if self.third is None:
                out[:, at : at + width] = part
            else:
                out[0:192, at : at + width] = part[0:192]
                out[192:256, at : at + width] = dot_tn(self.third[core], part[192:256]).astype(BF)


def backward(w, gb, sv, decay, cos, sin_a, sin_b, g, spare):
    f = g.astype(BF)
    dup, dgt = spare.at[0], spare.at[1]
    for at, end in CHUNKS:
        dh = w.times(f, D0 + at, end - at)
        up = sv.up[:, at:end]
        t = gelu_tanh(up)
        half = 0.5 * (1.0 + t)
        dgt[:, at:end] = (dh * (up * half)).astype(BF)
        slope = half + 0.5 * up * (1.0 - t * t) * (GELU_C * (1.0 + 3 * 0.044715 * (up * up)))
        dup[:, at:end] = (dh * sv.gt[:, at:end] * slope).astype(BF)
    db = w.turned(dup[...], U0, VP) + w.turned(dgt[...], G0, VP)
    w.put(D0, VP, dot_tn(f, sv.h[...]))
    b = sv.b[...]
    w.put(U0, VP, dot_tn(b, dup[...]))
    w.put(G0, VP, dot_tn(b, dgt[...]))
    hat, inv = norm_parts(sv.m[...])
    dgain_two = jnp.sum(db * hat, axis=0, keepdims=True)
    dbias_two = jnp.sum(db, axis=0, keepdims=True)
    dm = g + norm_back(db, hat, inv, gb[1:2, :])
    e = dm.astype(BF)
    scales = group_scales(sv.r[...])
    sums = [0.0, 0.0]
    dgp, dr, dn = spare.at[0], spare.at[1], sv.up
    for at, end in CHUNKS:
        du = w.times(e, O0 + at, end - at)
        r = sv.r[:, at:end]
        gate = sv.gp[:, at:end]
        sig = sigmoid(gate)
        dgp[:, at:end] = (du * (r * by_head(*scales, at, end)) * (sig * (1.0 + gate * (1.0 - sig)))).astype(BF)
        part = du * (gate * sig)
        dn[:, at:end] = part
        lane = iota((ROWS, end - at), 1) + at
        product = part * r
        sums[0] = sums[0] + jnp.sum(jnp.where(lane < DV, product, 0.0), axis=-1, keepdims=True)
        sums[1] = sums[1] + jnp.sum(jnp.where((lane >= DV) & (lane < 2 * DV), product, 0.0), axis=-1, keepdims=True)
    w.put(O0, VP, dot_tn(e, sv.u[...]))
    cubes = [scale * scale * scale * (total / DV) for scale, total in zip(scales, sums)]
    for at, end in CHUNKS:
        part = by_head(*scales, at, end) * dn[:, at:end] - sv.r[:, at:end] * by_head(*cubes, at, end)
        dr[:, at:end] = part.astype(BF)
    a = sv.a[...]
    da = w.turned(dgp[...], S0, VP)
    w.put(S0, VP, dot_tn(a, dgp[...]))
    w.done(S0, WIDTH)
    in_head = head_masks(WIN)
    tabs = (cos[...], sin_a[...], sin_b[...])
    dvs, dqs, dks = [], [[], []], [[], []]
    for bt in range(2):
        rows = slice(bt * WIN, (bt + 1) * WIN)
        part = dr[rows, :]
        both = jnp.concatenate([jnp.where(in_head[0], part, 0), jnp.where(in_head[1], part, 0)], axis=0)
        p = sv.p[bt]
        stacked = jnp.concatenate([p[:, :WIN], p[:, WIN:]], axis=0)
        dvs.append(dot_tn(stacked, both).astype(BF))
        dp = dot_nt(both, sv.v[rows, :])
        for h in range(HEADS):
            at = slice(h * DK, (h + 1) * DK)
            ds = (decay[bt, h] * dp[h * WIN : (h + 1) * WIN]).astype(BF)
            dqs[h].append(dot(ds, sv.k[rows, at]))
            dks[h].append(dot_tn(ds, sv.q[rows, at]))
    dv = jnp.concatenate(dvs, axis=0)
    dq = jnp.concatenate([rotated_back(jnp.concatenate(dqs[h], axis=0), *tabs).astype(BF) for h in range(HEADS)], axis=1)
    dk = jnp.concatenate(
        [rotated_back(jnp.concatenate(dks[h], axis=0) * DK ** (-0.5), *tabs).astype(BF) for h in range(HEADS)], axis=1
    )
    da = da + w.turned(dv, V0, VP) + w.turned(dq, Q0, 512) + w.turned(dk, K0, 512)
    w.put(Q0, 512, dot_tn(a, dq))
    w.put(K0, 512, dot_tn(a, dk))
    hat, inv = norm_parts(sv.x[...])
    dgain_one = jnp.sum(da * hat, axis=0, keepdims=True)
    dbias_one = jnp.sum(da, axis=0, keepdims=True)
    norms = jnp.concatenate([dgain_one, dgain_two, dbias_one, dbias_two, jnp.zeros((4, D), F32)], axis=0).astype(BF)
    spread = (iota((8, VP), 1) == iota((8, VP), 0) + 864).astype(BF)
    w.put(V0, VP, dot_tn(a, dv) + dot_tn(norms, spread))
    w.done(Q0, S0)
    return dm + norm_back(da, hat, inv, gb[0:1, :])


def window_rows(here, behind, k):
    return jnp.concatenate([here[k, 0], behind[k, 0], here[k, 1], behind[k, 1]], axis=0)


def layers_kernel(*refs):
    pieces, refs = refs[:12], refs[4:]
    here, behind, decay, cos, sin_a, sin_b, live, order, third = refs[8:17]
    out, lent = refs[17:19]
    outs = (refs[19:21], refs[21:23])
    gb, sems, out_sems, spare = refs[23:27]
    held = (refs[27:29], refs[29:31])
    n = len(Saved.NAMES)
    saved = [Saved(refs[31 : 31 + n]), Saved(refs[31 + n :])]
    groups = []
    count = 0
    for layer, start, end in ((0, 0, S0), (0, S0, WIDTH), (1, 0, WIDTH)):
        group = []
        for core in range(2):
            for row in range(4):
                color, unit = COLOR_OF[(layer, row)]
                for half in range(2):
                    piece = pieces[core * 6 + half * 3 + color]
                    at = unit * WIDTH
                    rows = slice(row * 64 + half * 32, row * 64 + half * 32 + 32)
                    copy = pltpu.make_async_copy(
                        piece.at[:, at + start : at + end], held[layer][core].at[rows, start:end], sems.at[count]
                    )
                    group.append(copy)
                    count += 1
        groups.append(group)
    for copy in groups[0] + groups[1]:
        copy.start()
    saved[0].x[...] = dot(window_rows(here, behind, 0), order[...])
    tabs = (decay, cos, sin_a, sin_b)
    weights = (
        Weights(*held[0], None, outs[0], out_sems.at[0]),
        Weights(*held[1], third, outs[1], out_sems.at[1]),
    )
    pick = ((iota((8, 128), 1) == iota((8, 128), 0) + NORM_LANE) & (iota((8, 128), 0) < 4)).astype(BF)
    for copy in groups[0]:
        copy.wait()
    for copy in groups[2]:
        copy.start()
    gb[0] = weights[0].turned(pick, V0 + 768, 128)
    saved[1].x[...] = forward(weights[0], gb.at[0], saved[0], *tabs, groups[1])
    for copy in groups[2]:
        copy.wait()
    for core in range(2):
        at = slice(192, 256)
        held[1][core][at, :] = dot(third[core], held[1][core][at, :]).astype(BF)
    gb[1] = weights[1].turned(pick, V0 + 768, 128)
    last = forward(weights[1], gb.at[1], saved[1], *tabs, []).astype(BF)
    last = dot_nt(last, order[...]).astype(BF)
    g = dot(window_rows(here, behind, 1), order[...]) * live[:, 0:1]
    g = backward(weights[1], gb.at[1], saved[1], *tabs, g, spare)
    g = backward(weights[0], gb.at[0], saved[0], *tabs, g, spare)
    g = dot_nt(g.astype(BF), order[...]).astype(BF)
    for k, result in enumerate((last, g)):
        for b in range(2):
            out[k, b] = result[b * WIN : b * WIN + BLOCK]
            lent[k, b] = result[b * WIN + BLOCK : (b + 1) * WIN]
    for one in weights:
        for copy in one.leaving:
            copy.wait()


def layers(pieces, here, behind, tabs):
    grads = jax.ShapeDtypeStruct((256, WIDTH), BF)
    rows = jax.ShapeDtypeStruct((2, 2, BLOCK, D), BF)
    any_space = pl.BlockSpec(memory_space=pl.ANY)
    vmem = pl.BlockSpec(memory_space=pltpu.VMEM)
    return pl.pallas_call(
        layers_kernel,
        in_specs=[any_space] * 6 + [pl.BlockSpec(memory_space=pltpu.HBM)] * 3 + [any_space] * 3 + [vmem] * 9,
        out_specs=[vmem] * 2 + [any_space] * 4,
        out_shape=[rows, rows, grads, grads, grads, grads],
        scratch_shapes=[pltpu.VMEM((2, 8, D), F32), pltpu.SemaphoreType.DMA((48,)), pltpu.SemaphoreType.DMA((2, 12))]
        + [pltpu.VMEM((2, ROWS, VP), BF)]
        + [pltpu.VMEM((256, WIDTH), BF)] * 4
        + [pltpu.VMEM(shape, dtype) for _ in range(2) for shape, dtype in Saved.shapes()],
        compiler_params=pltpu.CompilerParams(vmem_limit_bytes=LAYERS_VMEM),
    )(*pieces, here, behind, *tabs)


def pair_sum(layer, own, got, before, passed):
    order = [(c, k, row) for c in range(3) for k, (at, row) in enumerate(UNITS[c]) if at == layer]
    extra = len(before)

    def kernel(own, got, passed, *refs):
        befores, outs, (mine, theirs, sems) = refs[:extra], refs[extra : extra + 7], refs[extra + 7 :]
        copies = []
        for n, (_, _, row) in enumerate(order):
            at = slice(row * 64, (row + 1) * 64)
            pair = [
                pltpu.make_async_copy(src.at[at, :], dst.at[n], sems.at[n, k])
                for k, (src, dst) in enumerate(((own, mine), (got, theirs)))
            ]
            for copy in pair:
                copy.start()
            copies.append(pair)
        outs[6][...] = passed[...]
        if befores:
            for c in range(3):
                for k, (at, _) in enumerate(UNITS[c]):
                    if at != layer:
                        cols = slice(k * WIDTH, (k + 1) * WIDTH)
                        for half in range(2):
                            outs[2 * c + half][:, cols] = befores[2 * c + half][:, cols]
        for n, (c, k, _) in enumerate(order):
            for copy in copies[n]:
                copy.wait()
            total = (mine[n].astype(F32) + theirs[n].astype(F32)).astype(BF)
            outs[2 * c][:, k * WIDTH : (k + 1) * WIDTH] = total[:32]
            outs[2 * c + 1][:, k * WIDTH : (k + 1) * WIDTH] = total[32:]

    vmem, anywhere = pl.BlockSpec(memory_space=pltpu.VMEM), pl.BlockSpec(memory_space=pl.ANY)
    return pl.pallas_call(
        kernel,
        in_specs=[anywhere] * 2 + [vmem] * (1 + extra),
        out_shape=[jax.ShapeDtypeStruct((32, w), BF) for w in WIDE for _ in range(2)]
        + [jax.ShapeDtypeStruct(passed.shape, BF)],
        scratch_shapes=[pltpu.VMEM((4, 64, WIDTH), BF), pltpu.VMEM((4, 64, WIDTH), BF), pltpu.SemaphoreType.DMA((4, 2))],
        compiler_params=pltpu.CompilerParams(vmem_limit_bytes=PAIR_VMEM),
    )(own, got, passed, *before)


def halve_kernel(*refs):
    for c in range(3):
        total = (refs[c][...].astype(F32) + refs[3 + c][...].astype(F32)).astype(BF)
        half = total.shape[0] // 2
        refs[-6 + 2 * c][...] = total[:half]
        refs[-5 + 2 * c][...] = total[half:]


def halve(keep, got, after):
    vmem, anywhere = pl.BlockSpec(memory_space=pltpu.VMEM), pl.BlockSpec(memory_space=pl.ANY)
    halves = pl.pallas_call(
        halve_kernel,
        in_specs=[vmem] * 6 + [anywhere] * len(after),
        out_shape=[jax.ShapeDtypeStruct((k.shape[0] // 2, *k.shape[1:]), BF) for k in keep for _ in range(2)],
        compiler_params=pltpu.CompilerParams(vmem_limit_bytes=24 << 20),
    )(*keep, *got, *after)
    return halves[0::2], halves[1::2]


def lines_kernel(*refs):
    swap = swap_rows()
    for c in range(3):
        keep, got, keep_out, send_out = refs[c], refs[3 + c], refs[6 + 2 * c], refs[7 + 2 * c]
        lines = keep.shape[1] // 128
        for i in range(0, keep_out.shape[1], 16):
            parts = []
            for k in range(16):
                if i + k < lines:
                    at = slice((i + k) * 128, (i + k + 1) * 128)
                    parts.append((keep[:, at].astype(F32) + got[:, at].astype(F32)).astype(BF))
                else:
                    parts.append(jnp.zeros((16, 128), BF))
            turned = dot(swap, jnp.concatenate(parts, axis=0)).astype(BF).reshape(16, 16, 128)
            keep_out[:, i : i + 16, :] = turned[:8]
            send_out[:, i : i + 16, :] = turned[8:]


def to_lines(keep, got):
    halves = pl.pallas_call(
        lines_kernel,
        out_shape=[jax.ShapeDtypeStruct((8, n, 128), BF) for n in FLAT for _ in range(2)],
        compiler_params=pltpu.CompilerParams(vmem_limit_bytes=24 << 20),
    )(*keep, *got)
    return halves[0::2], halves[1::2]


def cube_kernel(*refs):
    for c, start in enumerate((0, FLAT[0], FLAT[0] + FLAT[1])):
        for k in range(8):
            total = refs[c][k].astype(F32) + refs[3 + c][k].astype(F32)
            refs[6 + k][start : start + FLAT[c]] = total.astype(BF)


def to_cube(keep, got):
    return pl.pallas_call(
        cube_kernel,
        out_shape=[jax.ShapeDtypeStruct((LINES_ALL, 128), BF) for _ in range(8)],
        compiler_params=pltpu.CompilerParams(vmem_limit_bytes=16 << 20),
    )(*keep, *got)


def scatter_sum(own0, oth0, own1, oth1, lent, finish):
    got1, got0 = swap_cores(oth1), swap_cores(oth0)
    *before, lent = pair_sum(1, own1, got1, (), lent)
    *halves, lent = pair_sum(0, own0, got0, before, lent)
    finals = finish(from_behind(lent, 1))
    keep, send = halves[0::2], halves[1::2]
    keep, send = halve(keep, permute_all(send, 2), finals)
    keep, send = to_lines(keep, permute_all(send, 1))
    mine, *rest = to_cube(keep, permute_all(send, 0))
    return finals, [mine] + [lax.ppermute(rest[bits - 1], "fsdp", low_pairs(bits)) for bits in range(1, 8)]


def unpack_kernel(*refs):
    q, k, v, s, o, u, g, d, gain, bias, row = refs[8:]
    row[...] = jnp.zeros_like(row)
    total = refs[0][...].astype(F32)
    for part in refs[1:8]:
        total = total + part[...].astype(F32)
    for units, start in zip(UNITS, (0, FLAT[0], FLAT[0] + FLAT[1])):
        for n, (layer, r) in enumerate(units):
            for j in range(LINES):
                at = start + n * LINES + j
                row[layer, r : r + 1, j * 128 : (j + 1) * 128] = total[at : at + 1]
    for layer in range(2):
        for out, at, width in (
            (q, Q0, 512), (k, K0, 512), (v, V0, 864), (s, S0, 864), (o, O0, 864), (u, U0, 864), (g, G0, 864), (d, D0, 864),
        ):
            out[layer] = row[layer, 0:4, at : at + width]
        norms = jnp.transpose(row[layer, :, V0 + 768 : V0 + VP])
        for kind in range(2):
            gain[layer, kind : kind + 1, :] = norms[NORM_LANE + kind : NORM_LANE + kind + 1, 0:4]
            bias[layer, kind : kind + 1, :] = norms[NORM_LANE + 2 + kind : NORM_LANE + 3 + kind, 0:4]


def unpack(parts):
    shapes = [(2, 4, 512)] * 2 + [(2, 4, 864)] * 6 + [(2, 2, 4)] * 2
    return pl.pallas_call(
        unpack_kernel,
        out_shape=[jax.ShapeDtypeStruct(shape, F32) for shape in shapes],
        scratch_shapes=[pltpu.VMEM((2, 8, WIDTH), F32)],
        compiler_params=pltpu.CompilerParams(vmem_limit_bytes=8 << 20),
    )(*parts)


def from_behind(value, by):
    pairs = [(i, i + by) for i in range(128) if 0 <= i + by < 128]
    return lax.ppermute(value, "fsdp", pairs)


def local(inputs, cotangent, lengths, *weights):
    me = lax.axis_index("fsdp").astype(jnp.int32)
    q, k, v, s, o, u, g, d, gain, bias = weights
    o, d = jnp.swapaxes(o, 1, 2), jnp.swapaxes(d, 1, 2)
    flat, both = pack((q, k, v, s, o, u, g, d, gain, bias), inputs, cotangent)
    pieces, here, behind = gather(flat, both)
    decay, cos, sin_a, sin_b, live, flags, order, third, here = tables(me[None], lengths, here)
    out, lent, own0, oth0, own1, oth1 = layers(
        pieces, here, behind, (decay, cos, sin_a, sin_b, live, order, third)
    )

    def finish(borrowed):
        mine = flags[:, :, 0:1] > 0
        return [jnp.where(mine, out[k], borrowed[k]) for k in range(2)]

    (result, grad), parts = scatter_sum(own0, oth0, own1, oth1, lent, finish)
    q, k, v, s, o, u, g, d, gain, bias = unpack(parts)
    return result, grad, q, k, v, s, jnp.swapaxes(o, 1, 2), u, g, jnp.swapaxes(d, 1, 2), gain, bias


def solution(mesh):
    rows, wide = P(None, "fsdp", None), P(None, None, "fsdp")
    weights = (rows, rows, rows, rows, wide, rows, rows, wide, wide, wide)
    return jax.shard_map(
        local,
        mesh=mesh,
        in_specs=(rows, rows, P(), *weights),
        out_specs=(rows, rows, *weights),
        check_vma=False,
    )
```

```python
import functools

import jax
import jax.numpy as jnp
import numpy as np
from jax import lax
from jax.experimental import pallas as pl
from jax.experimental.pallas import tpu as pltpu
from jax.sharding import PartitionSpec as P

HEADS = 2
DK = 256
DV = 432
D = 512
ROWS = 256
WIN = 128
BLOCK = 64
TOKENS = 8192
NSEQ = 192
NORM_EPSILON = 1e-05
GROUP_EPSILON = 1.0
BF = jnp.bfloat16
F32 = jnp.float32

Q0, K0, V0, S0, O0, U0, G0, D0, WIDTH = 0, 512, 1024, 1920, 2816, 3712, 4608, 5504, 6400
VP = 896
NORM_LANE = 96
LINES = WIDTH // 128
FIRST_VMEM = 19 << 20
SECOND_VMEM = 14 << 20
PAIR_VMEM = 24 << 20

UNITS = (((0, 0), (1, 0), (0, 3)), ((0, 1), (1, 1), (1, 3)), ((0, 2), (1, 2)))
FLAT = (160, 160, 112)
LINES_ALL = sum(FLAT)
WIDE = tuple(len(u) * WIDTH for u in UNITS)
COLOR_OF = {unit: (c, k) for c, units in enumerate(UNITS) for k, unit in enumerate(units)}
STRIDE = {"x": 32, "z": 8, "y": 2}
LOW_AXES = "xzy"
HIGH_AXES = ("yzx", "xyz", "zxy")


def mask_of(core, second):
    return 3 if (core == 0) == bool(second) else 1


def low_pairs(bits):
    flip = [(STRIDE[LOW_AXES[k]], bits >> k & 1) for k in range(3)]
    return [(i, i ^ sum(mask_of(i & 1, 0) * stride * bit for stride, bit in flip)) for i in range(128)]


def high_pairs(color, step):
    stride = STRIDE[HIGH_AXES[color][step]]
    return [(i, i ^ (mask_of(i & 1, 1) * stride)) for i in range(128)]


CORE_PAIRS = [(i, i ^ 1) for i in range(128)]


def dot(a, b):
    return lax.dot_general(a, b, (((1,), (0,)), ((), ())), preferred_element_type=F32)


def dot_nt(a, b):
    return lax.dot_general(a, b, (((1,), (1,)), ((), ())), preferred_element_type=F32)


def dot_tn(a, b):
    return lax.dot_general(a, b, (((0,), (0,)), ((), ())), preferred_element_type=F32)


def iota(shape, dim):
    return lax.broadcasted_iota(jnp.int32, shape, dim)


def source_feature(pos, me, third_color):
    core = (me & 1) ^ (pos >> 8)
    row = (pos >> 6) & 3
    color = jnp.where(row == 3, third_color, row)
    device = (me & ~1) | core
    first = jnp.where(core == 0, mask_of(0, 0), mask_of(1, 0))
    second = jnp.where(core == 0, mask_of(0, 1), mask_of(1, 1))
    for k in range(3):
        device = device ^ (((pos >> k) & 1) * first * STRIDE[LOW_AXES[k]])
        strides = [STRIDE[HIGH_AXES[c][k]] for c in range(3)]
        stride = jnp.where(color == 0, strides[0], jnp.where(color == 1, strides[1], strides[2]))
        device = device ^ (((pos >> (3 + k)) & 1) * second * stride)
    return device * 4 + row


def swap_rows():
    r, c = iota((256, 256), 0), iota((256, 256), 1)
    return (((r & 15) * 16 + (r >> 4)) == c).astype(BF)


def pack_kernel(*refs):
    given, (flat, both, row, sems), held = refs[:12], refs[12:16], refs[16:]
    copies = [pltpu.make_async_copy(src, dst, sems.at[k]) for k, (src, dst) in enumerate(zip(given, held))]
    for copy in copies:
        copy.start()
    q, k, v, s, o, u, g, d, gain, bias, x, cot = held
    row[...] = jnp.zeros_like(row)
    for copy in copies:
        copy.wait()
    both[0] = x[...]
    both[1] = cot[...]
    for layer in range(2):
        for weight, at, width in (
            (q, Q0, 512), (k, K0, 512), (v, V0, 864), (s, S0, 864), (o, O0, 864), (u, U0, 864), (g, G0, 864), (d, D0, 864),
        ):
            row[layer, 0:4, at : at + width] = weight[layer].astype(F32)
        norms = jnp.concatenate(
            [part[layer, kind : kind + 1].astype(F32) for part in (gain, bias) for kind in range(2)], axis=0
        ).astype(BF)
        spread = (iota((4, 128), 1) == iota((4, 128), 0) + NORM_LANE).astype(BF)
        row[layer, 0:4, V0 + 768 : V0 + 896] = row[layer, 0:4, V0 + 768 : V0 + 896] + dot_tn(norms, spread)
    for units, lines, start in zip(UNITS, FLAT, (0, FLAT[0], FLAT[0] + FLAT[1])):
        pieces = []
        for layer, r in units:
            for j in range(LINES):
                pieces.append(row[layer, r : r + 1, j * 128 : (j + 1) * 128])
        pad = lines - len(pieces)
        flat[start : start + lines] = jnp.concatenate(pieces + [jnp.zeros((pad, 128), F32)], axis=0).astype(BF)


def in_hbm(values):
    return [pltpu.with_memory_space_constraint(v, pltpu.HBM) for v in values]


def pack(weights, inputs, cotangent):
    values = (*weights, inputs, cotangent)
    return pl.pallas_call(
        pack_kernel,
        in_specs=[pl.BlockSpec(memory_space=pltpu.HBM)] * len(values),
        out_shape=[jax.ShapeDtypeStruct((LINES_ALL, 128), BF), jax.ShapeDtypeStruct((2, 2, BLOCK, D), BF)],
        scratch_shapes=[pltpu.VMEM((2, 8, WIDTH), F32), pltpu.SemaphoreType.DMA((len(values),))]
        + [pltpu.VMEM(v.shape, v.dtype) for v in values],
        compiler_params=pltpu.CompilerParams(vmem_limit_bytes=8 << 20),
    )(*in_hbm(values))


def stack_kernel(*refs):
    for k in range(8):
        start = 0
        for out, lines in zip(refs[8:], FLAT):
            out[k] = refs[k][start : start + lines]
            start += lines


def stack(parts):
    return pl.pallas_call(
        stack_kernel,
        out_shape=[jax.ShapeDtypeStruct((8, n, 128), BF) for n in FLAT],
        compiler_params=pltpu.CompilerParams(vmem_limit_bytes=16 << 20),
    )(*parts)


def rows_kernel(a, b, c, a_got, b_got, c_got, both, a_out, b_out, c_out, both_out):
    both_out[...] = both[...]
    swap = swap_rows()
    for src, got, out, wide in zip((a, b, c), (a_got, b_got, c_got), (a_out, b_out, c_out), WIDE):
        lines = wide // 128
        for i in range(0, lines, 16):
            at = slice(i, i + 16)
            block = jnp.concatenate([src[:, at, :].reshape(128, 128), got[:, at, :].reshape(128, 128)], axis=0)
            turned = dot(swap, block).astype(BF)
            for k in range(min(16, lines - i)):
                out[:, (i + k) * 128 : (i + k + 1) * 128] = turned[k * 16 : (k + 1) * 16]


def to_rows(mine, got, both):
    return pl.pallas_call(
        rows_kernel,
        out_shape=[jax.ShapeDtypeStruct((16, w), BF) for w in WIDE] + [jax.ShapeDtypeStruct(both.shape, BF)],
        compiler_params=pltpu.CompilerParams(vmem_limit_bytes=16 << 20),
    )(*mine, *got, both)


def stack_all_kernel(a, b, c, a_got, b_got, c_got, behind, a_out, b_out, c_out):
    del behind
    for mine, got, out in ((a, a_got, a_out), (b, b_got, b_out), (c, c_got, c_out)):
        out[0:16] = mine[...]
        out[16:32] = got[...]


def stack_all(mine, got, behind):
    vmem, anywhere = pl.BlockSpec(memory_space=pltpu.VMEM), pl.BlockSpec(memory_space=pl.ANY)
    return pl.pallas_call(
        stack_all_kernel,
        in_specs=[vmem] * 6 + [anywhere],
        out_shape=[jax.ShapeDtypeStruct((32, w), BF) for w in WIDE],
        compiler_params=pltpu.CompilerParams(vmem_limit_bytes=24 << 20),
    )(*mine, *got, behind)


def permute_all(values, step):
    return [lax.ppermute(values[c], "fsdp", high_pairs(c, step)) for c in range(3)]


def swap_cores(value):
    return lax.ppermute(value, "fsdp", CORE_PAIRS)


def gather(flat, both):
    cur = stack([flat] + [lax.ppermute(flat, "fsdp", low_pairs(bits)) for bits in range(1, 8)])
    *first, both = to_rows(cur, permute_all(cur, 0), both)
    next_in = from_behind(both, -1)
    halves = stack_all(first, permute_all(first, 1), next_in)
    rest = permute_all(halves, 2)
    return [*halves, *rest, *in_hbm([swap_cores(h) for h in halves]), *[swap_cores(r) for r in rest]], both, next_in


def tables_kernel(me_ref, lengths, trig, here, decay, cos, sin_a, sin_b, live, flags, order, third, here_out):
    here_out[...] = here[...]
    me = me_ref[0]
    first_row = me * BLOCK
    tri = (iota((NSEQ, NSEQ), 0) > iota((NSEQ, NSEQ), 1)).astype(BF)
    lens = lengths[...].astype(F32).astype(BF)
    lens8 = jnp.concatenate([lens, jnp.zeros((6, NSEQ), BF)], axis=0)
    starts_col = dot_nt(tri, lens8)
    starts_row = dot_nt(lens8, tri)
    for b in range(2):
        rows_c = (iota((WIN, NSEQ), 0) + first_row).astype(F32)
        st_r = starts_row[b : b + 1, :]
        anchor_c = jnp.max(jnp.where(st_r <= rows_c, st_r, 0.0), axis=1, keepdims=True)
        rows_r = (iota((NSEQ, WIN), 1) + first_row).astype(F32)
        st_c = starts_col[:, b : b + 1]
        anchor_r = jnp.max(jnp.where(st_c <= rows_r, st_c, 0.0), axis=0, keepdims=True)
        low = first_row.astype(F32)
        row_c = (iota((WIN, 1), 0) + first_row).astype(F32)
        row_r = (iota((1, WIN), 1) + first_row).astype(F32)
        own_c = (anchor_c >= low) & (anchor_c < low + BLOCK) & (row_c < TOKENS)
        own_r = (anchor_r >= low) & (anchor_r < low + BLOCK) & (row_r < TOKENS)
        distance = row_c - row_r
        allowed = (anchor_c == anchor_r) & own_c & own_r & (distance >= 0)
        clamped = jnp.maximum(distance, 0.0)
        for h in range(HEADS):
            rate = float(np.log(np.float32(1.0 - 2.0 ** (-5.0 - h))))
            decay[b, h] = jnp.where(allowed, jnp.exp(rate * clamped), 0.0)
        live[b * WIN : (b + 1) * WIN, :] = jnp.broadcast_to(own_c.astype(F32), (WIN, 128))
        flags[b] = jnp.broadcast_to((anchor_c[:BLOCK] >= low).astype(F32), (BLOCK, 128))
        position = jnp.minimum(row_c - anchor_c, float(WIN - 1))
        hot = (position == iota((WIN, WIN), 1).astype(F32)).astype(F32)
        values = lax.dot_general(
            hot, trig[...], (((1,), (0,)), ((), ())), preferred_element_type=F32, precision=lax.Precision.HIGHEST
        )
        sin = values[:, DK:]
        even = (iota((WIN, DK), 1) & 1) == 0
        cos[b * WIN : (b + 1) * WIN, :] = values[:, :DK]
        sin_a[b * WIN : (b + 1) * WIN, :] = jnp.where(even, -sin, 0.0)
        sin_b[b * WIN : (b + 1) * WIN, :] = jnp.where(even, 0.0, sin)
    pos = iota((1, D), 1)
    order[...] = (iota((D, D), 0) == source_feature(pos, me, 0)).astype(BF)
    for core in range(2):
        base = core * 256 + 192
        want = source_feature(base + iota((64, 1), 0), me, 0)
        have = source_feature(base + iota((1, 64), 1), me, 1)
        third[core] = (want == have).astype(BF)


def trig_table():
    frequency = 1.0 / 10000.0 ** np.linspace(0.0, 1.0, DK // 2, dtype=np.float32)
    frequency = np.repeat(frequency.astype(np.float32), 2)
    phases = np.arange(WIN, dtype=np.float32)[:, None] * frequency
    phases = phases.astype(np.float32).astype(np.float64)
    return np.concatenate([np.cos(phases), np.sin(phases)], axis=1).astype(np.float32)


def tables(me, lengths, here):
    return pl.pallas_call(
        tables_kernel,
        in_specs=[
            pl.BlockSpec(memory_space=pltpu.SMEM),
            pl.BlockSpec(memory_space=pltpu.VMEM),
            pl.BlockSpec(memory_space=pltpu.VMEM),
            pl.BlockSpec(memory_space=pltpu.VMEM),
        ],
        out_shape=[
            jax.ShapeDtypeStruct((2, HEADS, WIN, WIN), F32),
            jax.ShapeDtypeStruct((ROWS, DK), F32),
            jax.ShapeDtypeStruct((ROWS, DK), F32),
            jax.ShapeDtypeStruct((ROWS, DK), F32),
            jax.ShapeDtypeStruct((ROWS, 128), F32),
            jax.ShapeDtypeStruct((2, BLOCK, 128), F32),
            jax.ShapeDtypeStruct((D, D), BF),
            jax.ShapeDtypeStruct((2, 64, 64), BF),
            jax.ShapeDtypeStruct(here.shape, BF),
        ],
        compiler_params=pltpu.CompilerParams(vmem_limit_bytes=16 << 20),
    )(me, lengths, jnp.asarray(trig_table()), here)


def norm_parts(values):
    center = values - jnp.mean(values, axis=-1, keepdims=True)
    inv = lax.rsqrt(jnp.mean(center * center, axis=-1, keepdims=True) + NORM_EPSILON)
    return center * inv, inv


def norm_back(grad, hat, inv, gain):
    scaled = grad * gain
    mean_one = jnp.mean(scaled, axis=-1, keepdims=True)
    mean_two = jnp.mean(scaled * hat, axis=-1, keepdims=True)
    return inv * (scaled - mean_one - hat * mean_two)


def rotated(v, cos, sin_a, sin_b):
    return v * cos + pltpu.roll(v, DK - 1, 1) * sin_a + pltpu.roll(v, 1, 1) * sin_b


def rotated_back(v, cos, sin_a, sin_b):
    return v * cos - pltpu.roll(v, DK - 1, 1) * sin_a - pltpu.roll(v, 1, 1) * sin_b


def sigmoid(v):
    return 0.5 * jnp.tanh(0.5 * v) + 0.5


GELU_C = float(np.sqrt(2.0 / np.pi))


def gelu_tanh(v):
    return jnp.tanh(GELU_C * (v + 0.044715 * (v * v * v)))


class Saved:
    F32_PARTS = (("up", VP), ("gt", VP), ("m", D), ("r", VP), ("gp", VP), ("x", D))
    BF_PARTS = (("h", VP), ("b", D), ("u", VP), ("p", 2 * WIN), ("v", VP), ("k", D), ("q", D), ("a", D))
    WIDTHS = tuple(sum(width for _, width in parts) for parts in (F32_PARTS, BF_PARTS))
    DTYPES = (F32, BF)

    def __init__(self, refs):
        for ref, parts in zip(refs, (self.F32_PARTS, self.BF_PARTS)):
            at = 0
            for name, width in parts:
                setattr(self, name, ref.at[:, at : at + width])
                at += width

    @classmethod
    def shapes(cls):
        return [((ROWS, width), dtype) for width, dtype in zip(cls.WIDTHS, cls.DTYPES)]


def head_masks(rows):
    lane = iota((rows, VP), 1)
    return lane < DV, (lane >= DV) & (lane < 2 * DV)


def forward(w, gb, sv, decay, cos, sin_a, sin_b, later):
    x = sv.x[...]
    hat, _ = norm_parts(x)
    sv.a[...] = (hat * gb[0:1, :] + gb[2:3, :]).astype(BF)
    a = sv.a[...]
    tabs = (cos[...], sin_a[...], sin_b[...])
    for h in range(HEADS):
        at = slice(h * DK, (h + 1) * DK)
        sv.q[:, at] = rotated(w.times(a, Q0 + h * DK, DK), *tabs).astype(BF)
        key = rotated(w.times(a, K0 + h * DK, DK), *tabs) * DK ** (-0.5)
        sv.k[:, at] = key.astype(BF)
    sv.v[...] = w.times(a, V0, VP).astype(BF)
    in_head = head_masks(WIN)
    for b in range(2):
        rows = slice(b * WIN, (b + 1) * WIN)
        for h in range(HEADS):
            at = slice(h * DK, (h + 1) * DK)
            scores = dot_nt(sv.q[rows, at], sv.k[rows, at])
            sv.p[rows, h * WIN : (h + 1) * WIN] = (decay[b, h] * scores).astype(BF)
        v = sv.v[rows, :]
        both = jnp.concatenate([jnp.where(in_head[0], v, 0), jnp.where(in_head[1], v, 0)], axis=0)
        sv.r[rows, :] = dot(sv.p[rows, :], both)
    for copy in later:
        copy.wait()
    one, two = group_scales(sv.r[...])
    for at, end in CHUNKS:
        gate = w.times(a, S0 + at, end - at)
        sv.gp[:, at:end] = gate
        scale = by_head(one, two, at, end)
        sv.u[:, at:end] = (sv.r[:, at:end] * scale * (gate * sigmoid(gate))).astype(BF)
    sv.m[...] = x + w.turned(sv.u[...], O0, VP)
    hat, _ = norm_parts(sv.m[...])
    sv.b[...] = (hat * gb[1:2, :] + gb[3:4, :]).astype(BF)
    b = sv.b[...]
    for at, end in CHUNKS:
        up = w.times(b, U0 + at, end - at)
        gate = w.times(b, G0 + at, end - at)
        sv.up[:, at:end] = up
        sv.gt[:, at:end] = gate
        sv.h[:, at:end] = (0.5 * up * (1.0 + gelu_tanh(up)) * gate).astype(BF)
    return sv.m[...] + w.turned(sv.h[...], D0, VP)


def head_sums(values):
    first, second = head_masks(ROWS)
    return (
        jnp.sum(jnp.where(first, values, 0.0), axis=-1, keepdims=True),
        jnp.sum(jnp.where(second, values, 0.0), axis=-1, keepdims=True),
    )


def by_head(one, two, at=0, end=VP):
    return jnp.where(iota((ROWS, end - at), 1) + at < DV, one, two)


def group_scales(r):
    one, two = head_sums(r * r)
    return lax.rsqrt(one / DV + GROUP_EPSILON), lax.rsqrt(two / DV + GROUP_EPSILON)


CHUNKS = ((0, 256), (256, 512), (512, 768), (768, 896))


class Weights:
    def __init__(self, refs, third, outs=None):
        self.own, self.oth = refs
        self.third, self.outs = third, outs or refs

    def times(self, a, at, width):
        one = dot(a[:, :256], self.own[:, at : at + width])
        return one + dot(a[:, 256:], self.oth[:, at : at + width])

    def turned(self, a, at, width):
        return jnp.concatenate([dot_nt(a, self.own[:, at : at + width]), dot_nt(a, self.oth[:, at : at + width])], axis=1)

    def put(self, at, width, grad):
        low = grad.astype(BF)
        for core, out in enumerate(self.outs):
            part = low[core * 256 : (core + 1) * 256]
            if self.third is None:
                out[:, at : at + width] = part
            else:
                out[0:192, at : at + width] = part[0:192]
                out[192:256, at : at + width] = dot_tn(self.third[core], part[192:256]).astype(BF)


def backward(w, gb, sv, decay, cos, sin_a, sin_b, g, spare, dn):
    f = g.astype(BF)
    dup, dgt = spare.at[0], spare.at[1]
    for at, end in CHUNKS:
        dh = w.times(f, D0 + at, end - at)
        up = sv.up[:, at:end]
        t = gelu_tanh(up)
        half = 0.5 * (1.0 + t)
        dgt[:, at:end] = (dh * (up * half)).astype(BF)
        slope = half + 0.5 * up * (1.0 - t * t) * (GELU_C * (1.0 + 3 * 0.044715 * (up * up)))
        dup[:, at:end] = (dh * sv.gt[:, at:end] * slope).astype(BF)
    db = w.turned(dup[...], U0, VP) + w.turned(dgt[...], G0, VP)
    w.put(D0, VP, dot_tn(f, sv.h[...]))
    b = sv.b[...]
    w.put(U0, VP, dot_tn(b, dup[...]))
    w.put(G0, VP, dot_tn(b, dgt[...]))
    hat, inv = norm_parts(sv.m[...])
    dgain_two = jnp.sum(db * hat, axis=0, keepdims=True)
    dbias_two = jnp.sum(db, axis=0, keepdims=True)
    dm = g + norm_back(db, hat, inv, gb[1:2, :])
    e = dm.astype(BF)
    scales = group_scales(sv.r[...])
    sums = [0.0, 0.0]
    dgp, dr = spare.at[0], spare.at[1]
    for at, end in CHUNKS:
        du = w.times(e, O0 + at, end - at)
        r = sv.r[:, at:end]
        gate = sv.gp[:, at:end]
        sig = sigmoid(gate)
        dgp[:, at:end] = (du * (r * by_head(*scales, at, end)) * (sig * (1.0 + gate * (1.0 - sig)))).astype(BF)
        part = du * (gate * sig)
        dn[:, at:end] = part
        lane = iota((ROWS, end - at), 1) + at
        product = part * r
        sums[0] = sums[0] + jnp.sum(jnp.where(lane < DV, product, 0.0), axis=-1, keepdims=True)
        sums[1] = sums[1] + jnp.sum(jnp.where((lane >= DV) & (lane < 2 * DV), product, 0.0), axis=-1, keepdims=True)
    w.put(O0, VP, dot_tn(e, sv.u[...]))
    cubes = [scale * scale * scale * (total / DV) for scale, total in zip(scales, sums)]
    for at, end in CHUNKS:
        part = by_head(*scales, at, end) * dn[:, at:end] - sv.r[:, at:end] * by_head(*cubes, at, end)
        dr[:, at:end] = part.astype(BF)
    a = sv.a[...]
    da = w.turned(dgp[...], S0, VP)
    w.put(S0, VP, dot_tn(a, dgp[...]))
    in_head = head_masks(WIN)
    tabs = (cos[...], sin_a[...], sin_b[...])
    dvs, dqs, dks = [], [[], []], [[], []]
    for bt in range(2):
        rows = slice(bt * WIN, (bt + 1) * WIN)
        part = dr[rows, :]
        both = jnp.concatenate([jnp.where(in_head[0], part, 0), jnp.where(in_head[1], part, 0)], axis=0)
        p = sv.p[rows, :]
        stacked = jnp.concatenate([p[:, :WIN], p[:, WIN:]], axis=0)
        dvs.append(dot_tn(stacked, both).astype(BF))
        dp = dot_nt(both, sv.v[rows, :])
        for h in range(HEADS):
            at = slice(h * DK, (h + 1) * DK)
            ds = (decay[bt, h] * dp[h * WIN : (h + 1) * WIN]).astype(BF)
            dqs[h].append(dot(ds, sv.k[rows, at]))
            dks[h].append(dot_tn(ds, sv.q[rows, at]))
    dv = jnp.concatenate(dvs, axis=0)
    dq = jnp.concatenate([rotated_back(jnp.concatenate(dqs[h], axis=0), *tabs).astype(BF) for h in range(HEADS)], axis=1)
    dk = jnp.concatenate(
        [rotated_back(jnp.concatenate(dks[h], axis=0) * DK ** (-0.5), *tabs).astype(BF) for h in range(HEADS)], axis=1
    )
    da = da + w.turned(dv, V0, VP) + w.turned(dq, Q0, 512) + w.turned(dk, K0, 512)
    w.put(Q0, 512, dot_tn(a, dq))
    w.put(K0, 512, dot_tn(a, dk))
    hat, inv = norm_parts(sv.x[...])
    dgain_one = jnp.sum(da * hat, axis=0, keepdims=True)
    dbias_one = jnp.sum(da, axis=0, keepdims=True)
    norms = jnp.concatenate([dgain_one, dgain_two, dbias_one, dbias_two, jnp.zeros((4, D), F32)], axis=0).astype(BF)
    spread = (iota((8, VP), 1) == iota((8, VP), 0) + 864).astype(BF)
    w.put(V0, VP, dot_tn(a, dv) + dot_tn(norms, spread))
    return dm + norm_back(da, hat, inv, gb[0:1, :])


def window_rows(here, behind, k):
    return jnp.concatenate([here[k, 0], behind[k, 0], here[k, 1], behind[k, 1]], axis=0)


def put_norms(gb, weights):
    pick = ((iota((8, 128), 1) == iota((8, 128), 0) + NORM_LANE) & (iota((8, 128), 0) < 4)).astype(BF)
    gb[...] = weights.turned(pick, V0 + 768, 128)


def put_rows(result, order, out, lent):
    result = dot_nt(result.astype(BF), order[...]).astype(BF)
    for b in range(2):
        out[b] = result[b * WIN : b * WIN + BLOCK]
        lent[b] = result[b * WIN + BLOCK : (b + 1) * WIN]


def first_kernel(*refs):
    pieces, refs = refs[:12], refs[12:]
    here, behind, decay, cos, sin_a, sin_b, live, order, third = refs[:9]
    out, lent, g_out = refs[9:12]
    held = (refs[12:14], refs[14:16])
    gb, sems, spare, dn = refs[18:22]
    saved = [Saved(refs[16:18]), Saved(refs[22:24])]
    groups = []
    count = 0
    for layer, start, end in ((0, 0, S0), (0, S0, WIDTH), (1, 0, WIDTH)):
        group = []
        for core in range(2):
            for row in range(4):
                color, unit = COLOR_OF[(layer, row)]
                for half in range(2):
                    piece = pieces[core * 6 + half * 3 + color]
                    at = unit * WIDTH
                    rows = slice(row * 64 + half * 32, row * 64 + half * 32 + 32)
                    copy = pltpu.make_async_copy(
                        piece.at[:, at + start : at + end], held[layer][core].at[rows, start:end], sems.at[count]
                    )
                    group.append(copy)
                    count += 1
        groups.append(group)
    for copy in groups[0] + groups[1]:
        copy.start()
    saved[0].x[...] = dot(window_rows(here, behind, 0), order[...])
    tabs = (decay, cos, sin_a, sin_b)
    weights = [Weights(held[0], None), Weights(held[1], third)]
    for copy in groups[0]:
        copy.wait()
    for copy in groups[2]:
        copy.start()
    put_norms(gb.at[0], weights[0])
    saved[1].x[...] = forward(weights[0], gb.at[0], saved[0], *tabs, groups[1])
    for copy in groups[2]:
        copy.wait()
    for core in range(2):
        at = slice(192, 256)
        held[1][core][at, :] = dot(third[core], held[1][core][at, :]).astype(BF)
    put_norms(gb.at[1], weights[1])
    put_rows(forward(weights[1], gb.at[1], saved[1], *tabs, []), order, out, lent)
    g = dot(window_rows(here, behind, 1), order[...]) * live[:, 0:1]
    g_out[...] = backward(weights[1], gb.at[1], saved[1], *tabs, g, spare, dn)


def second_kernel(*refs):
    held, kept = refs[:2], refs[2:4]
    g_in, decay, cos, sin_a, sin_b, order, out_one, lent_one = refs[4:12]
    out, lent = refs[12:14]
    gb, spare, dn = refs[16:19]
    weights = Weights(held, None, refs[14:16])
    put_norms(gb, weights)
    g = backward(weights, gb, Saved(kept), decay, cos, sin_a, sin_b, g_in[...], spare, dn)
    out[0] = out_one[...]
    lent[0] = lent_one[...]
    put_rows(g, order, out.at[1], lent.at[1])


def layers(pieces, here, behind, tabs):
    decay, cos, sin_a, sin_b, live, order, third = tabs
    grads = [jax.ShapeDtypeStruct((256, WIDTH), BF)] * 2
    saved = Saved.shapes()
    spare = [pltpu.VMEM((2, ROWS, VP), BF), pltpu.VMEM((ROWS, VP), F32)]
    any_space, hbm = pl.BlockSpec(memory_space=pl.ANY), pl.BlockSpec(memory_space=pltpu.HBM)
    vmem = pl.BlockSpec(memory_space=pltpu.VMEM)
    out, lent, g, own0, oth0, own1, oth1, *kept = pl.pallas_call(
        first_kernel,
        in_specs=[any_space] * 6 + [hbm] * 3 + [any_space] * 3 + [vmem] * 9,
        out_specs=[vmem] * 9,
        out_shape=[jax.ShapeDtypeStruct((2, BLOCK, D), BF)] * 2
        + [jax.ShapeDtypeStruct((ROWS, D), F32), *grads, *grads]
        + [jax.ShapeDtypeStruct(*one) for one in saved],
        scratch_shapes=[pltpu.VMEM((2, 8, D), F32), pltpu.SemaphoreType.DMA((48,)), *spare]
        + [pltpu.VMEM(*one) for one in saved],
        compiler_params=pltpu.CompilerParams(vmem_limit_bytes=FIRST_VMEM),
    )(*pieces, here, behind, *tabs)
    got1 = swap_cores(oth1)
    rows = jax.ShapeDtypeStruct((2, 2, BLOCK, D), BF)
    out, lent, own0, oth0 = pl.pallas_call(
        second_kernel,
        in_specs=[vmem] * 12,
        out_specs=[vmem] * 4,
        out_shape=[rows, rows, *grads],
        scratch_shapes=[pltpu.VMEM((8, D), F32), *spare],
        input_output_aliases={0: 2, 1: 3},
        compiler_params=pltpu.CompilerParams(vmem_limit_bytes=SECOND_VMEM),
    )(own0, oth0, *kept, g, decay, cos, sin_a, sin_b, order, out, lent)
    return out, lent, own0, swap_cores(oth0), own1, got1


def pair_sum(layer, own, got, before, passed):
    order = [(c, k, row) for c in range(3) for k, (at, row) in enumerate(UNITS[c]) if at == layer]
    extra = len(before)

    def kernel(own, got, passed, *refs):
        befores, outs, (mine, theirs, sems) = refs[:extra], refs[extra : extra + 7], refs[extra + 7 :]
        copies = []
        for n, (_, _, row) in enumerate(order):
            at = slice(row * 64, (row + 1) * 64)
            pair = [
                pltpu.make_async_copy(src.at[at, :], dst.at[n], sems.at[n, k])
                for k, (src, dst) in enumerate(((own, mine), (got, theirs)))
            ]
            for copy in pair:
                copy.start()
            copies.append(pair)
        outs[6][...] = passed[...]
        if befores:
            for c in range(3):
                for k, (at, _) in enumerate(UNITS[c]):
                    if at != layer:
                        cols = slice(k * WIDTH, (k + 1) * WIDTH)
                        for half in range(2):
                            outs[2 * c + half][:, cols] = befores[2 * c + half][:, cols]
        for n, (c, k, _) in enumerate(order):
            for copy in copies[n]:
                copy.wait()
            total = (mine[n].astype(F32) + theirs[n].astype(F32)).astype(BF)
            outs[2 * c][:, k * WIDTH : (k + 1) * WIDTH] = total[:32]
            outs[2 * c + 1][:, k * WIDTH : (k + 1) * WIDTH] = total[32:]

    vmem, anywhere = pl.BlockSpec(memory_space=pltpu.VMEM), pl.BlockSpec(memory_space=pl.ANY)
    return pl.pallas_call(
        kernel,
        in_specs=[anywhere] * 2 + [vmem] * (1 + extra),
        out_shape=[jax.ShapeDtypeStruct((32, w), BF) for w in WIDE for _ in range(2)]
        + [jax.ShapeDtypeStruct(passed.shape, BF)],
        scratch_shapes=[pltpu.VMEM((4, 64, WIDTH), BF), pltpu.VMEM((4, 64, WIDTH), BF), pltpu.SemaphoreType.DMA((4, 2))],
        compiler_params=pltpu.CompilerParams(vmem_limit_bytes=PAIR_VMEM),
    )(own, got, passed, *before)


def halve_kernel(*refs):
    for c in range(3):
        total = (refs[c][...].astype(F32) + refs[3 + c][...].astype(F32)).astype(BF)
        half = total.shape[0] // 2
        refs[-6 + 2 * c][...] = total[:half]
        refs[-5 + 2 * c][...] = total[half:]


def halve(keep, got, after):
    vmem, anywhere = pl.BlockSpec(memory_space=pltpu.VMEM), pl.BlockSpec(memory_space=pl.ANY)
    halves = pl.pallas_call(
        halve_kernel,
        in_specs=[vmem] * 6 + [anywhere] * len(after),
        out_shape=[jax.ShapeDtypeStruct((k.shape[0] // 2, *k.shape[1:]), BF) for k in keep for _ in range(2)],
        compiler_params=pltpu.CompilerParams(vmem_limit_bytes=24 << 20),
    )(*keep, *got, *after)
    return halves[0::2], halves[1::2]


def lines_kernel(*refs):
    swap = swap_rows()
    for c in range(3):
        keep, got, keep_out, send_out = refs[c], refs[3 + c], refs[6 + 2 * c], refs[7 + 2 * c]
        lines = keep.shape[1] // 128
        for i in range(0, keep_out.shape[1], 16):
            parts = []
            for k in range(16):
                if i + k < lines:
                    at = slice((i + k) * 128, (i + k + 1) * 128)
                    parts.append((keep[:, at].astype(F32) + got[:, at].astype(F32)).astype(BF))
                else:
                    parts.append(jnp.zeros((16, 128), BF))
            turned = dot(swap, jnp.concatenate(parts, axis=0)).astype(BF).reshape(16, 16, 128)
            keep_out[:, i : i + 16, :] = turned[:8]
            send_out[:, i : i + 16, :] = turned[8:]


def to_lines(keep, got):
    halves = pl.pallas_call(
        lines_kernel,
        out_shape=[jax.ShapeDtypeStruct((8, n, 128), BF) for n in FLAT for _ in range(2)],
        compiler_params=pltpu.CompilerParams(vmem_limit_bytes=24 << 20),
    )(*keep, *got)
    return halves[0::2], halves[1::2]


def cube_kernel(*refs):
    for c, start in enumerate((0, FLAT[0], FLAT[0] + FLAT[1])):
        for k in range(8):
            total = refs[c][k].astype(F32) + refs[3 + c][k].astype(F32)
            refs[6 + k][start : start + FLAT[c]] = total.astype(BF)


def to_cube(keep, got):
    return pl.pallas_call(
        cube_kernel,
        out_shape=[jax.ShapeDtypeStruct((LINES_ALL, 128), BF) for _ in range(8)],
        compiler_params=pltpu.CompilerParams(vmem_limit_bytes=16 << 20),
    )(*keep, *got)


def scatter_sum(own0, got0, own1, got1, lent, finish):
    *before, lent = pair_sum(1, own1, got1, (), lent)
    *halves, lent = pair_sum(0, own0, got0, before, lent)
    finals = finish(from_behind(lent, 1))
    keep, send = halves[0::2], halves[1::2]
    keep, send = halve(keep, permute_all(send, 2), finals)
    keep, send = to_lines(keep, permute_all(send, 1))
    mine, *rest = to_cube(keep, permute_all(send, 0))
    return finals, [mine] + [lax.ppermute(rest[bits - 1], "fsdp", low_pairs(bits)) for bits in range(1, 8)]


def unpack_kernel(*refs):
    q, k, v, s, o, u, g, d, gain, bias, row = refs[8:]
    row[...] = jnp.zeros_like(row)
    total = refs[0][...].astype(F32)
    for part in refs[1:8]:
        total = total + part[...].astype(F32)
    for units, start in zip(UNITS, (0, FLAT[0], FLAT[0] + FLAT[1])):
        for n, (layer, r) in enumerate(units):
            for j in range(LINES):
                at = start + n * LINES + j
                row[layer, r : r + 1, j * 128 : (j + 1) * 128] = total[at : at + 1]
    for layer in range(2):
        for out, at, width in (
            (q, Q0, 512), (k, K0, 512), (v, V0, 864), (s, S0, 864), (o, O0, 864), (u, U0, 864), (g, G0, 864), (d, D0, 864),
        ):
            out[layer] = row[layer, 0:4, at : at + width]
        norms = jnp.transpose(row[layer, :, V0 + 768 : V0 + VP])
        for kind in range(2):
            gain[layer, kind : kind + 1, :] = norms[NORM_LANE + kind : NORM_LANE + kind + 1, 0:4]
            bias[layer, kind : kind + 1, :] = norms[NORM_LANE + 2 + kind : NORM_LANE + 3 + kind, 0:4]


def unpack(parts):
    shapes = [(2, 4, 512)] * 2 + [(2, 4, 864)] * 6 + [(2, 2, 4)] * 2
    return pl.pallas_call(
        unpack_kernel,
        out_shape=[jax.ShapeDtypeStruct(shape, F32) for shape in shapes],
        scratch_shapes=[pltpu.VMEM((2, 8, WIDTH), F32)],
        compiler_params=pltpu.CompilerParams(vmem_limit_bytes=8 << 20),
    )(*parts)


def from_behind(value, by):
    pairs = [(i, i + by) for i in range(128) if 0 <= i + by < 128]
    return lax.ppermute(value, "fsdp", pairs)


def local(inputs, cotangent, lengths, *weights):
    me = lax.axis_index("fsdp").astype(jnp.int32)
    q, k, v, s, o, u, g, d, gain, bias = weights
    o, d = jnp.swapaxes(o, 1, 2), jnp.swapaxes(d, 1, 2)
    flat, both = pack((q, k, v, s, o, u, g, d, gain, bias), inputs, cotangent)
    pieces, here, behind = gather(flat, both)
    decay, cos, sin_a, sin_b, live, flags, order, third, here = tables(me[None], lengths, here)
    out, lent, own0, got0, own1, got1 = layers(
        pieces, here, behind, (decay, cos, sin_a, sin_b, live, order, third)
    )

    def finish(borrowed):
        mine = flags[:, :, 0:1] > 0
        return [jnp.where(mine, out[k], borrowed[k]) for k in range(2)]

    (result, grad), parts = scatter_sum(own0, got0, own1, got1, lent, finish)
    q, k, v, s, o, u, g, d, gain, bias = unpack(parts)
    return result, grad, q, k, v, s, jnp.swapaxes(o, 1, 2), u, g, jnp.swapaxes(d, 1, 2), gain, bias


def solution(mesh):
    rows, wide = P(None, "fsdp", None), P(None, None, "fsdp")
    weights = (rows, rows, rows, rows, wide, rows, rows, wide, wide, wide)
    return jax.shard_map(
        local,
        mesh=mesh,
        in_specs=(rows, rows, P(), *weights),
        out_specs=(rows, rows, *weights),
        check_vma=False,
    )
```

```python
import functools

import jax
import jax.numpy as jnp
import numpy as np
from jax import lax
from jax.experimental import pallas as pl
from jax.experimental.pallas import tpu as pltpu
from jax.sharding import PartitionSpec as P

HEADS = 2
DK = 256
DV = 432
D = 512
ROWS = 256
WIN = 128
BLOCK = 64
TOKENS = 8192
NSEQ = 192
NORM_EPSILON = 1e-05
GROUP_EPSILON = 1.0
BF = jnp.bfloat16
F32 = jnp.float32

Q0, K0, V0, S0, O0, U0, G0, D0, WIDTH = 0, 512, 1024, 1920, 2816, 3712, 4608, 5504, 6400
VP = 896
NORM_LANE = 96
LINES = WIDTH // 128
FIRST_VMEM = 19 << 20
SECOND_VMEM = 14 << 20
PAIR_VMEM = 20 << 20

UNITS = (((0, 0), (1, 0), (0, 3)), ((0, 1), (1, 1), (1, 3)), ((0, 2), (1, 2)))
FLAT = (160, 160, 112)
LINES_ALL = sum(FLAT)
WIDE = tuple(len(u) * WIDTH for u in UNITS)
COLOR_OF = {unit: (c, k) for c, units in enumerate(UNITS) for k, unit in enumerate(units)}
STRIDE = {"x": 32, "z": 8, "y": 2}
LOW_AXES = "xzy"
HIGH_AXES = ("yzx", "xyz", "zxy")


def mask_of(core, second):
    return 3 if (core == 0) == bool(second) else 1


def low_pairs(bits):
    flip = [(STRIDE[LOW_AXES[k]], bits >> k & 1) for k in range(3)]
    return [(i, i ^ sum(mask_of(i & 1, 0) * stride * bit for stride, bit in flip)) for i in range(128)]


def high_pairs(color, step):
    stride = STRIDE[HIGH_AXES[color][step]]
    return [(i, i ^ (mask_of(i & 1, 1) * stride)) for i in range(128)]


CORE_PAIRS = [(i, i ^ 1) for i in range(128)]


def dot(a, b):
    return lax.dot_general(a, b, (((1,), (0,)), ((), ())), preferred_element_type=F32)


def dot_nt(a, b):
    return lax.dot_general(a, b, (((1,), (1,)), ((), ())), preferred_element_type=F32)


def dot_tn(a, b):
    return lax.dot_general(a, b, (((0,), (0,)), ((), ())), preferred_element_type=F32)


def iota(shape, dim):
    return lax.broadcasted_iota(jnp.int32, shape, dim)


def source_feature(pos, me, third_color):
    core = (me & 1) ^ (pos >> 8)
    row = (pos >> 6) & 3
    color = jnp.where(row == 3, third_color, row)
    device = (me & ~1) | core
    first = jnp.where(core == 0, mask_of(0, 0), mask_of(1, 0))
    second = jnp.where(core == 0, mask_of(0, 1), mask_of(1, 1))
    for k in range(3):
        device = device ^ (((pos >> k) & 1) * first * STRIDE[LOW_AXES[k]])
        strides = [STRIDE[HIGH_AXES[c][k]] for c in range(3)]
        stride = jnp.where(color == 0, strides[0], jnp.where(color == 1, strides[1], strides[2]))
        device = device ^ (((pos >> (3 + k)) & 1) * second * stride)
    return device * 4 + row


def swap_rows():
    r, c = iota((128, 128), 0), iota((128, 128), 1)
    return (((r & 7) * 16 + (r >> 3)) == c).astype(BF)


COLOR_START = (0, FLAT[0], FLAT[0] + FLAT[1])


def pack_kernel(*refs):
    given, (flat, both, row, sems), held = refs[:12], refs[12:16], refs[16:]
    copies = [pltpu.make_async_copy(src, dst, sems.at[k]) for k, (src, dst) in enumerate(zip(given, held))]
    for copy in copies:
        copy.start()
    q, k, v, s, o, u, g, d, gain, bias, x, cot = held
    row[...] = jnp.zeros_like(row)
    for copy in copies:
        copy.wait()
    both[0] = x[...]
    both[1] = cot[...]
    for layer in range(2):
        for weight, at, width in (
            (q, Q0, 512), (k, K0, 512), (v, V0, 864), (s, S0, 864), (o, O0, 864), (u, U0, 864), (g, G0, 864), (d, D0, 864),
        ):
            row[layer, 0:4, at : at + width] = weight[layer].astype(F32)
        norms = jnp.concatenate(
            [part[layer, kind : kind + 1].astype(F32) for part in (gain, bias) for kind in range(2)], axis=0
        ).astype(BF)
        spread = (iota((4, 128), 1) == iota((4, 128), 0) + NORM_LANE).astype(BF)
        row[layer, 0:4, V0 + 768 : V0 + 896] = row[layer, 0:4, V0 + 768 : V0 + 896] + dot_tn(norms, spread)
    for units, lines, start in zip(UNITS, FLAT, (0, FLAT[0], FLAT[0] + FLAT[1])):
        pieces = []
        for layer, r in units:
            for j in range(LINES):
                pieces.append(row[layer, r : r + 1, j * 128 : (j + 1) * 128])
        pad = lines - len(pieces)
        flat[start : start + lines] = jnp.concatenate(pieces + [jnp.zeros((pad, 128), F32)], axis=0).astype(BF)


def in_hbm(values):
    return [pltpu.with_memory_space_constraint(v, pltpu.HBM) for v in values]


def pack(weights, inputs, cotangent):
    values = (*weights, inputs, cotangent)
    return pl.pallas_call(
        pack_kernel,
        in_specs=[pl.BlockSpec(memory_space=pltpu.HBM)] * len(values),
        out_shape=[jax.ShapeDtypeStruct((LINES_ALL, 128), BF), jax.ShapeDtypeStruct((2, 2, BLOCK, D), BF)],
        scratch_shapes=[pltpu.VMEM((2, 8, WIDTH), F32), pltpu.SemaphoreType.DMA((len(values),))]
        + [pltpu.VMEM(v.shape, v.dtype) for v in values],
        compiler_params=pltpu.CompilerParams(vmem_limit_bytes=8 << 20),
    )(*in_hbm(values))


def rows_kernel(*refs):
    parts, both, outs, both_out = refs[:8], refs[8], refs[9:12], refs[12]
    both_out[...] = both[...]
    swap = swap_rows()
    for out, wide, start in zip(outs, WIDE, COLOR_START):
        lines = wide // 128
        for i in range(0, lines, 16):
            block = jnp.concatenate([part[start + i : start + i + 16] for part in parts], axis=0)
            turned = dot(swap, block).astype(BF)
            for k in range(min(16, lines - i)):
                out[:, (i + k) * 128 : (i + k + 1) * 128] = turned[k * 8 : (k + 1) * 8]


def to_rows(parts, both):
    return pl.pallas_call(
        rows_kernel,
        out_shape=[jax.ShapeDtypeStruct((8, w), BF) for w in WIDE] + [jax.ShapeDtypeStruct(both.shape, BF)],
        compiler_params=pltpu.CompilerParams(vmem_limit_bytes=16 << 20),
    )(*parts, both)


def pair_rows_kernel(a, b, c, a_got, b_got, c_got, both, a_out, b_out, c_out, both_out):
    both_out[...] = both[...]
    for mine, got, out in ((a, a_got, a_out), (b, b_got, b_out), (c, c_got, c_out)):
        out[...] = jnp.concatenate([mine[...].astype(F32), got[...].astype(F32)], axis=0).astype(BF)


def pair_rows(mine, got, both):
    return pl.pallas_call(
        pair_rows_kernel,
        out_shape=[jax.ShapeDtypeStruct((16, w), BF) for w in WIDE] + [jax.ShapeDtypeStruct(both.shape, BF)],
        compiler_params=pltpu.CompilerParams(vmem_limit_bytes=16 << 20),
    )(*mine, *got, both)


def stack_all_kernel(a, b, c, a_got, b_got, c_got, behind, a_out, b_out, c_out):
    del behind
    for mine, got, out in ((a, a_got, a_out), (b, b_got, b_out), (c, c_got, c_out)):
        out[0:16] = mine[...]
        out[16:32] = got[...]


def stack_all(mine, got, behind):
    vmem, anywhere = pl.BlockSpec(memory_space=pltpu.VMEM), pl.BlockSpec(memory_space=pl.ANY)
    return pl.pallas_call(
        stack_all_kernel,
        in_specs=[vmem] * 6 + [anywhere],
        out_shape=[jax.ShapeDtypeStruct((32, w), BF) for w in WIDE],
        compiler_params=pltpu.CompilerParams(vmem_limit_bytes=24 << 20),
    )(*mine, *got, behind)


def permute_all(values, step):
    return [lax.ppermute(values[c], "fsdp", high_pairs(c, step)) for c in range(3)]


def swap_cores(value):
    return lax.ppermute(value, "fsdp", CORE_PAIRS)


def gather(flat, both):
    *first, both = to_rows([flat] + [lax.ppermute(flat, "fsdp", low_pairs(bits)) for bits in range(1, 8)], both)
    *first, both = pair_rows(first, permute_all(first, 0), both)
    next_in = from_behind(both, -1)
    halves = stack_all(first, permute_all(first, 1), next_in)
    rest = permute_all(halves, 2)
    return [*halves, *rest, *in_hbm([swap_cores(h) for h in halves]), *[swap_cores(r) for r in rest]], both, next_in


def tables_kernel(me_ref, lengths, trig, here, decay, cos, sin_a, sin_b, live, flags, order, third, here_out):
    here_out[...] = here[...]
    me = me_ref[0]
    first_row = me * BLOCK
    tri = (iota((NSEQ, NSEQ), 0) > iota((NSEQ, NSEQ), 1)).astype(BF)
    lens = lengths[...].astype(F32).astype(BF)
    lens8 = jnp.concatenate([lens, jnp.zeros((6, NSEQ), BF)], axis=0)
    starts_col = dot_nt(tri, lens8)
    starts_row = dot_nt(lens8, tri)
    for b in range(2):
        rows_c = (iota((WIN, NSEQ), 0) + first_row).astype(F32)
        st_r = starts_row[b : b + 1, :]
        anchor_c = jnp.max(jnp.where(st_r <= rows_c, st_r, 0.0), axis=1, keepdims=True)
        rows_r = (iota((NSEQ, WIN), 1) + first_row).astype(F32)
        st_c = starts_col[:, b : b + 1]
        anchor_r = jnp.max(jnp.where(st_c <= rows_r, st_c, 0.0), axis=0, keepdims=True)
        low = first_row.astype(F32)
        row_c = (iota((WIN, 1), 0) + first_row).astype(F32)
        row_r = (iota((1, WIN), 1) + first_row).astype(F32)
        own_c = (anchor_c >= low) & (anchor_c < low + BLOCK) & (row_c < TOKENS)
        own_r = (anchor_r >= low) & (anchor_r < low + BLOCK) & (row_r < TOKENS)
        distance = row_c - row_r
        allowed = (anchor_c == anchor_r) & own_c & own_r & (distance >= 0)
        clamped = jnp.maximum(distance, 0.0)
        for h in range(HEADS):
            rate = float(np.log(np.float32(1.0 - 2.0 ** (-5.0 - h))))
            decay[b, h] = jnp.where(allowed, jnp.exp(rate * clamped), 0.0)
        live[b * WIN : (b + 1) * WIN, :] = jnp.broadcast_to(own_c.astype(F32), (WIN, 128))
        flags[b] = jnp.broadcast_to((anchor_c[:BLOCK] >= low).astype(F32), (BLOCK, 128))
        position = jnp.minimum(row_c - anchor_c, float(WIN - 1))
        hot = (position == iota((WIN, WIN), 1).astype(F32)).astype(F32)
        values = lax.dot_general(
            hot, trig[...], (((1,), (0,)), ((), ())), preferred_element_type=F32, precision=lax.Precision.HIGHEST
        )
        sin = values[:, DK:]
        even = (iota((WIN, DK), 1) & 1) == 0
        cos[b * WIN : (b + 1) * WIN, :] = values[:, :DK]
        sin_a[b * WIN : (b + 1) * WIN, :] = jnp.where(even, -sin, 0.0)
        sin_b[b * WIN : (b + 1) * WIN, :] = jnp.where(even, 0.0, sin)
    pos = iota((1, D), 1)
    order[...] = (iota((D, D), 0) == source_feature(pos, me, 0)).astype(BF)
    for core in range(2):
        base = core * 256 + 192
        want = source_feature(base + iota((64, 1), 0), me, 0)
        have = source_feature(base + iota((1, 64), 1), me, 1)
        third[core] = (want == have).astype(BF)


def trig_table():
    frequency = 1.0 / 10000.0 ** np.linspace(0.0, 1.0, DK // 2, dtype=np.float32)
    frequency = np.repeat(frequency.astype(np.float32), 2)
    phases = np.arange(WIN, dtype=np.float32)[:, None] * frequency
    phases = phases.astype(np.float32).astype(np.float64)
    return np.concatenate([np.cos(phases), np.sin(phases)], axis=1).astype(np.float32)


def tables(me, lengths, here):
    return pl.pallas_call(
        tables_kernel,
        in_specs=[
            pl.BlockSpec(memory_space=pltpu.SMEM),
            pl.BlockSpec(memory_space=pltpu.VMEM),
            pl.BlockSpec(memory_space=pltpu.VMEM),
            pl.BlockSpec(memory_space=pltpu.VMEM),
        ],
        out_shape=[
            jax.ShapeDtypeStruct((2, HEADS, WIN, WIN), F32),
            jax.ShapeDtypeStruct((ROWS, DK), F32),
            jax.ShapeDtypeStruct((ROWS, DK), F32),
            jax.ShapeDtypeStruct((ROWS, DK), F32),
            jax.ShapeDtypeStruct((ROWS, 128), F32),
            jax.ShapeDtypeStruct((2, BLOCK, 128), F32),
            jax.ShapeDtypeStruct((D, D), BF),
            jax.ShapeDtypeStruct((2, 64, 64), BF),
            jax.ShapeDtypeStruct(here.shape, BF),
        ],
        compiler_params=pltpu.CompilerParams(vmem_limit_bytes=16 << 20),
    )(me, lengths, jnp.asarray(trig_table()), here)


def norm_parts(values):
    center = values - jnp.mean(values, axis=-1, keepdims=True)
    inv = lax.rsqrt(jnp.mean(center * center, axis=-1, keepdims=True) + NORM_EPSILON)
    return center * inv, inv


def norm_back(grad, hat, inv, gain):
    scaled = grad * gain
    mean_one = jnp.mean(scaled, axis=-1, keepdims=True)
    mean_two = jnp.mean(scaled * hat, axis=-1, keepdims=True)
    return inv * (scaled - mean_one - hat * mean_two)


def rotated(v, cos, sin_a, sin_b):
    return v * cos + pltpu.roll(v, DK - 1, 1) * sin_a + pltpu.roll(v, 1, 1) * sin_b


def rotated_back(v, cos, sin_a, sin_b):
    return v * cos - pltpu.roll(v, DK - 1, 1) * sin_a - pltpu.roll(v, 1, 1) * sin_b


def sigmoid(v):
    return 0.5 * jnp.tanh(0.5 * v) + 0.5


GELU_C = float(np.sqrt(2.0 / np.pi))


def gelu_tanh(v):
    return jnp.tanh(GELU_C * (v + 0.044715 * (v * v * v)))


class Saved:
    F32_PARTS = (("up", VP), ("gt", VP), ("m", D), ("r", VP), ("gp", VP), ("x", D))
    BF_PARTS = (("h", VP), ("b", D), ("u", VP), ("p", 2 * WIN), ("v", VP), ("k", D), ("q", D), ("a", D))
    WIDTHS = tuple(sum(width for _, width in parts) for parts in (F32_PARTS, BF_PARTS))
    DTYPES = (F32, BF)

    def __init__(self, refs):
        for ref, parts in zip(refs, (self.F32_PARTS, self.BF_PARTS)):
            at = 0
            for name, width in parts:
                setattr(self, name, ref.at[:, at : at + width])
                at += width

    @classmethod
    def shapes(cls):
        return [((ROWS, width), dtype) for width, dtype in zip(cls.WIDTHS, cls.DTYPES)]


def head_masks(rows):
    lane = iota((rows, VP), 1)
    return lane < DV, (lane >= DV) & (lane < 2 * DV)


def forward(w, gb, sv, decay, cos, sin_a, sin_b, later):
    x = sv.x[...]
    hat, _ = norm_parts(x)
    sv.a[...] = (hat * gb[0:1, :] + gb[2:3, :]).astype(BF)
    a = sv.a[...]
    tabs = (cos[...], sin_a[...], sin_b[...])
    for h in range(HEADS):
        at = slice(h * DK, (h + 1) * DK)
        sv.q[:, at] = rotated(w.times(a, Q0 + h * DK, DK), *tabs).astype(BF)
        key = rotated(w.times(a, K0 + h * DK, DK), *tabs) * DK ** (-0.5)
        sv.k[:, at] = key.astype(BF)
    sv.v[...] = w.times(a, V0, VP).astype(BF)
    in_head = head_masks(WIN)
    for b in range(2):
        rows = slice(b * WIN, (b + 1) * WIN)
        for h in range(HEADS):
            at = slice(h * DK, (h + 1) * DK)
            scores = dot_nt(sv.q[rows, at], sv.k[rows, at])
            sv.p[rows, h * WIN : (h + 1) * WIN] = (decay[b, h] * scores).astype(BF)
        v = sv.v[rows, :]
        both = jnp.concatenate([jnp.where(in_head[0], v, 0), jnp.where(in_head[1], v, 0)], axis=0)
        sv.r[rows, :] = dot(sv.p[rows, :], both)
    for copy in later:
        copy.wait()
    one, two = group_scales(sv.r[...])
    for at, end in CHUNKS:
        gate = w.times(a, S0 + at, end - at)
        sv.gp[:, at:end] = gate
        scale = by_head(one, two, at, end)
        sv.u[:, at:end] = (sv.r[:, at:end] * scale * (gate * sigmoid(gate))).astype(BF)
    sv.m[...] = x + w.turned(sv.u[...], O0, VP)
    hat, _ = norm_parts(sv.m[...])
    sv.b[...] = (hat * gb[1:2, :] + gb[3:4, :]).astype(BF)
    b = sv.b[...]
    for at, end in CHUNKS:
        up = w.times(b, U0 + at, end - at)
        gate = w.times(b, G0 + at, end - at)
        sv.up[:, at:end] = up
        sv.gt[:, at:end] = gate
        sv.h[:, at:end] = (0.5 * up * (1.0 + gelu_tanh(up)) * gate).astype(BF)
    return sv.m[...] + w.turned(sv.h[...], D0, VP)


def head_sums(values):
    first, second = head_masks(ROWS)
    return (
        jnp.sum(jnp.where(first, values, 0.0), axis=-1, keepdims=True),
        jnp.sum(jnp.where(second, values, 0.0), axis=-1, keepdims=True),
    )


def by_head(one, two, at=0, end=VP):
    return jnp.where(iota((ROWS, end - at), 1) + at < DV, one, two)


def group_scales(r):
    one, two = head_sums(r * r)
    return lax.rsqrt(one / DV + GROUP_EPSILON), lax.rsqrt(two / DV + GROUP_EPSILON)


CHUNKS = ((0, 256), (256, 512), (512, 768), (768, 896))


class Weights:
    def __init__(self, refs, third, outs=None):
        self.own, self.oth = refs
        self.third, self.outs = third, outs or refs

    def times(self, a, at, width):
        one = dot(a[:, :256], self.own[:, at : at + width])
        return one + dot(a[:, 256:], self.oth[:, at : at + width])

    def turned(self, a, at, width):
        return jnp.concatenate([dot_nt(a, self.own[:, at : at + width]), dot_nt(a, self.oth[:, at : at + width])], axis=1)

    def put(self, at, width, grad):
        low = grad.astype(BF)
        for core, out in enumerate(self.outs):
            part = low[core * 256 : (core + 1) * 256]
            if self.third is None:
                out[:, at : at + width] = part
            else:
                out[0:192, at : at + width] = part[0:192]
                out[192:256, at : at + width] = dot_tn(self.third[core], part[192:256]).astype(BF)


def backward(w, gb, sv, decay, cos, sin_a, sin_b, g, spare, dn):
    f = g.astype(BF)
    dup, dgt = spare.at[0], spare.at[1]
    for at, end in CHUNKS:
        dh = w.times(f, D0 + at, end - at)
        up = sv.up[:, at:end]
        t = gelu_tanh(up)
        half = 0.5 * (1.0 + t)
        dgt[:, at:end] = (dh * (up * half)).astype(BF)
        slope = half + 0.5 * up * (1.0 - t * t) * (GELU_C * (1.0 + 3 * 0.044715 * (up * up)))
        dup[:, at:end] = (dh * sv.gt[:, at:end] * slope).astype(BF)
    db = w.turned(dup[...], U0, VP) + w.turned(dgt[...], G0, VP)
    w.put(D0, VP, dot_tn(f, sv.h[...]))
    b = sv.b[...]
    w.put(U0, VP, dot_tn(b, dup[...]))
    w.put(G0, VP, dot_tn(b, dgt[...]))
    hat, inv = norm_parts(sv.m[...])
    dgain_two = jnp.sum(db * hat, axis=0, keepdims=True)
    dbias_two = jnp.sum(db, axis=0, keepdims=True)
    dm = g + norm_back(db, hat, inv, gb[1:2, :])
    e = dm.astype(BF)
    scales = group_scales(sv.r[...])
    sums = [0.0, 0.0]
    dgp, dr = spare.at[0], spare.at[1]
    for at, end in CHUNKS:
        du = w.times(e, O0 + at, end - at)
        r = sv.r[:, at:end]
        gate = sv.gp[:, at:end]
        sig = sigmoid(gate)
        dgp[:, at:end] = (du * (r * by_head(*scales, at, end)) * (sig * (1.0 + gate * (1.0 - sig)))).astype(BF)
        part = du * (gate * sig)
        dn[:, at:end] = part
        lane = iota((ROWS, end - at), 1) + at
        product = part * r
        sums[0] = sums[0] + jnp.sum(jnp.where(lane < DV, product, 0.0), axis=-1, keepdims=True)
        sums[1] = sums[1] + jnp.sum(jnp.where((lane >= DV) & (lane < 2 * DV), product, 0.0), axis=-1, keepdims=True)
    w.put(O0, VP, dot_tn(e, sv.u[...]))
    cubes = [scale * scale * scale * (total / DV) for scale, total in zip(scales, sums)]
    for at, end in CHUNKS:
        part = by_head(*scales, at, end) * dn[:, at:end] - sv.r[:, at:end] * by_head(*cubes, at, end)
        dr[:, at:end] = part.astype(BF)
    a = sv.a[...]
    da = w.turned(dgp[...], S0, VP)
    w.put(S0, VP, dot_tn(a, dgp[...]))
    in_head = head_masks(WIN)
    tabs = (cos[...], sin_a[...], sin_b[...])
    dvs, dqs, dks = [], [[], []], [[], []]
    for bt in range(2):
        rows = slice(bt * WIN, (bt + 1) * WIN)
        part = dr[rows, :]
        both = jnp.concatenate([jnp.where(in_head[0], part, 0), jnp.where(in_head[1], part, 0)], axis=0)
        p = sv.p[rows, :]
        stacked = jnp.concatenate([p[:, :WIN], p[:, WIN:]], axis=0)
        dvs.append(dot_tn(stacked, both).astype(BF))
        dp = dot_nt(both, sv.v[rows, :])
        for h in range(HEADS):
            at = slice(h * DK, (h + 1) * DK)
            ds = (decay[bt, h] * dp[h * WIN : (h + 1) * WIN]).astype(BF)
            dqs[h].append(dot(ds, sv.k[rows, at]))
            dks[h].append(dot_tn(ds, sv.q[rows, at]))
    dv = jnp.concatenate(dvs, axis=0)
    dq = jnp.concatenate([rotated_back(jnp.concatenate(dqs[h], axis=0), *tabs).astype(BF) for h in range(HEADS)], axis=1)
    dk = jnp.concatenate(
        [rotated_back(jnp.concatenate(dks[h], axis=0) * DK ** (-0.5), *tabs).astype(BF) for h in range(HEADS)], axis=1
    )
    da = da + w.turned(dv, V0, VP) + w.turned(dq, Q0, 512) + w.turned(dk, K0, 512)
    w.put(Q0, 512, dot_tn(a, dq))
    w.put(K0, 512, dot_tn(a, dk))
    hat, inv = norm_parts(sv.x[...])
    dgain_one = jnp.sum(da * hat, axis=0, keepdims=True)
    dbias_one = jnp.sum(da, axis=0, keepdims=True)
    norms = jnp.concatenate([dgain_one, dgain_two, dbias_one, dbias_two, jnp.zeros((4, D), F32)], axis=0).astype(BF)
    spread = (iota((8, VP), 1) == iota((8, VP), 0) + 864).astype(BF)
    w.put(V0, VP, dot_tn(a, dv) + dot_tn(norms, spread))
    return dm + norm_back(da, hat, inv, gb[0:1, :])


def window_rows(here, behind, k):
    return jnp.concatenate([here[k, 0], behind[k, 0], here[k, 1], behind[k, 1]], axis=0)


def put_norms(gb, weights):
    pick = ((iota((8, 128), 1) == iota((8, 128), 0) + NORM_LANE) & (iota((8, 128), 0) < 4)).astype(BF)
    gb[...] = weights.turned(pick, V0 + 768, 128)


def put_rows(result, order, out, lent):
    result = dot_nt(result.astype(BF), order[...]).astype(BF)
    for b in range(2):
        out[b] = result[b * WIN : b * WIN + BLOCK]
        lent[b] = result[b * WIN + BLOCK : (b + 1) * WIN]


def first_kernel(*refs):
    pieces, refs = refs[:12], refs[12:]
    here, behind, decay, cos, sin_a, sin_b, live, order, third = refs[:9]
    out, lent, g_out = refs[9:12]
    held = (refs[12:14], refs[14:16])
    gb, sems, spare, dn = refs[18:22]
    saved = [Saved(refs[16:18]), Saved(refs[22:24])]
    groups = []
    count = 0
    for layer, start, end in ((0, 0, S0), (0, S0, WIDTH), (1, 0, WIDTH)):
        group = []
        for core in range(2):
            for row in range(4):
                color, unit = COLOR_OF[(layer, row)]
                for half in range(2):
                    piece = pieces[core * 6 + half * 3 + color]
                    at = unit * WIDTH
                    rows = slice(row * 64 + half * 32, row * 64 + half * 32 + 32)
                    copy = pltpu.make_async_copy(
                        piece.at[:, at + start : at + end], held[layer][core].at[rows, start:end], sems.at[count]
                    )
                    group.append(copy)
                    count += 1
        groups.append(group)
    for copy in groups[0] + groups[1]:
        copy.start()
    saved[0].x[...] = dot(window_rows(here, behind, 0), order[...])
    tabs = (decay, cos, sin_a, sin_b)
    weights = [Weights(held[0], None), Weights(held[1], third)]
    for copy in groups[0]:
        copy.wait()
    for copy in groups[2]:
        copy.start()
    put_norms(gb.at[0], weights[0])
    saved[1].x[...] = forward(weights[0], gb.at[0], saved[0], *tabs, groups[1])
    for copy in groups[2]:
        copy.wait()
    for core in range(2):
        at = slice(192, 256)
        held[1][core][at, :] = dot(third[core], held[1][core][at, :]).astype(BF)
    put_norms(gb.at[1], weights[1])
    put_rows(forward(weights[1], gb.at[1], saved[1], *tabs, []), order, out, lent)
    g = dot(window_rows(here, behind, 1), order[...]) * live[:, 0:1]
    g_out[...] = backward(weights[1], gb.at[1], saved[1], *tabs, g, spare, dn)


def second_kernel(*refs):
    held, kept = refs[:2], refs[2:4]
    g_in, decay, cos, sin_a, sin_b, order, out_one, lent_one = refs[4:12]
    out, lent = refs[12:14]
    gb, spare, dn = refs[16:19]
    weights = Weights(held, None, refs[14:16])
    put_norms(gb, weights)
    g = backward(weights, gb, Saved(kept), decay, cos, sin_a, sin_b, g_in[...], spare, dn)
    out[0] = out_one[...]
    lent[0] = lent_one[...]
    put_rows(g, order, out.at[1], lent.at[1])


def layers(pieces, here, behind, tabs):
    decay, cos, sin_a, sin_b, live, order, third = tabs
    grads = [jax.ShapeDtypeStruct((256, WIDTH), BF)] * 2
    saved = Saved.shapes()
    spare = [pltpu.VMEM((2, ROWS, VP), BF), pltpu.VMEM((ROWS, VP), F32)]
    any_space, hbm = pl.BlockSpec(memory_space=pl.ANY), pl.BlockSpec(memory_space=pltpu.HBM)
    vmem = pl.BlockSpec(memory_space=pltpu.VMEM)
    out, lent, g, own0, oth0, own1, oth1, *kept = pl.pallas_call(
        first_kernel,
        in_specs=[any_space] * 6 + [hbm] * 3 + [any_space] * 3 + [vmem] * 9,
        out_specs=[vmem] * 9,
        out_shape=[jax.ShapeDtypeStruct((2, BLOCK, D), BF)] * 2
        + [jax.ShapeDtypeStruct((ROWS, D), F32), *grads, *grads]
        + [jax.ShapeDtypeStruct(*one) for one in saved],
        scratch_shapes=[pltpu.VMEM((2, 8, D), F32), pltpu.SemaphoreType.DMA((48,)), *spare]
        + [pltpu.VMEM(*one) for one in saved],
        compiler_params=pltpu.CompilerParams(vmem_limit_bytes=FIRST_VMEM),
    )(*pieces, here, behind, *tabs)
    got1 = swap_cores(oth1)
    rows = jax.ShapeDtypeStruct((2, 2, BLOCK, D), BF)
    out, lent, own0, oth0 = pl.pallas_call(
        second_kernel,
        in_specs=[vmem] * 12,
        out_specs=[vmem] * 4,
        out_shape=[rows, rows, *grads],
        scratch_shapes=[pltpu.VMEM((8, D), F32), *spare],
        input_output_aliases={0: 2, 1: 3},
        compiler_params=pltpu.CompilerParams(vmem_limit_bytes=SECOND_VMEM),
    )(own0, oth0, *kept, g, decay, cos, sin_a, sin_b, order, out, lent)
    return out, lent, own0, swap_cores(oth0), own1, got1


def pair_sum(layer, own, got, before, passed):
    extra = len(before)

    def kernel(own, got, passed, *refs):
        befores, outs = refs[:extra], refs[extra:]
        outs[6][...] = passed[...]
        for c in range(3):
            for k, (at, row) in enumerate(UNITS[c]):
                rows, cols = slice(row * 64, (row + 1) * 64), slice(k * WIDTH, (k + 1) * WIDTH)
                if at == layer:
                    total = (own[rows, :].astype(F32) + got[rows, :].astype(F32)).astype(BF)
                    outs[2 * c][:, cols] = total[:32]
                    outs[2 * c + 1][:, cols] = total[32:]
                elif befores:
                    for half in range(2):
                        outs[2 * c + half][:, cols] = befores[2 * c + half][:, cols]

    return pl.pallas_call(
        kernel,
        out_shape=[jax.ShapeDtypeStruct((32, w), BF) for w in WIDE for _ in range(2)]
        + [jax.ShapeDtypeStruct(passed.shape, BF)],
        compiler_params=pltpu.CompilerParams(vmem_limit_bytes=PAIR_VMEM),
    )(own, got, passed, *before)


def halve_kernel(*refs):
    for c in range(3):
        total = (refs[c][...].astype(F32) + refs[3 + c][...].astype(F32)).astype(BF)
        half = total.shape[0] // 2
        refs[-6 + 2 * c][...] = total[:half]
        refs[-5 + 2 * c][...] = total[half:]


def halve(keep, got, after):
    vmem, anywhere = pl.BlockSpec(memory_space=pltpu.VMEM), pl.BlockSpec(memory_space=pl.ANY)
    halves = pl.pallas_call(
        halve_kernel,
        in_specs=[vmem] * 6 + [anywhere] * len(after),
        out_shape=[jax.ShapeDtypeStruct((k.shape[0] // 2, *k.shape[1:]), BF) for k in keep for _ in range(2)],
        compiler_params=pltpu.CompilerParams(vmem_limit_bytes=24 << 20),
    )(*keep, *got, *after)
    return halves[0::2], halves[1::2]


def lines_kernel(*refs):
    swap = swap_rows()
    for c, start in enumerate(COLOR_START):
        keep, got = refs[c], refs[3 + c]
        lines = keep.shape[1] // 128
        for i in range(0, FLAT[c], 16):
            block = []
            for k in range(i, i + 16):
                if k < lines:
                    at = slice(k * 128, (k + 1) * 128)
                    block.append(keep[:, at].astype(F32) + got[:, at].astype(F32))
                else:
                    block.append(jnp.zeros((8, 128), F32))
            turned = dot_tn(swap, jnp.concatenate(block, axis=0).astype(BF)).astype(BF)
            for k in range(8):
                refs[6 + k][start + i : start + i + 16] = turned[k * 16 : (k + 1) * 16]


def to_lines(keep, got):
    return pl.pallas_call(
        lines_kernel,
        out_shape=[jax.ShapeDtypeStruct((LINES_ALL, 128), BF) for _ in range(8)],
        compiler_params=pltpu.CompilerParams(vmem_limit_bytes=16 << 20),
    )(*keep, *got)


def scatter_sum(own0, got0, own1, got1, lent, finish):
    *before, lent = pair_sum(1, own1, got1, (), lent)
    *halves, lent = pair_sum(0, own0, got0, before, lent)
    finals = finish(from_behind(lent, 1))
    keep, send = halves[0::2], halves[1::2]
    keep, send = halve(keep, permute_all(send, 2), finals)
    keep, send = halve(keep, permute_all(send, 1), ())
    mine, *rest = to_lines(keep, permute_all(send, 0))
    return finals, [mine] + [lax.ppermute(rest[bits - 1], "fsdp", low_pairs(bits)) for bits in range(1, 8)]


def unpack_kernel(*refs):
    q, k, v, s, o, u, g, d, gain, bias, row = refs[8:]
    row[...] = jnp.zeros_like(row)
    total = refs[0][...].astype(F32)
    for part in refs[1:8]:
        total = total + part[...].astype(F32)
    for units, start in zip(UNITS, (0, FLAT[0], FLAT[0] + FLAT[1])):
        for n, (layer, r) in enumerate(units):
            for j in range(LINES):
                at = start + n * LINES + j
                row[layer, r : r + 1, j * 128 : (j + 1) * 128] = total[at : at + 1]
    for layer in range(2):
        for out, at, width in (
            (q, Q0, 512), (k, K0, 512), (v, V0, 864), (s, S0, 864), (o, O0, 864), (u, U0, 864), (g, G0, 864), (d, D0, 864),
        ):
            out[layer] = row[layer, 0:4, at : at + width]
        norms = jnp.transpose(row[layer, :, V0 + 768 : V0 + VP])
        for kind in range(2):
            gain[layer, kind : kind + 1, :] = norms[NORM_LANE + kind : NORM_LANE + kind + 1, 0:4]
            bias[layer, kind : kind + 1, :] = norms[NORM_LANE + 2 + kind : NORM_LANE + 3 + kind, 0:4]


def unpack(parts):
    shapes = [(2, 4, 512)] * 2 + [(2, 4, 864)] * 6 + [(2, 2, 4)] * 2
    return pl.pallas_call(
        unpack_kernel,
        out_shape=[jax.ShapeDtypeStruct(shape, F32) for shape in shapes],
        scratch_shapes=[pltpu.VMEM((2, 8, WIDTH), F32)],
        compiler_params=pltpu.CompilerParams(vmem_limit_bytes=8 << 20),
    )(*parts)


def from_behind(value, by):
    pairs = [(i, i + by) for i in range(128) if 0 <= i + by < 128]
    return lax.ppermute(value, "fsdp", pairs)


def local(inputs, cotangent, lengths, *weights):
    me = lax.axis_index("fsdp").astype(jnp.int32)
    q, k, v, s, o, u, g, d, gain, bias = weights
    o, d = jnp.swapaxes(o, 1, 2), jnp.swapaxes(d, 1, 2)
    flat, both = pack((q, k, v, s, o, u, g, d, gain, bias), inputs, cotangent)
    pieces, here, behind = gather(flat, both)
    decay, cos, sin_a, sin_b, live, flags, order, third, here = tables(me[None], lengths, here)
    out, lent, own0, got0, own1, got1 = layers(
        pieces, here, behind, (decay, cos, sin_a, sin_b, live, order, third)
    )

    def finish(borrowed):
        mine = flags[:, :, 0:1] > 0
        return [jnp.where(mine, out[k], borrowed[k]) for k in range(2)]

    (result, grad), parts = scatter_sum(own0, got0, own1, got1, lent, finish)
    q, k, v, s, o, u, g, d, gain, bias = unpack(parts)
    return result, grad, q, k, v, s, jnp.swapaxes(o, 1, 2), u, g, jnp.swapaxes(d, 1, 2), gain, bias


def solution(mesh):
    rows, wide = P(None, "fsdp", None), P(None, None, "fsdp")
    weights = (rows, rows, rows, rows, wide, rows, rows, wide, wide, wide)
    return jax.shard_map(
        local,
        mesh=mesh,
        in_specs=(rows, rows, P(), *weights),
        out_specs=(rows, rows, *weights),
        check_vma=False,
    )
```

```python
import functools

import jax
import jax.numpy as jnp
import numpy as np
from jax import lax
from jax.experimental import pallas as pl
from jax.experimental.pallas import tpu as pltpu
from jax.sharding import PartitionSpec as P

HEADS = 2
DK = 256
DV = 432
D = 512
ROWS = 256
WIN = 128
BLOCK = 64
TOKENS = 8192
NSEQ = 192
NORM_EPSILON = 1e-05
GROUP_EPSILON = 1.0
BF = jnp.bfloat16
F32 = jnp.float32

Q0, K0, V0, S0, O0, U0, G0, D0, WIDTH = 0, 512, 1024, 1920, 2816, 3712, 4608, 5504, 6400
VP = 896
NORM_LANE = 96
LINES = WIDTH // 128
FIRST_VMEM = 19 << 20
SECOND_VMEM = 14 << 20
PAIR_VMEM = 20 << 20

UNITS = (((0, 0), (1, 0), (0, 3)), ((0, 1), (1, 1), (1, 3)), ((0, 2), (1, 2)))
FLAT = (160, 160, 112)
LINES_ALL = sum(FLAT)
WIDE = tuple(len(u) * WIDTH for u in UNITS)
COLOR_OF = {unit: (c, k) for c, units in enumerate(UNITS) for k, unit in enumerate(units)}
STRIDE = {"x": 32, "z": 8, "y": 2}
LOW_AXES = "xzy"
HIGH_AXES = ("zyx", "yxz", "xzy")


def mask_of(core, second):
    return 3 if (core == 0) == bool(second) else 1


def low_pairs(bits):
    flip = [(STRIDE[LOW_AXES[k]], bits >> k & 1) for k in range(3)]
    return [(i, i ^ sum(mask_of(i & 1, 0) * stride * bit for stride, bit in flip)) for i in range(128)]


def high_pairs(color, step):
    stride = STRIDE[HIGH_AXES[color][step]]
    return [(i, i ^ (mask_of(i & 1, 1) * stride)) for i in range(128)]


CORE_PAIRS = [(i, i ^ 1) for i in range(128)]


def dot(a, b):
    return lax.dot_general(a, b, (((1,), (0,)), ((), ())), preferred_element_type=F32)


def dot_nt(a, b):
    return lax.dot_general(a, b, (((1,), (1,)), ((), ())), preferred_element_type=F32)


def dot_tn(a, b):
    return lax.dot_general(a, b, (((0,), (0,)), ((), ())), preferred_element_type=F32)


def iota(shape, dim):
    return lax.broadcasted_iota(jnp.int32, shape, dim)


def source_feature(pos, me, third_color):
    core = (me & 1) ^ (pos >> 8)
    row = (pos >> 6) & 3
    color = jnp.where(row == 3, third_color, row)
    device = (me & ~1) | core
    first = jnp.where(core == 0, mask_of(0, 0), mask_of(1, 0))
    second = jnp.where(core == 0, mask_of(0, 1), mask_of(1, 1))
    for k in range(3):
        device = device ^ (((pos >> k) & 1) * first * STRIDE[LOW_AXES[k]])
        strides = [STRIDE[HIGH_AXES[c][k]] for c in range(3)]
        stride = jnp.where(color == 0, strides[0], jnp.where(color == 1, strides[1], strides[2]))
        device = device ^ (((pos >> (3 + k)) & 1) * second * stride)
    return device * 4 + row


def swap_rows():
    r, c = iota((128, 128), 0), iota((128, 128), 1)
    return (((r & 7) * 16 + (r >> 3)) == c).astype(BF)


COLOR_START = (0, FLAT[0], FLAT[0] + FLAT[1])


def pack_kernel(*refs):
    given, (flat, both, row, sems), held = refs[:12], refs[12:16], refs[16:]
    copies = [pltpu.make_async_copy(src, dst, sems.at[k]) for k, (src, dst) in enumerate(zip(given, held))]
    for copy in copies:
        copy.start()
    q, k, v, s, o, u, g, d, gain, bias, x, cot = held
    row[...] = jnp.zeros_like(row)
    for copy in copies:
        copy.wait()
    both[0] = x[...]
    both[1] = cot[...]
    for layer in range(2):
        for weight, at, width in (
            (q, Q0, 512), (k, K0, 512), (v, V0, 864), (s, S0, 864), (o, O0, 864), (u, U0, 864), (g, G0, 864), (d, D0, 864),
        ):
            row[layer, 0:4, at : at + width] = weight[layer].astype(F32)
        norms = jnp.concatenate(
            [part[layer, kind : kind + 1].astype(F32) for part in (gain, bias) for kind in range(2)], axis=0
        ).astype(BF)
        spread = (iota((4, 128), 1) == iota((4, 128), 0) + NORM_LANE).astype(BF)
        row[layer, 0:4, V0 + 768 : V0 + 896] = row[layer, 0:4, V0 + 768 : V0 + 896] + dot_tn(norms, spread)
    for units, lines, start in zip(UNITS, FLAT, (0, FLAT[0], FLAT[0] + FLAT[1])):
        pieces = []
        for layer, r in units:
            for j in range(LINES):
                pieces.append(row[layer, r : r + 1, j * 128 : (j + 1) * 128])
        pad = lines - len(pieces)
        flat[start : start + lines] = jnp.concatenate(pieces + [jnp.zeros((pad, 128), F32)], axis=0).astype(BF)


def in_hbm(values):
    return [pltpu.with_memory_space_constraint(v, pltpu.HBM) for v in values]


def pack(weights, inputs, cotangent):
    values = (*weights, inputs, cotangent)
    return pl.pallas_call(
        pack_kernel,
        in_specs=[pl.BlockSpec(memory_space=pltpu.HBM)] * len(values),
        out_shape=[jax.ShapeDtypeStruct((LINES_ALL, 128), BF), jax.ShapeDtypeStruct((2, 2, BLOCK, D), BF)],
        scratch_shapes=[pltpu.VMEM((2, 8, WIDTH), F32), pltpu.SemaphoreType.DMA((len(values),))]
        + [pltpu.VMEM(v.shape, v.dtype) for v in values],
        compiler_params=pltpu.CompilerParams(vmem_limit_bytes=8 << 20),
    )(*in_hbm(values))


def rows_kernel(*refs):
    parts, both, outs, both_out = refs[:8], refs[8], refs[9:12], refs[12]
    both_out[...] = both[...]
    swap = swap_rows()
    for out, wide, start in zip(outs, WIDE, COLOR_START):
        lines = wide // 128
        for i in range(0, lines, 16):
            block = jnp.concatenate([part[start + i : start + i + 16] for part in parts], axis=0)
            turned = dot(swap, block).astype(BF)
            for k in range(min(16, lines - i)):
                out[:, (i + k) * 128 : (i + k + 1) * 128] = turned[k * 8 : (k + 1) * 8]


def to_rows(parts, both):
    return pl.pallas_call(
        rows_kernel,
        out_shape=[jax.ShapeDtypeStruct((8, w), BF) for w in WIDE] + [jax.ShapeDtypeStruct(both.shape, BF)],
        compiler_params=pltpu.CompilerParams(vmem_limit_bytes=16 << 20),
    )(*parts, both)


def pair_rows_kernel(a, b, c, a_got, b_got, c_got, both, a_out, b_out, c_out, both_out):
    both_out[...] = both[...]
    for mine, got, out in ((a, a_got, a_out), (b, b_got, b_out), (c, c_got, c_out)):
        out[...] = jnp.concatenate([mine[...].astype(F32), got[...].astype(F32)], axis=0).astype(BF)


def pair_rows(mine, got, both):
    return pl.pallas_call(
        pair_rows_kernel,
        out_shape=[jax.ShapeDtypeStruct((16, w), BF) for w in WIDE] + [jax.ShapeDtypeStruct(both.shape, BF)],
        compiler_params=pltpu.CompilerParams(vmem_limit_bytes=16 << 20),
    )(*mine, *got, both)


def stack_all_kernel(a, b, c, a_got, b_got, c_got, behind, a_out, b_out, c_out):
    del behind
    for mine, got, out in ((a, a_got, a_out), (b, b_got, b_out), (c, c_got, c_out)):
        out[0:16] = mine[...]
        out[16:32] = got[...]


def stack_all(mine, got, behind):
    vmem, anywhere = pl.BlockSpec(memory_space=pltpu.VMEM), pl.BlockSpec(memory_space=pl.ANY)
    return pl.pallas_call(
        stack_all_kernel,
        in_specs=[vmem] * 6 + [anywhere],
        out_shape=[jax.ShapeDtypeStruct((32, w), BF) for w in WIDE],
        compiler_params=pltpu.CompilerParams(vmem_limit_bytes=24 << 20),
    )(*mine, *got, behind)


def permute_all(values, step):
    return [lax.ppermute(values[c], "fsdp", high_pairs(c, step)) for c in range(3)]


def swap_cores(value):
    return lax.ppermute(value, "fsdp", CORE_PAIRS)


def gather(flat, both):
    *first, both = to_rows([flat] + [lax.ppermute(flat, "fsdp", low_pairs(bits)) for bits in range(1, 8)], both)
    *first, both = pair_rows(first, permute_all(first, 0), both)
    next_in = from_behind(both, -1)
    halves = stack_all(first, permute_all(first, 1), next_in)
    rest = permute_all(halves, 2)
    return [*halves, *rest, *in_hbm([swap_cores(h) for h in halves]), *[swap_cores(r) for r in rest]], both, next_in


def tables_kernel(me_ref, lengths, trig, here, decay, cos, sin_a, sin_b, live, flags, order, third, here_out):
    here_out[...] = here[...]
    me = me_ref[0]
    first_row = me * BLOCK
    tri = (iota((NSEQ, NSEQ), 0) > iota((NSEQ, NSEQ), 1)).astype(BF)
    lens = lengths[...].astype(F32).astype(BF)
    lens8 = jnp.concatenate([lens, jnp.zeros((6, NSEQ), BF)], axis=0)
    starts_col = dot_nt(tri, lens8)
    starts_row = dot_nt(lens8, tri)
    for b in range(2):
        rows_c = (iota((WIN, NSEQ), 0) + first_row).astype(F32)
        st_r = starts_row[b : b + 1, :]
        anchor_c = jnp.max(jnp.where(st_r <= rows_c, st_r, 0.0), axis=1, keepdims=True)
        rows_r = (iota((NSEQ, WIN), 1) + first_row).astype(F32)
        st_c = starts_col[:, b : b + 1]
        anchor_r = jnp.max(jnp.where(st_c <= rows_r, st_c, 0.0), axis=0, keepdims=True)
        low = first_row.astype(F32)
        row_c = (iota((WIN, 1), 0) + first_row).astype(F32)
        row_r = (iota((1, WIN), 1) + first_row).astype(F32)
        own_c = (anchor_c >= low) & (anchor_c < low + BLOCK) & (row_c < TOKENS)
        own_r = (anchor_r >= low) & (anchor_r < low + BLOCK) & (row_r < TOKENS)
        distance = row_c - row_r
        allowed = (anchor_c == anchor_r) & own_c & own_r & (distance >= 0)
        clamped = jnp.maximum(distance, 0.0)
        for h in range(HEADS):
            rate = float(np.log(np.float32(1.0 - 2.0 ** (-5.0 - h))))
            decay[b, h] = jnp.where(allowed, jnp.exp(rate * clamped), 0.0)
        live[b * WIN : (b + 1) * WIN, :] = jnp.broadcast_to(own_c.astype(F32), (WIN, 128))
        flags[b] = jnp.broadcast_to((anchor_c[:BLOCK] >= low).astype(F32), (BLOCK, 128))
        position = jnp.minimum(row_c - anchor_c, float(WIN - 1))
        hot = (position == iota((WIN, WIN), 1).astype(F32)).astype(F32)
        values = lax.dot_general(
            hot, trig[...], (((1,), (0,)), ((), ())), preferred_element_type=F32, precision=lax.Precision.HIGHEST
        )
        sin = values[:, DK:]
        even = (iota((WIN, DK), 1) & 1) == 0
        cos[b * WIN : (b + 1) * WIN, :] = values[:, :DK]
        sin_a[b * WIN : (b + 1) * WIN, :] = jnp.where(even, -sin, 0.0)
        sin_b[b * WIN : (b + 1) * WIN, :] = jnp.where(even, 0.0, sin)
    pos = iota((1, D), 1)
    order[...] = (iota((D, D), 0) == source_feature(pos, me, 0)).astype(BF)
    for core in range(2):
        base = core * 256 + 192
        want = source_feature(base + iota((64, 1), 0), me, 0)
        have = source_feature(base + iota((1, 64), 1), me, 1)
        third[core] = (want == have).astype(BF)


def trig_table():
    frequency = 1.0 / 10000.0 ** np.linspace(0.0, 1.0, DK // 2, dtype=np.float32)
    frequency = np.repeat(frequency.astype(np.float32), 2)
    phases = np.arange(WIN, dtype=np.float32)[:, None] * frequency
    phases = phases.astype(np.float32).astype(np.float64)
    return np.concatenate([np.cos(phases), np.sin(phases)], axis=1).astype(np.float32)


def tables(me, lengths, here):
    return pl.pallas_call(
        tables_kernel,
        in_specs=[
            pl.BlockSpec(memory_space=pltpu.SMEM),
            pl.BlockSpec(memory_space=pltpu.VMEM),
            pl.BlockSpec(memory_space=pltpu.VMEM),
            pl.BlockSpec(memory_space=pltpu.VMEM),
        ],
        out_shape=[
            jax.ShapeDtypeStruct((2, HEADS, WIN, WIN), F32),
            jax.ShapeDtypeStruct((ROWS, DK), F32),
            jax.ShapeDtypeStruct((ROWS, DK), F32),
            jax.ShapeDtypeStruct((ROWS, DK), F32),
            jax.ShapeDtypeStruct((ROWS, 128), F32),
            jax.ShapeDtypeStruct((2, BLOCK, 128), F32),
            jax.ShapeDtypeStruct((D, D), BF),
            jax.ShapeDtypeStruct((2, 64, 64), BF),
            jax.ShapeDtypeStruct(here.shape, BF),
        ],
        compiler_params=pltpu.CompilerParams(vmem_limit_bytes=16 << 20),
    )(me, lengths, jnp.asarray(trig_table()), here)


def norm_parts(values):
    center = values - jnp.mean(values, axis=-1, keepdims=True)
    inv = lax.rsqrt(jnp.mean(center * center, axis=-1, keepdims=True) + NORM_EPSILON)
    return center * inv, inv


def norm_back(grad, hat, inv, gain):
    scaled = grad * gain
    mean_one = jnp.mean(scaled, axis=-1, keepdims=True)
    mean_two = jnp.mean(scaled * hat, axis=-1, keepdims=True)
    return inv * (scaled - mean_one - hat * mean_two)


def rotated(v, cos, sin_a, sin_b):
    return v * cos + pltpu.roll(v, DK - 1, 1) * sin_a + pltpu.roll(v, 1, 1) * sin_b


def rotated_back(v, cos, sin_a, sin_b):
    return v * cos - pltpu.roll(v, DK - 1, 1) * sin_a - pltpu.roll(v, 1, 1) * sin_b


def sigmoid(v):
    return 0.5 * jnp.tanh(0.5 * v) + 0.5


GELU_C = float(np.sqrt(2.0 / np.pi))


def gelu_tanh(v):
    return jnp.tanh(GELU_C * (v + 0.044715 * (v * v * v)))


class Saved:
    F32_PARTS = (("up", VP), ("gt", VP), ("m", D), ("r", VP), ("gp", VP), ("x", D))
    BF_PARTS = (("h", VP), ("b", D), ("u", VP), ("p", 2 * WIN), ("v", VP), ("k", D), ("q", D), ("a", D))
    WIDTHS = tuple(sum(width for _, width in parts) for parts in (F32_PARTS, BF_PARTS))
    DTYPES = (F32, BF)

    def __init__(self, refs):
        for ref, parts in zip(refs, (self.F32_PARTS, self.BF_PARTS)):
            at = 0
            for name, width in parts:
                setattr(self, name, ref.at[:, at : at + width])
                at += width

    @classmethod
    def shapes(cls):
        return [((ROWS, width), dtype) for width, dtype in zip(cls.WIDTHS, cls.DTYPES)]


def head_masks(rows):
    lane = iota((rows, VP), 1)
    return lane < DV, (lane >= DV) & (lane < 2 * DV)


def forward(w, gb, sv, decay, cos, sin_a, sin_b, later):
    x = sv.x[...]
    hat, _ = norm_parts(x)
    sv.a[...] = (hat * gb[0:1, :] + gb[2:3, :]).astype(BF)
    a = sv.a[...]
    tabs = (cos[...], sin_a[...], sin_b[...])
    for h in range(HEADS):
        at = slice(h * DK, (h + 1) * DK)
        sv.q[:, at] = rotated(w.times(a, Q0 + h * DK, DK), *tabs).astype(BF)
        key = rotated(w.times(a, K0 + h * DK, DK), *tabs) * DK ** (-0.5)
        sv.k[:, at] = key.astype(BF)
    sv.v[...] = w.times(a, V0, VP).astype(BF)
    in_head = head_masks(WIN)
    for b in range(2):
        rows = slice(b * WIN, (b + 1) * WIN)
        for h in range(HEADS):
            at = slice(h * DK, (h + 1) * DK)
            scores = dot_nt(sv.q[rows, at], sv.k[rows, at])
            sv.p[rows, h * WIN : (h + 1) * WIN] = (decay[b, h] * scores).astype(BF)
        v = sv.v[rows, :]
        both = jnp.concatenate([jnp.where(in_head[0], v, 0), jnp.where(in_head[1], v, 0)], axis=0)
        sv.r[rows, :] = dot(sv.p[rows, :], both)
    for copy in later:
        copy.wait()
    one, two = group_scales(sv.r[...])
    for at, end in CHUNKS:
        gate = w.times(a, S0 + at, end - at)
        sv.gp[:, at:end] = gate
        scale = by_head(one, two, at, end)
        sv.u[:, at:end] = (sv.r[:, at:end] * scale * (gate * sigmoid(gate))).astype(BF)
    sv.m[...] = x + w.turned(sv.u[...], O0, VP)
    hat, _ = norm_parts(sv.m[...])
    sv.b[...] = (hat * gb[1:2, :] + gb[3:4, :]).astype(BF)
    b = sv.b[...]
    for at, end in CHUNKS:
        up = w.times(b, U0 + at, end - at)
        gate = w.times(b, G0 + at, end - at)
        sv.up[:, at:end] = up
        sv.gt[:, at:end] = gate
        sv.h[:, at:end] = (0.5 * up * (1.0 + gelu_tanh(up)) * gate).astype(BF)
    return sv.m[...] + w.turned(sv.h[...], D0, VP)


def head_sums(values):
    first, second = head_masks(ROWS)
    return (
        jnp.sum(jnp.where(first, values, 0.0), axis=-1, keepdims=True),
        jnp.sum(jnp.where(second, values, 0.0), axis=-1, keepdims=True),
    )


def by_head(one, two, at=0, end=VP):
    return jnp.where(iota((ROWS, end - at), 1) + at < DV, one, two)


def group_scales(r):
    one, two = head_sums(r * r)
    return lax.rsqrt(one / DV + GROUP_EPSILON), lax.rsqrt(two / DV + GROUP_EPSILON)


CHUNKS = ((0, 256), (256, 512), (512, 768), (768, 896))


class Weights:
    def __init__(self, refs, third, outs=None):
        self.own, self.oth = refs
        self.third, self.outs = third, outs or refs

    def times(self, a, at, width):
        one = dot(a[:, :256], self.own[:, at : at + width])
        return one + dot(a[:, 256:], self.oth[:, at : at + width])

    def turned(self, a, at, width):
        return jnp.concatenate([dot_nt(a, self.own[:, at : at + width]), dot_nt(a, self.oth[:, at : at + width])], axis=1)

    def put(self, at, width, grad):
        low = grad.astype(BF)
        for core, out in enumerate(self.outs):
            part = low[core * 256 : (core + 1) * 256]
            if self.third is None:
                out[:, at : at + width] = part
            else:
                out[0:192, at : at + width] = part[0:192]
                out[192:256, at : at + width] = dot_tn(self.third[core], part[192:256]).astype(BF)


def backward(w, gb, sv, decay, cos, sin_a, sin_b, g, spare, dn):
    f = g.astype(BF)
    dup, dgt = spare.at[0], spare.at[1]
    for at, end in CHUNKS:
        dh = w.times(f, D0 + at, end - at)
        up = sv.up[:, at:end]
        t = gelu_tanh(up)
        half = 0.5 * (1.0 + t)
        dgt[:, at:end] = (dh * (up * half)).astype(BF)
        slope = half + 0.5 * up * (1.0 - t * t) * (GELU_C * (1.0 + 3 * 0.044715 * (up * up)))
        dup[:, at:end] = (dh * sv.gt[:, at:end] * slope).astype(BF)
    db = w.turned(dup[...], U0, VP) + w.turned(dgt[...], G0, VP)
    w.put(D0, VP, dot_tn(f, sv.h[...]))
    b = sv.b[...]
    w.put(U0, VP, dot_tn(b, dup[...]))
    w.put(G0, VP, dot_tn(b, dgt[...]))
    hat, inv = norm_parts(sv.m[...])
    dgain_two = jnp.sum(db * hat, axis=0, keepdims=True)
    dbias_two = jnp.sum(db, axis=0, keepdims=True)
    dm = g + norm_back(db, hat, inv, gb[1:2, :])
    e = dm.astype(BF)
    scales = group_scales(sv.r[...])
    sums = [0.0, 0.0]
    dgp, dr = spare.at[0], spare.at[1]
    for at, end in CHUNKS:
        du = w.times(e, O0 + at, end - at)
        r = sv.r[:, at:end]
        gate = sv.gp[:, at:end]
        sig = sigmoid(gate)
        dgp[:, at:end] = (du * (r * by_head(*scales, at, end)) * (sig * (1.0 + gate * (1.0 - sig)))).astype(BF)
        part = du * (gate * sig)
        dn[:, at:end] = part
        lane = iota((ROWS, end - at), 1) + at
        product = part * r
        sums[0] = sums[0] + jnp.sum(jnp.where(lane < DV, product, 0.0), axis=-1, keepdims=True)
        sums[1] = sums[1] + jnp.sum(jnp.where((lane >= DV) & (lane < 2 * DV), product, 0.0), axis=-1, keepdims=True)
    w.put(O0, VP, dot_tn(e, sv.u[...]))
    cubes = [scale * scale * scale * (total / DV) for scale, total in zip(scales, sums)]
    for at, end in CHUNKS:
        part = by_head(*scales, at, end) * dn[:, at:end] - sv.r[:, at:end] * by_head(*cubes, at, end)
        dr[:, at:end] = part.astype(BF)
    a = sv.a[...]
    da = w.turned(dgp[...], S0, VP)
    w.put(S0, VP, dot_tn(a, dgp[...]))
    in_head = head_masks(WIN)
    tabs = (cos[...], sin_a[...], sin_b[...])
    dvs, dqs, dks = [], [[], []], [[], []]
    for bt in range(2):
        rows = slice(bt * WIN, (bt + 1) * WIN)
        part = dr[rows, :]
        both = jnp.concatenate([jnp.where(in_head[0], part, 0), jnp.where(in_head[1], part, 0)], axis=0)
        p = sv.p[rows, :]
        stacked = jnp.concatenate([p[:, :WIN], p[:, WIN:]], axis=0)
        dvs.append(dot_tn(stacked, both).astype(BF))
        dp = dot_nt(both, sv.v[rows, :])
        for h in range(HEADS):
            at = slice(h * DK, (h + 1) * DK)
            ds = (decay[bt, h] * dp[h * WIN : (h + 1) * WIN]).astype(BF)
            dqs[h].append(dot(ds, sv.k[rows, at]))
            dks[h].append(dot_tn(ds, sv.q[rows, at]))
    dv = jnp.concatenate(dvs, axis=0)
    dq = jnp.concatenate([rotated_back(jnp.concatenate(dqs[h], axis=0), *tabs).astype(BF) for h in range(HEADS)], axis=1)
    dk = jnp.concatenate(
        [rotated_back(jnp.concatenate(dks[h], axis=0) * DK ** (-0.5), *tabs).astype(BF) for h in range(HEADS)], axis=1
    )
    da = da + w.turned(dv, V0, VP) + w.turned(dq, Q0, 512) + w.turned(dk, K0, 512)
    w.put(Q0, 512, dot_tn(a, dq))
    w.put(K0, 512, dot_tn(a, dk))
    hat, inv = norm_parts(sv.x[...])
    dgain_one = jnp.sum(da * hat, axis=0, keepdims=True)
    dbias_one = jnp.sum(da, axis=0, keepdims=True)
    norms = jnp.concatenate([dgain_one, dgain_two, dbias_one, dbias_two, jnp.zeros((4, D), F32)], axis=0).astype(BF)
    spread = (iota((8, VP), 1) == iota((8, VP), 0) + 864).astype(BF)
    w.put(V0, VP, dot_tn(a, dv) + dot_tn(norms, spread))
    return dm + norm_back(da, hat, inv, gb[0:1, :])


def window_rows(here, behind, k):
    return jnp.concatenate([here[k, 0], behind[k, 0], here[k, 1], behind[k, 1]], axis=0)


def put_norms(gb, weights):
    pick = ((iota((8, 128), 1) == iota((8, 128), 0) + NORM_LANE) & (iota((8, 128), 0) < 4)).astype(BF)
    gb[...] = weights.turned(pick, V0 + 768, 128)


def put_rows(result, order, out, lent):
    result = dot_nt(result.astype(BF), order[...]).astype(BF)
    for b in range(2):
        out[b] = result[b * WIN : b * WIN + BLOCK]
        lent[b] = result[b * WIN + BLOCK : (b + 1) * WIN]


def first_kernel(*refs):
    pieces, refs = refs[:12], refs[12:]
    here, behind, decay, cos, sin_a, sin_b, live, order, third = refs[:9]
    out, lent, g_out = refs[9:12]
    held = (refs[12:14], refs[14:16])
    gb, sems, spare, dn = refs[18:22]
    saved = [Saved(refs[16:18]), Saved(refs[22:24])]
    groups = []
    count = 0
    for layer, start, end in ((0, 0, S0), (0, S0, WIDTH), (1, 0, WIDTH)):
        group = []
        for core in range(2):
            for row in range(4):
                color, unit = COLOR_OF[(layer, row)]
                for half in range(2):
                    piece = pieces[core * 6 + half * 3 + color]
                    at = unit * WIDTH
                    rows = slice(row * 64 + half * 32, row * 64 + half * 32 + 32)
                    copy = pltpu.make_async_copy(
                        piece.at[:, at + start : at + end], held[layer][core].at[rows, start:end], sems.at[count]
                    )
                    group.append(copy)
                    count += 1
        groups.append(group)
    for copy in groups[0] + groups[1]:
        copy.start()
    saved[0].x[...] = dot(window_rows(here, behind, 0), order[...])
    tabs = (decay, cos, sin_a, sin_b)
    weights = [Weights(held[0], None), Weights(held[1], third)]
    for copy in groups[0]:
        copy.wait()
    for copy in groups[2]:
        copy.start()
    put_norms(gb.at[0], weights[0])
    saved[1].x[...] = forward(weights[0], gb.at[0], saved[0], *tabs, groups[1])
    for copy in groups[2]:
        copy.wait()
    for core in range(2):
        at = slice(192, 256)
        held[1][core][at, :] = dot(third[core], held[1][core][at, :]).astype(BF)
    put_norms(gb.at[1], weights[1])
    put_rows(forward(weights[1], gb.at[1], saved[1], *tabs, []), order, out, lent)
    g = dot(window_rows(here, behind, 1), order[...]) * live[:, 0:1]
    g_out[...] = backward(weights[1], gb.at[1], saved[1], *tabs, g, spare, dn)


def second_kernel(*refs):
    held, kept = refs[:2], refs[2:4]
    g_in, decay, cos, sin_a, sin_b, order, out_one, lent_one = refs[4:12]
    out, lent = refs[12:14]
    gb, spare, dn = refs[16:19]
    weights = Weights(held, None, refs[14:16])
    put_norms(gb, weights)
    g = backward(weights, gb, Saved(kept), decay, cos, sin_a, sin_b, g_in[...], spare, dn)
    out[0] = out_one[...]
    lent[0] = lent_one[...]
    put_rows(g, order, out.at[1], lent.at[1])


def layers(pieces, here, behind, tabs):
    decay, cos, sin_a, sin_b, live, order, third = tabs
    grads = [jax.ShapeDtypeStruct((256, WIDTH), BF)] * 2
    saved = Saved.shapes()
    spare = [pltpu.VMEM((2, ROWS, VP), BF), pltpu.VMEM((ROWS, VP), F32)]
    any_space, hbm = pl.BlockSpec(memory_space=pl.ANY), pl.BlockSpec(memory_space=pltpu.HBM)
    vmem = pl.BlockSpec(memory_space=pltpu.VMEM)
    out, lent, g, own0, oth0, own1, oth1, *kept = pl.pallas_call(
        first_kernel,
        in_specs=[any_space] * 6 + [hbm] * 3 + [any_space] * 3 + [vmem] * 9,
        out_specs=[vmem] * 9,
        out_shape=[jax.ShapeDtypeStruct((2, BLOCK, D), BF)] * 2
        + [jax.ShapeDtypeStruct((ROWS, D), F32), *grads, *grads]
        + [jax.ShapeDtypeStruct(*one) for one in saved],
        scratch_shapes=[pltpu.VMEM((2, 8, D), F32), pltpu.SemaphoreType.DMA((48,)), *spare]
        + [pltpu.VMEM(*one) for one in saved],
        compiler_params=pltpu.CompilerParams(vmem_limit_bytes=FIRST_VMEM),
    )(*pieces, here, behind, *tabs)
    got1 = swap_cores(oth1)
    rows = jax.ShapeDtypeStruct((2, 2, BLOCK, D), BF)
    out, lent, own0, oth0 = pl.pallas_call(
        second_kernel,
        in_specs=[vmem] * 12,
        out_specs=[vmem] * 4,
        out_shape=[rows, rows, *grads],
        scratch_shapes=[pltpu.VMEM((8, D), F32), *spare],
        input_output_aliases={0: 2, 1: 3},
        compiler_params=pltpu.CompilerParams(vmem_limit_bytes=SECOND_VMEM),
    )(own0, oth0, *kept, g, decay, cos, sin_a, sin_b, order, out, lent)
    return out, lent, own0, swap_cores(oth0), own1, got1


def pair_sum(layer, own, got, before, passed):
    extra = len(before)

    def kernel(own, got, passed, *refs):
        befores, outs = refs[:extra], refs[extra:]
        outs[6][...] = passed[...]
        for c in range(3):
            for k, (at, row) in enumerate(UNITS[c]):
                rows, cols = slice(row * 64, (row + 1) * 64), slice(k * WIDTH, (k + 1) * WIDTH)
                if at == layer:
                    total = (own[rows, :].astype(F32) + got[rows, :].astype(F32)).astype(BF)
                    outs[2 * c][:, cols] = total[:32]
                    outs[2 * c + 1][:, cols] = total[32:]
                elif befores:
                    for half in range(2):
                        outs[2 * c + half][:, cols] = befores[2 * c + half][:, cols]

    return pl.pallas_call(
        kernel,
        out_shape=[jax.ShapeDtypeStruct((32, w), BF) for w in WIDE for _ in range(2)]
        + [jax.ShapeDtypeStruct(passed.shape, BF)],
        compiler_params=pltpu.CompilerParams(vmem_limit_bytes=PAIR_VMEM),
    )(own, got, passed, *before)


def halve_kernel(*refs):
    for c in range(3):
        total = (refs[c][...].astype(F32) + refs[3 + c][...].astype(F32)).astype(BF)
        half = total.shape[0] // 2
        refs[-6 + 2 * c][...] = total[:half]
        refs[-5 + 2 * c][...] = total[half:]


def halve(keep, got, after):
    vmem, anywhere = pl.BlockSpec(memory_space=pltpu.VMEM), pl.BlockSpec(memory_space=pl.ANY)
    halves = pl.pallas_call(
        halve_kernel,
        in_specs=[vmem] * 6 + [anywhere] * len(after),
        out_shape=[jax.ShapeDtypeStruct((k.shape[0] // 2, *k.shape[1:]), BF) for k in keep for _ in range(2)],
        compiler_params=pltpu.CompilerParams(vmem_limit_bytes=24 << 20),
    )(*keep, *got, *after)
    return halves[0::2], halves[1::2]


def lines_kernel(*refs):
    swap = swap_rows()
    for c, start in enumerate(COLOR_START):
        keep, got = refs[c], refs[3 + c]
        lines = keep.shape[1] // 128
        for i in range(0, FLAT[c], 16):
            block = []
            for k in range(i, i + 16):
                if k < lines:
                    at = slice(k * 128, (k + 1) * 128)
                    block.append(keep[:, at].astype(F32) + got[:, at].astype(F32))
                else:
                    block.append(jnp.zeros((8, 128), F32))
            turned = dot_tn(swap, jnp.concatenate(block, axis=0).astype(BF)).astype(BF)
            for k in range(8):
                refs[6 + k][start + i : start + i + 16] = turned[k * 16 : (k + 1) * 16]


def to_lines(keep, got):
    return pl.pallas_call(
        lines_kernel,
        out_shape=[jax.ShapeDtypeStruct((LINES_ALL, 128), BF) for _ in range(8)],
        compiler_params=pltpu.CompilerParams(vmem_limit_bytes=16 << 20),
    )(*keep, *got)


def scatter_sum(own0, got0, own1, got1, lent, finish):
    *before, lent = pair_sum(1, own1, got1, (), lent)
    *halves, lent = pair_sum(0, own0, got0, before, lent)
    finals = finish(from_behind(lent, 1))
    keep, send = halves[0::2], halves[1::2]
    keep, send = halve(keep, permute_all(send, 2), finals)
    keep, send = halve(keep, permute_all(send, 1), ())
    mine, *rest = to_lines(keep, permute_all(send, 0))
    return finals, [mine] + [lax.ppermute(rest[bits - 1], "fsdp", low_pairs(bits)) for bits in range(1, 8)]


def unpack_kernel(*refs):
    q, k, v, s, o, u, g, d, gain, bias, row = refs[8:]
    row[...] = jnp.zeros_like(row)
    total = refs[0][...].astype(F32)
    for part in refs[1:8]:
        total = total + part[...].astype(F32)
    for units, start in zip(UNITS, (0, FLAT[0], FLAT[0] + FLAT[1])):
        for n, (layer, r) in enumerate(units):
            for j in range(LINES):
                at = start + n * LINES + j
                row[layer, r : r + 1, j * 128 : (j + 1) * 128] = total[at : at + 1]
    for layer in range(2):
        for out, at, width in (
            (q, Q0, 512), (k, K0, 512), (v, V0, 864), (s, S0, 864), (o, O0, 864), (u, U0, 864), (g, G0, 864), (d, D0, 864),
        ):
            out[layer] = row[layer, 0:4, at : at + width]
        norms = jnp.transpose(row[layer, :, V0 + 768 : V0 + VP])
        for kind in range(2):
            gain[layer, kind : kind + 1, :] = norms[NORM_LANE + kind : NORM_LANE + kind + 1, 0:4]
            bias[layer, kind : kind + 1, :] = norms[NORM_LANE + 2 + kind : NORM_LANE + 3 + kind, 0:4]


def unpack(parts):
    shapes = [(2, 4, 512)] * 2 + [(2, 4, 864)] * 6 + [(2, 2, 4)] * 2
    return pl.pallas_call(
        unpack_kernel,
        out_shape=[jax.ShapeDtypeStruct(shape, F32) for shape in shapes],
        scratch_shapes=[pltpu.VMEM((2, 8, WIDTH), F32)],
        compiler_params=pltpu.CompilerParams(vmem_limit_bytes=8 << 20),
    )(*parts)


def from_behind(value, by):
    pairs = [(i, i + by) for i in range(128) if 0 <= i + by < 128]
    return lax.ppermute(value, "fsdp", pairs)


def local(inputs, cotangent, lengths, *weights):
    me = lax.axis_index("fsdp").astype(jnp.int32)
    q, k, v, s, o, u, g, d, gain, bias = weights
    o, d = jnp.swapaxes(o, 1, 2), jnp.swapaxes(d, 1, 2)
    flat, both = pack((q, k, v, s, o, u, g, d, gain, bias), inputs, cotangent)
    pieces, here, behind = gather(flat, both)
    decay, cos, sin_a, sin_b, live, flags, order, third, here = tables(me[None], lengths, here)
    out, lent, own0, got0, own1, got1 = layers(
        pieces, here, behind, (decay, cos, sin_a, sin_b, live, order, third)
    )

    def finish(borrowed):
        mine = flags[:, :, 0:1] > 0
        return [jnp.where(mine, out[k], borrowed[k]) for k in range(2)]

    (result, grad), parts = scatter_sum(own0, got0, own1, got1, lent, finish)
    q, k, v, s, o, u, g, d, gain, bias = unpack(parts)
    return result, grad, q, k, v, s, jnp.swapaxes(o, 1, 2), u, g, jnp.swapaxes(d, 1, 2), gain, bias


def solution(mesh):
    rows, wide = P(None, "fsdp", None), P(None, None, "fsdp")
    weights = (rows, rows, rows, rows, wide, rows, rows, wide, wide, wide)
    return jax.shard_map(
        local,
        mesh=mesh,
        in_specs=(rows, rows, P(), *weights),
        out_specs=(rows, rows, *weights),
        check_vma=False,
    )
```

```python
import functools

import jax
import jax.numpy as jnp
import numpy as np
from jax import lax
from jax.experimental import pallas as pl
from jax.experimental.pallas import tpu as pltpu
from jax.sharding import PartitionSpec as P

HEADS = 2
DK = 256
DV = 432
D = 512
ROWS = 256
WIN = 128
BLOCK = 64
TOKENS = 8192
NSEQ = 192
NORM_EPSILON = 1e-05
GROUP_EPSILON = 1.0
BF = jnp.bfloat16
F32 = jnp.float32

Q0, K0, V0, S0, O0, U0, G0, D0, WIDTH = 0, 512, 1024, 1920, 2816, 3712, 4608, 5504, 6400
VP = 896
NORM_LANE = 96
LINES = WIDTH // 128
FIRST_VMEM = 19 << 20
SECOND_VMEM = 14 << 20
PAIR_VMEM = 20 << 20

UNITS = (((0, 0), (1, 0), (0, 3)), ((0, 1), (1, 1), (1, 3)), ((0, 2), (1, 2)))
FLAT = (160, 160, 112)
LINES_ALL = sum(FLAT)
WIDE = tuple(len(u) * WIDTH for u in UNITS)
COLOR_OF = {unit: (c, k) for c, units in enumerate(UNITS) for k, unit in enumerate(units)}
STRIDE = {"x": 32, "z": 8, "y": 2}
LOW_AXES = "xzy"
HIGH_AXES = ("zyx", "yxz", "xzy")


def mask_of(core, second):
    return 3 if (core == 0) == bool(second) else 1


def low_pairs(bits):
    flip = [(STRIDE[LOW_AXES[k]], bits >> k & 1) for k in range(3)]
    return [(i, i ^ sum(mask_of(i & 1, 0) * stride * bit for stride, bit in flip)) for i in range(128)]


def high_pairs(color, step):
    stride = STRIDE[HIGH_AXES[color][step]]
    return [(i, i ^ (mask_of(i & 1, 1) * stride)) for i in range(128)]


CORE_PAIRS = [(i, i ^ 1) for i in range(128)]


def dot(a, b):
    return lax.dot_general(a, b, (((1,), (0,)), ((), ())), preferred_element_type=F32)


def dot_nt(a, b):
    return lax.dot_general(a, b, (((1,), (1,)), ((), ())), preferred_element_type=F32)


def dot_tn(a, b):
    return lax.dot_general(a, b, (((0,), (0,)), ((), ())), preferred_element_type=F32)


def iota(shape, dim):
    return lax.broadcasted_iota(jnp.int32, shape, dim)


def source_feature(pos, me, third_color):
    core = (me & 1) ^ (pos >> 8)
    row = (pos >> 6) & 3
    color = jnp.where(row == 3, third_color, row)
    device = (me & ~1) | core
    first = jnp.where(core == 0, mask_of(0, 0), mask_of(1, 0))
    second = jnp.where(core == 0, mask_of(0, 1), mask_of(1, 1))
    for k in range(3):
        device = device ^ (((pos >> k) & 1) * first * STRIDE[LOW_AXES[k]])
        strides = [STRIDE[HIGH_AXES[c][k]] for c in range(3)]
        stride = jnp.where(color == 0, strides[0], jnp.where(color == 1, strides[1], strides[2]))
        device = device ^ (((pos >> (3 + k)) & 1) * second * stride)
    return device * 4 + row


def swap_rows():
    r, c = iota((128, 128), 0), iota((128, 128), 1)
    return (((r & 7) * 16 + (r >> 3)) == c).astype(BF)


COLOR_START = (0, FLAT[0], FLAT[0] + FLAT[1])


def pack_kernel(*refs):
    given, (flat, both, row, sems), held = refs[:12], refs[12:16], refs[16:]
    copies = [pltpu.make_async_copy(src, dst, sems.at[k]) for k, (src, dst) in enumerate(zip(given, held))]
    for copy in copies:
        copy.start()
    q, k, v, s, o, u, g, d, gain, bias, x, cot = held
    row[...] = jnp.zeros_like(row)
    for copy in copies:
        copy.wait()
    both[0] = x[...]
    both[1] = cot[...]
    for layer in range(2):
        for weight, at, width in (
            (q, Q0, 512), (k, K0, 512), (v, V0, 864), (s, S0, 864), (o, O0, 864), (u, U0, 864), (g, G0, 864), (d, D0, 864),
        ):
            row[layer, 0:4, at : at + width] = weight[layer].astype(F32)
        norms = jnp.concatenate(
            [part[layer, kind : kind + 1].astype(F32) for part in (gain, bias) for kind in range(2)], axis=0
        ).astype(BF)
        spread = (iota((4, 128), 1) == iota((4, 128), 0) + NORM_LANE).astype(BF)
        row[layer, 0:4, V0 + 768 : V0 + 896] = row[layer, 0:4, V0 + 768 : V0 + 896] + dot_tn(norms, spread)
    for units, lines, start in zip(UNITS, FLAT, (0, FLAT[0], FLAT[0] + FLAT[1])):
        pieces = []
        for layer, r in units:
            for j in range(LINES):
                pieces.append(row[layer, r : r + 1, j * 128 : (j + 1) * 128])
        pad = lines - len(pieces)
        flat[start : start + lines] = jnp.concatenate(pieces + [jnp.zeros((pad, 128), F32)], axis=0).astype(BF)


def in_hbm(values):
    return [pltpu.with_memory_space_constraint(v, pltpu.HBM) for v in values]


def pack(weights, inputs, cotangent):
    values = (*weights, inputs, cotangent)
    return pl.pallas_call(
        pack_kernel,
        in_specs=[pl.BlockSpec(memory_space=pltpu.HBM)] * len(values),
        out_shape=[jax.ShapeDtypeStruct((LINES_ALL, 128), BF), jax.ShapeDtypeStruct((2, 2, BLOCK, D), BF)],
        scratch_shapes=[pltpu.VMEM((2, 8, WIDTH), F32), pltpu.SemaphoreType.DMA((len(values),))]
        + [pltpu.VMEM(v.shape, v.dtype) for v in values],
        compiler_params=pltpu.CompilerParams(vmem_limit_bytes=8 << 20),
    )(*in_hbm(values))


def rows_kernel(*refs):
    parts, both, outs, both_out = refs[:8], refs[8], refs[9:12], refs[12]
    both_out[...] = both[...]
    swap = swap_rows()
    for out, wide, start in zip(outs, WIDE, COLOR_START):
        lines = wide // 128
        for i in range(0, lines, 16):
            block = jnp.concatenate([part[start + i : start + i + 16] for part in parts], axis=0)
            turned = dot(swap, block).astype(BF)
            for k in range(min(16, lines - i)):
                out[:, (i + k) * 128 : (i + k + 1) * 128] = turned[k * 8 : (k + 1) * 8]


def to_rows(parts, both):
    return pl.pallas_call(
        rows_kernel,
        out_shape=[jax.ShapeDtypeStruct((8, w), BF) for w in WIDE] + [jax.ShapeDtypeStruct(both.shape, BF)],
        compiler_params=pltpu.CompilerParams(vmem_limit_bytes=16 << 20),
    )(*parts, both)


def pair_rows_kernel(a, b, c, a_got, b_got, c_got, both, a_out, b_out, c_out, both_out):
    both_out[...] = both[...]
    for mine, got, out in ((a, a_got, a_out), (b, b_got, b_out), (c, c_got, c_out)):
        out[...] = jnp.concatenate([mine[...].astype(F32), got[...].astype(F32)], axis=0).astype(BF)


def pair_rows(mine, got, both):
    return pl.pallas_call(
        pair_rows_kernel,
        out_shape=[jax.ShapeDtypeStruct((16, w), BF) for w in WIDE] + [jax.ShapeDtypeStruct(both.shape, BF)],
        compiler_params=pltpu.CompilerParams(vmem_limit_bytes=16 << 20),
    )(*mine, *got, both)


def stack_all_kernel(a, b, c, a_got, b_got, c_got, behind, a_out, b_out, c_out):
    del behind
    for mine, got, out in ((a, a_got, a_out), (b, b_got, b_out), (c, c_got, c_out)):
        out[0:16] = mine[...]
        out[16:32] = got[...]


def stack_all(mine, got, behind):
    vmem, anywhere = pl.BlockSpec(memory_space=pltpu.VMEM), pl.BlockSpec(memory_space=pl.ANY)
    return pl.pallas_call(
        stack_all_kernel,
        in_specs=[vmem] * 6 + [anywhere],
        out_shape=[jax.ShapeDtypeStruct((32, w), BF) for w in WIDE],
        compiler_params=pltpu.CompilerParams(vmem_limit_bytes=24 << 20),
    )(*mine, *got, behind)


def permute_all(values, step):
    return [lax.ppermute(values[c], "fsdp", high_pairs(c, step)) for c in range(3)]


def swap_cores(value):
    return lax.ppermute(value, "fsdp", CORE_PAIRS)


def gather(flat, both):
    *first, both = to_rows([flat] + [lax.ppermute(flat, "fsdp", low_pairs(bits)) for bits in range(1, 8)], both)
    *first, both = pair_rows(first, permute_all(first, 0), both)
    next_in = from_behind(both, -1)
    halves = stack_all(first, permute_all(first, 1), next_in)
    rest = permute_all(halves, 2)
    return [*halves, *rest, *in_hbm([swap_cores(h) for h in halves]), *[swap_cores(r) for r in rest]], both, next_in


def tables_kernel(me_ref, lengths, trig, here, decay, cos, sin_a, sin_b, live, flags, order, third, here_out):
    here_out[...] = here[...]
    me = me_ref[0]
    first_row = me * BLOCK
    tri = (iota((NSEQ, NSEQ), 0) > iota((NSEQ, NSEQ), 1)).astype(BF)
    lens = lengths[...].astype(F32).astype(BF)
    lens8 = jnp.concatenate([lens, jnp.zeros((6, NSEQ), BF)], axis=0)
    starts_col = dot_nt(tri, lens8)
    starts_row = dot_nt(lens8, tri)
    for b in range(2):
        rows_c = (iota((WIN, NSEQ), 0) + first_row).astype(F32)
        st_r = starts_row[b : b + 1, :]
        anchor_c = jnp.max(jnp.where(st_r <= rows_c, st_r, 0.0), axis=1, keepdims=True)
        rows_r = (iota((NSEQ, WIN), 1) + first_row).astype(F32)
        st_c = starts_col[:, b : b + 1]
        anchor_r = jnp.max(jnp.where(st_c <= rows_r, st_c, 0.0), axis=0, keepdims=True)
        low = first_row.astype(F32)
        row_c = (iota((WIN, 1), 0) + first_row).astype(F32)
        row_r = (iota((1, WIN), 1) + first_row).astype(F32)
        own_c = (anchor_c >= low) & (anchor_c < low + BLOCK) & (row_c < TOKENS)
        own_r = (anchor_r >= low) & (anchor_r < low + BLOCK) & (row_r < TOKENS)
        distance = row_c - row_r
        allowed = (anchor_c == anchor_r) & own_c & own_r & (distance >= 0)
        clamped = jnp.maximum(distance, 0.0)
        for h in range(HEADS):
            rate = float(np.log(np.float32(1.0 - 2.0 ** (-5.0 - h))))
            decay[b, h] = jnp.where(allowed, jnp.exp(rate * clamped), 0.0)
        live[b * WIN : (b + 1) * WIN, :] = jnp.broadcast_to(own_c.astype(F32), (WIN, 128))
        flags[b] = jnp.broadcast_to((anchor_c[:BLOCK] >= low).astype(F32), (BLOCK, 128))
        position = jnp.minimum(row_c - anchor_c, float(WIN - 1))
        hot = (position == iota((WIN, WIN), 1).astype(F32)).astype(F32)
        values = lax.dot_general(
            hot, trig[...], (((1,), (0,)), ((), ())), preferred_element_type=F32, precision=lax.Precision.HIGHEST
        )
        sin = values[:, DK:]
        even = (iota((WIN, DK), 1) & 1) == 0
        cos[b * WIN : (b + 1) * WIN, :] = values[:, :DK]
        sin_a[b * WIN : (b + 1) * WIN, :] = jnp.where(even, -sin, 0.0)
        sin_b[b * WIN : (b + 1) * WIN, :] = jnp.where(even, 0.0, sin)
    pos = iota((1, D), 1)
    order[...] = (iota((D, D), 0) == source_feature(pos, me, 0)).astype(BF)
    for core in range(2):
        base = core * 256 + 192
        want = source_feature(base + iota((64, 1), 0), me, 0)
        have = source_feature(base + iota((1, 64), 1), me, 1)
        third[core] = (want == have).astype(BF)


def trig_table():
    frequency = 1.0 / 10000.0 ** np.linspace(0.0, 1.0, DK // 2, dtype=np.float32)
    frequency = np.repeat(frequency.astype(np.float32), 2)
    phases = np.arange(WIN, dtype=np.float32)[:, None] * frequency
    phases = phases.astype(np.float32).astype(np.float64)
    return np.concatenate([np.cos(phases), np.sin(phases)], axis=1).astype(np.float32)


def tables(me, lengths, here):
    return pl.pallas_call(
        tables_kernel,
        in_specs=[
            pl.BlockSpec(memory_space=pltpu.SMEM),
            pl.BlockSpec(memory_space=pltpu.VMEM),
            pl.BlockSpec(memory_space=pltpu.VMEM),
            pl.BlockSpec(memory_space=pltpu.VMEM),
        ],
        out_shape=[
            jax.ShapeDtypeStruct((2, HEADS, WIN, WIN), F32),
            jax.ShapeDtypeStruct((ROWS, DK), F32),
            jax.ShapeDtypeStruct((ROWS, DK), F32),
            jax.ShapeDtypeStruct((ROWS, DK), F32),
            jax.ShapeDtypeStruct((ROWS, 128), F32),
            jax.ShapeDtypeStruct((2, BLOCK, 128), F32),
            jax.ShapeDtypeStruct((D, D), BF),
            jax.ShapeDtypeStruct((2, 64, 64), BF),
            jax.ShapeDtypeStruct(here.shape, BF),
        ],
        compiler_params=pltpu.CompilerParams(vmem_limit_bytes=16 << 20),
    )(me, lengths, jnp.asarray(trig_table()), here)


def norm_parts(values):
    center = values - jnp.mean(values, axis=-1, keepdims=True)
    inv = lax.rsqrt(jnp.mean(center * center, axis=-1, keepdims=True) + NORM_EPSILON)
    return center * inv, inv


def norm_back(grad, hat, inv, gain):
    scaled = grad * gain
    mean_one = jnp.mean(scaled, axis=-1, keepdims=True)
    mean_two = jnp.mean(scaled * hat, axis=-1, keepdims=True)
    return inv * (scaled - mean_one - hat * mean_two)


def rotated(v, cos, sin_a, sin_b):
    return v * cos + pltpu.roll(v, DK - 1, 1) * sin_a + pltpu.roll(v, 1, 1) * sin_b


def rotated_back(v, cos, sin_a, sin_b):
    return v * cos - pltpu.roll(v, DK - 1, 1) * sin_a - pltpu.roll(v, 1, 1) * sin_b


def sigmoid(v):
    return 0.5 * jnp.tanh(0.5 * v) + 0.5


GELU_C = float(np.sqrt(2.0 / np.pi))


def gelu_tanh(v):
    return jnp.tanh(GELU_C * (v + 0.044715 * (v * v * v)))


class Saved:
    F32_PARTS = (("up", VP), ("gt", VP), ("m", D), ("r", VP), ("gp", VP), ("x", D))
    BF_PARTS = (("h", VP), ("b", D), ("u", VP), ("p", 2 * WIN), ("v", VP), ("k", D), ("q", D), ("a", D))
    WIDTHS = tuple(sum(width for _, width in parts) for parts in (F32_PARTS, BF_PARTS))
    DTYPES = (F32, BF)

    def __init__(self, refs):
        for ref, parts in zip(refs, (self.F32_PARTS, self.BF_PARTS)):
            at = 0
            for name, width in parts:
                setattr(self, name, ref.at[:, at : at + width])
                at += width

    @classmethod
    def shapes(cls):
        return [((ROWS, width), dtype) for width, dtype in zip(cls.WIDTHS, cls.DTYPES)]


def head_masks(rows):
    lane = iota((rows, VP), 1)
    return lane < DV, (lane >= DV) & (lane < 2 * DV)


def forward(w, gb, sv, decay, cos, sin_a, sin_b, later):
    x = sv.x[...]
    hat, _ = norm_parts(x)
    sv.a[...] = (hat * gb[0:1, :] + gb[2:3, :]).astype(BF)
    a = sv.a[...]
    tabs = (cos[...], sin_a[...], sin_b[...])
    for h in range(HEADS):
        at = slice(h * DK, (h + 1) * DK)
        sv.q[:, at] = rotated(w.times(a, Q0 + h * DK, DK), *tabs).astype(BF)
        key = rotated(w.times(a, K0 + h * DK, DK), *tabs) * DK ** (-0.5)
        sv.k[:, at] = key.astype(BF)
    sv.v[...] = w.times(a, V0, VP).astype(BF)
    in_head = head_masks(WIN)
    for b in range(2):
        rows = slice(b * WIN, (b + 1) * WIN)
        for h in range(HEADS):
            at = slice(h * DK, (h + 1) * DK)
            scores = dot_nt(sv.q[rows, at], sv.k[rows, at])
            sv.p[rows, h * WIN : (h + 1) * WIN] = (decay[b, h] * scores).astype(BF)
        v = sv.v[rows, :]
        both = jnp.concatenate([jnp.where(in_head[0], v, 0), jnp.where(in_head[1], v, 0)], axis=0)
        sv.r[rows, :] = dot(sv.p[rows, :], both)
    for copy in later:
        copy.wait()
    one, two = group_scales(sv.r[...])
    for at, end in CHUNKS:
        gate = w.times(a, S0 + at, end - at)
        sv.gp[:, at:end] = gate
        scale = by_head(one, two, at, end)
        sv.u[:, at:end] = (sv.r[:, at:end] * scale * (gate * sigmoid(gate))).astype(BF)
    sv.m[...] = x + w.turned(sv.u[...], O0, VP)
    hat, _ = norm_parts(sv.m[...])
    sv.b[...] = (hat * gb[1:2, :] + gb[3:4, :]).astype(BF)
    b = sv.b[...]
    for at, end in CHUNKS:
        up = w.times(b, U0 + at, end - at)
        gate = w.times(b, G0 + at, end - at)
        sv.up[:, at:end] = up
        sv.gt[:, at:end] = gate
        sv.h[:, at:end] = (0.5 * up * (1.0 + gelu_tanh(up)) * gate).astype(BF)
    return sv.m[...] + w.turned(sv.h[...], D0, VP)


def head_sums(values):
    first, second = head_masks(ROWS)
    return (
        jnp.sum(jnp.where(first, values, 0.0), axis=-1, keepdims=True),
        jnp.sum(jnp.where(second, values, 0.0), axis=-1, keepdims=True),
    )


def by_head(one, two, at=0, end=VP):
    return jnp.where(iota((ROWS, end - at), 1) + at < DV, one, two)


def group_scales(r):
    one, two = head_sums(r * r)
    return lax.rsqrt(one / DV + GROUP_EPSILON), lax.rsqrt(two / DV + GROUP_EPSILON)


CHUNKS = ((0, 256), (256, 512), (512, 768), (768, 896))


class Weights:
    def __init__(self, refs, third, outs=None):
        self.own, self.oth = refs
        self.third, self.outs = third, outs or refs

    def times(self, a, at, width):
        one = dot(a[:, :256], self.own[:, at : at + width])
        return one + dot(a[:, 256:], self.oth[:, at : at + width])

    def turned(self, a, at, width):
        return jnp.concatenate([dot_nt(a, self.own[:, at : at + width]), dot_nt(a, self.oth[:, at : at + width])], axis=1)

    def put(self, at, width, grad):
        low = grad.astype(BF)
        for core, out in enumerate(self.outs):
            part = low[core * 256 : (core + 1) * 256]
            if self.third is None:
                out[:, at : at + width] = part
            else:
                out[0:192, at : at + width] = part[0:192]
                out[192:256, at : at + width] = dot_tn(self.third[core], part[192:256]).astype(BF)


def backward(w, gb, sv, decay, cos, sin_a, sin_b, g, spare, dn):
    f = g.astype(BF)
    dup, dgt = spare.at[0], spare.at[1]
    for at, end in CHUNKS:
        dh = w.times(f, D0 + at, end - at)
        up = sv.up[:, at:end]
        t = gelu_tanh(up)
        half = 0.5 * (1.0 + t)
        dgt[:, at:end] = (dh * (up * half)).astype(BF)
        slope = half + 0.5 * up * (1.0 - t * t) * (GELU_C * (1.0 + 3 * 0.044715 * (up * up)))
        dup[:, at:end] = (dh * sv.gt[:, at:end] * slope).astype(BF)
    db = w.turned(dup[...], U0, VP) + w.turned(dgt[...], G0, VP)
    w.put(D0, VP, dot_tn(f, sv.h[...]))
    b = sv.b[...]
    w.put(U0, VP, dot_tn(b, dup[...]))
    w.put(G0, VP, dot_tn(b, dgt[...]))
    hat, inv = norm_parts(sv.m[...])
    dgain_two = jnp.sum(db * hat, axis=0, keepdims=True)
    dbias_two = jnp.sum(db, axis=0, keepdims=True)
    dm = g + norm_back(db, hat, inv, gb[1:2, :])
    e = dm.astype(BF)
    scales = group_scales(sv.r[...])
    sums = [0.0, 0.0]
    dgp, dr = spare.at[0], spare.at[1]
    for at, end in CHUNKS:
        du = w.times(e, O0 + at, end - at)
        r = sv.r[:, at:end]
        gate = sv.gp[:, at:end]
        sig = sigmoid(gate)
        dgp[:, at:end] = (du * (r * by_head(*scales, at, end)) * (sig * (1.0 + gate * (1.0 - sig)))).astype(BF)
        part = du * (gate * sig)
        dn[:, at:end] = part
        lane = iota((ROWS, end - at), 1) + at
        product = part * r
        sums[0] = sums[0] + jnp.sum(jnp.where(lane < DV, product, 0.0), axis=-1, keepdims=True)
        sums[1] = sums[1] + jnp.sum(jnp.where((lane >= DV) & (lane < 2 * DV), product, 0.0), axis=-1, keepdims=True)
    w.put(O0, VP, dot_tn(e, sv.u[...]))
    cubes = [scale * scale * scale * (total / DV) for scale, total in zip(scales, sums)]
    for at, end in CHUNKS:
        part = by_head(*scales, at, end) * dn[:, at:end] - sv.r[:, at:end] * by_head(*cubes, at, end)
        dr[:, at:end] = part.astype(BF)
    a = sv.a[...]
    da = w.turned(dgp[...], S0, VP)
    w.put(S0, VP, dot_tn(a, dgp[...]))
    in_head = head_masks(WIN)
    tabs = (cos[...], sin_a[...], sin_b[...])
    dvs, dqs, dks = [], [[], []], [[], []]
    for bt in range(2):
        rows = slice(bt * WIN, (bt + 1) * WIN)
        part = dr[rows, :]
        both = jnp.concatenate([jnp.where(in_head[0], part, 0), jnp.where(in_head[1], part, 0)], axis=0)
        p = sv.p[rows, :]
        stacked = jnp.concatenate([p[:, :WIN], p[:, WIN:]], axis=0)
        dvs.append(dot_tn(stacked, both).astype(BF))
        dp = dot_nt(both, sv.v[rows, :])
        for h in range(HEADS):
            at = slice(h * DK, (h + 1) * DK)
            ds = (decay[bt, h] * dp[h * WIN : (h + 1) * WIN]).astype(BF)
            dqs[h].append(dot(ds, sv.k[rows, at]))
            dks[h].append(dot_tn(ds, sv.q[rows, at]))
    dv = jnp.concatenate(dvs, axis=0)
    dq = jnp.concatenate([rotated_back(jnp.concatenate(dqs[h], axis=0), *tabs).astype(BF) for h in range(HEADS)], axis=1)
    dk = jnp.concatenate(
        [rotated_back(jnp.concatenate(dks[h], axis=0) * DK ** (-0.5), *tabs).astype(BF) for h in range(HEADS)], axis=1
    )
    da = da + w.turned(dv, V0, VP) + w.turned(dq, Q0, 512) + w.turned(dk, K0, 512)
    w.put(Q0, 512, dot_tn(a, dq))
    w.put(K0, 512, dot_tn(a, dk))
    hat, inv = norm_parts(sv.x[...])
    dgain_one = jnp.sum(da * hat, axis=0, keepdims=True)
    dbias_one = jnp.sum(da, axis=0, keepdims=True)
    norms = jnp.concatenate([dgain_one, dgain_two, dbias_one, dbias_two, jnp.zeros((4, D), F32)], axis=0).astype(BF)
    spread = (iota((8, VP), 1) == iota((8, VP), 0) + 864).astype(BF)
    w.put(V0, VP, dot_tn(a, dv) + dot_tn(norms, spread))
    return dm + norm_back(da, hat, inv, gb[0:1, :])


def window_rows(here, behind, k):
    return jnp.concatenate([here[k, 0], behind[k, 0], here[k, 1], behind[k, 1]], axis=0)


def put_norms(gb, weights):
    pick = ((iota((8, 128), 1) == iota((8, 128), 0) + NORM_LANE) & (iota((8, 128), 0) < 4)).astype(BF)
    gb[...] = weights.turned(pick, V0 + 768, 128)


def put_rows(result, order, out, lent):
    result = dot_nt(result.astype(BF), order[...]).astype(BF)
    for b in range(2):
        out[b] = result[b * WIN : b * WIN + BLOCK]
        lent[b] = result[b * WIN + BLOCK : (b + 1) * WIN]


def first_kernel(*refs):
    pieces, refs = refs[:12], refs[12:]
    here, behind, decay, cos, sin_a, sin_b, live, order, third = refs[:9]
    out, lent, g_out = refs[9:12]
    held = (refs[12:14], refs[14:16])
    gb, sems, spare, dn = refs[18:22]
    saved = [Saved(refs[16:18]), Saved(refs[22:24])]
    groups = []
    count = 0
    for layer, start, end in ((0, 0, S0), (0, S0, WIDTH), (1, 0, WIDTH)):
        group = []
        for core in range(2):
            for row in range(4):
                color, unit = COLOR_OF[(layer, row)]
                for half in range(2):
                    piece = pieces[core * 6 + half * 3 + color]
                    at = unit * WIDTH
                    rows = slice(row * 64 + half * 32, row * 64 + half * 32 + 32)
                    copy = pltpu.make_async_copy(
                        piece.at[:, at + start : at + end], held[layer][core].at[rows, start:end], sems.at[count]
                    )
                    group.append(copy)
                    count += 1
        groups.append(group)
    for copy in groups[0] + groups[1]:
        copy.start()
    saved[0].x[...] = dot(window_rows(here, behind, 0), order[...])
    tabs = (decay, cos, sin_a, sin_b)
    weights = [Weights(held[0], None), Weights(held[1], third)]
    for copy in groups[0]:
        copy.wait()
    for copy in groups[2]:
        copy.start()
    put_norms(gb.at[0], weights[0])
    saved[1].x[...] = forward(weights[0], gb.at[0], saved[0], *tabs, groups[1])
    for copy in groups[2]:
        copy.wait()
    for core in range(2):
        at = slice(192, 256)
        held[1][core][at, :] = dot(third[core], held[1][core][at, :]).astype(BF)
    put_norms(gb.at[1], weights[1])
    put_rows(forward(weights[1], gb.at[1], saved[1], *tabs, []), order, out, lent)
    g = dot(window_rows(here, behind, 1), order[...]) * live[:, 0:1]
    g_out[...] = backward(weights[1], gb.at[1], saved[1], *tabs, g, spare, dn)


def second_kernel(*refs):
    held, kept = refs[:2], refs[2:4]
    g_in, decay, cos, sin_a, sin_b = refs[4:9]
    g_out, gb, spare, dn = refs[11:15]
    weights = Weights(held, None, refs[9:11])
    put_norms(gb, weights)
    g_out[...] = backward(weights, gb, Saved(kept), decay, cos, sin_a, sin_b, g_in[...], spare, dn)


def rows_out_kernel(g, order, out_one, lent_one, out, lent):
    out[0] = out_one[...]
    lent[0] = lent_one[...]
    put_rows(g[...], order, out.at[1], lent.at[1])


def layers(pieces, here, behind, tabs):
    decay, cos, sin_a, sin_b, live, order, third = tabs
    grads = [jax.ShapeDtypeStruct((256, WIDTH), BF)] * 2
    saved = Saved.shapes()
    spare = [pltpu.VMEM((2, ROWS, VP), BF), pltpu.VMEM((ROWS, VP), F32)]
    any_space, hbm = pl.BlockSpec(memory_space=pl.ANY), pl.BlockSpec(memory_space=pltpu.HBM)
    vmem = pl.BlockSpec(memory_space=pltpu.VMEM)
    out, lent, g, own0, oth0, own1, oth1, *kept = pl.pallas_call(
        first_kernel,
        in_specs=[any_space] * 6 + [hbm] * 3 + [any_space] * 3 + [vmem] * 9,
        out_specs=[vmem] * 9,
        out_shape=[jax.ShapeDtypeStruct((2, BLOCK, D), BF)] * 2
        + [jax.ShapeDtypeStruct((ROWS, D), F32), *grads, *grads]
        + [jax.ShapeDtypeStruct(*one) for one in saved],
        scratch_shapes=[pltpu.VMEM((2, 8, D), F32), pltpu.SemaphoreType.DMA((48,)), *spare]
        + [pltpu.VMEM(*one) for one in saved],
        compiler_params=pltpu.CompilerParams(vmem_limit_bytes=FIRST_VMEM),
    )(*pieces, here, behind, *tabs)
    got1 = swap_cores(oth1)
    own0, oth0, g = pl.pallas_call(
        second_kernel,
        in_specs=[vmem] * 9,
        out_specs=[vmem] * 3,
        out_shape=[*grads, jax.ShapeDtypeStruct((ROWS, D), F32)],
        scratch_shapes=[pltpu.VMEM((8, D), F32), *spare],
        input_output_aliases={0: 0, 1: 1},
        compiler_params=pltpu.CompilerParams(vmem_limit_bytes=SECOND_VMEM),
    )(own0, oth0, *kept, g, decay, cos, sin_a, sin_b)
    out, lent = pl.pallas_call(
        rows_out_kernel,
        out_shape=[jax.ShapeDtypeStruct((2, 2, BLOCK, D), BF)] * 2,
        compiler_params=pltpu.CompilerParams(vmem_limit_bytes=8 << 20),
    )(g, order, out, lent)
    return out, lent, own0, swap_cores(oth0), own1, got1


def pair_sum(layer, own, got, before, passed):
    extra = len(before)

    def kernel(own, got, passed, *refs):
        befores, outs = refs[:extra], refs[extra:]
        outs[6][...] = passed[...]
        for c in range(3):
            for k, (at, row) in enumerate(UNITS[c]):
                rows, cols = slice(row * 64, (row + 1) * 64), slice(k * WIDTH, (k + 1) * WIDTH)
                if at == layer:
                    total = (own[rows, :].astype(F32) + got[rows, :].astype(F32)).astype(BF)
                    outs[2 * c][:, cols] = total[:32]
                    outs[2 * c + 1][:, cols] = total[32:]
                elif befores:
                    for half in range(2):
                        outs[2 * c + half][:, cols] = befores[2 * c + half][:, cols]

    return pl.pallas_call(
        kernel,
        out_shape=[jax.ShapeDtypeStruct((32, w), BF) for w in WIDE for _ in range(2)]
        + [jax.ShapeDtypeStruct(passed.shape, BF)],
        compiler_params=pltpu.CompilerParams(vmem_limit_bytes=PAIR_VMEM),
    )(own, got, passed, *before)


def halve_kernel(*refs):
    for c in range(3):
        total = (refs[c][...].astype(F32) + refs[3 + c][...].astype(F32)).astype(BF)
        half = total.shape[0] // 2
        refs[-6 + 2 * c][...] = total[:half]
        refs[-5 + 2 * c][...] = total[half:]


def halve(keep, got, after):
    vmem, anywhere = pl.BlockSpec(memory_space=pltpu.VMEM), pl.BlockSpec(memory_space=pl.ANY)
    halves = pl.pallas_call(
        halve_kernel,
        in_specs=[vmem] * 6 + [anywhere] * len(after),
        out_shape=[jax.ShapeDtypeStruct((k.shape[0] // 2, *k.shape[1:]), BF) for k in keep for _ in range(2)],
        compiler_params=pltpu.CompilerParams(vmem_limit_bytes=24 << 20),
    )(*keep, *got, *after)
    return halves[0::2], halves[1::2]


def lines_kernel(*refs):
    swap = swap_rows()
    for c, start in enumerate(COLOR_START):
        keep, got = refs[c], refs[3 + c]
        lines = keep.shape[1] // 128
        for i in range(0, FLAT[c], 16):
            block = []
            for k in range(i, i + 16):
                if k < lines:
                    at = slice(k * 128, (k + 1) * 128)
                    block.append(keep[:, at].astype(F32) + got[:, at].astype(F32))
                else:
                    block.append(jnp.zeros((8, 128), F32))
            turned = dot_tn(swap, jnp.concatenate(block, axis=0).astype(BF)).astype(BF)
            for k in range(8):
                refs[6 + k][start + i : start + i + 16] = turned[k * 16 : (k + 1) * 16]


def to_lines(keep, got):
    return pl.pallas_call(
        lines_kernel,
        out_shape=[jax.ShapeDtypeStruct((LINES_ALL, 128), BF) for _ in range(8)],
        compiler_params=pltpu.CompilerParams(vmem_limit_bytes=16 << 20),
    )(*keep, *got)


def scatter_sum(own0, got0, own1, got1, lent, finish):
    *before, lent = pair_sum(1, own1, got1, (), lent)
    *halves, lent = pair_sum(0, own0, got0, before, lent)
    finals = finish(from_behind(lent, 1))
    keep, send = halves[0::2], halves[1::2]
    keep, send = halve(keep, permute_all(send, 2), finals)
    keep, send = halve(keep, permute_all(send, 1), ())
    mine, *rest = to_lines(keep, permute_all(send, 0))
    return finals, [mine] + [lax.ppermute(rest[bits - 1], "fsdp", low_pairs(bits)) for bits in range(1, 8)]


def unpack_kernel(*refs):
    q, k, v, s, o, u, g, d, gain, bias, row = refs[8:]
    row[...] = jnp.zeros_like(row)
    total = refs[0][...].astype(F32)
    for part in refs[1:8]:
        total = total + part[...].astype(F32)
    for units, start in zip(UNITS, (0, FLAT[0], FLAT[0] + FLAT[1])):
        for n, (layer, r) in enumerate(units):
            for j in range(LINES):
                at = start + n * LINES + j
                row[layer, r : r + 1, j * 128 : (j + 1) * 128] = total[at : at + 1]
    for layer in range(2):
        for out, at, width in (
            (q, Q0, 512), (k, K0, 512), (v, V0, 864), (s, S0, 864), (o, O0, 864), (u, U0, 864), (g, G0, 864), (d, D0, 864),
        ):
            out[layer] = row[layer, 0:4, at : at + width]
        norms = jnp.transpose(row[layer, :, V0 + 768 : V0 + VP])
        for kind in range(2):
            gain[layer, kind : kind + 1, :] = norms[NORM_LANE + kind : NORM_LANE + kind + 1, 0:4]
            bias[layer, kind : kind + 1, :] = norms[NORM_LANE + 2 + kind : NORM_LANE + 3 + kind, 0:4]


def unpack(parts):
    shapes = [(2, 4, 512)] * 2 + [(2, 4, 864)] * 6 + [(2, 2, 4)] * 2
    return pl.pallas_call(
        unpack_kernel,
        out_shape=[jax.ShapeDtypeStruct(shape, F32) for shape in shapes],
        scratch_shapes=[pltpu.VMEM((2, 8, WIDTH), F32)],
        compiler_params=pltpu.CompilerParams(vmem_limit_bytes=8 << 20),
    )(*parts)


def from_behind(value, by):
    pairs = [(i, i + by) for i in range(128) if 0 <= i + by < 128]
    return lax.ppermute(value, "fsdp", pairs)


def local(inputs, cotangent, lengths, *weights):
    me = lax.axis_index("fsdp").astype(jnp.int32)
    q, k, v, s, o, u, g, d, gain, bias = weights
    o, d = jnp.swapaxes(o, 1, 2), jnp.swapaxes(d, 1, 2)
    flat, both = pack((q, k, v, s, o, u, g, d, gain, bias), inputs, cotangent)
    pieces, here, behind = gather(flat, both)
    decay, cos, sin_a, sin_b, live, flags, order, third, here = tables(me[None], lengths, here)
    out, lent, own0, got0, own1, got1 = layers(
        pieces, here, behind, (decay, cos, sin_a, sin_b, live, order, third)
    )

    def finish(borrowed):
        mine = flags[:, :, 0:1] > 0
        return [jnp.where(mine, out[k], borrowed[k]) for k in range(2)]

    (result, grad), parts = scatter_sum(own0, got0, own1, got1, lent, finish)
    q, k, v, s, o, u, g, d, gain, bias = unpack(parts)
    return result, grad, q, k, v, s, jnp.swapaxes(o, 1, 2), u, g, jnp.swapaxes(d, 1, 2), gain, bias


def solution(mesh):
    rows, wide = P(None, "fsdp", None), P(None, None, "fsdp")
    weights = (rows, rows, rows, rows, wide, rows, rows, wide, wide, wide)
    return jax.shard_map(
        local,
        mesh=mesh,
        in_specs=(rows, rows, P(), *weights),
        out_specs=(rows, rows, *weights),
        check_vma=False,
    )
```
